32 devices in a mesh: parts: 2 (over x), query: 16 (over z, y, core).
Axes of the slice: x: 2, y: 2, z: 4, core: 2. Of those that a mesh axis runs over, the one named last changes fastest.
Arguments:
- train_inputs: bfloat16 [2, 256, 4096], P(None, ('parts', 'query')), parts along dimension 1, may hold values from -6 to 6
- train_outgrads: bfloat16 [2, 256, 12288], P(None, 'parts', 'query'), parts along dimension 1, may hold values from -0.0039978027 to 0.0039978027
- sequence_ids: int32 [256], P('parts'), parts along dimension 0, may hold values from 0 to 3, never falling along the last dimension, each value on 1 to 64 neighbouring positions
- query_inputs: bfloat16 [2, 256, 4096], P(None, 'query'), may hold values from -6 to 6
- query_outgrads: bfloat16 [2, 256, 12288], P(None, None, 'query'), may hold values from -0.0039978027 to 0.0039978027
- eigenvalues: float32 [2, 12288, 4096], P(None, 'query'), may hold values from 0.01 to 10
- input_basis: bfloat16 [64, 128, 128], P('query'), may hold values from -0.5 to 0.5
- slot_list: int32 [64], replicated, may hold values from 0 to 63, as said below
- output_basis: bfloat16 [2, 192, 64, 64], P(None, 'query'), may hold values from -0.75 to 0.75
Outputs:
- scores: float32 [16, 8], P(None, 'parts'), parts along dimension 1
- rotated_inputs: bfloat16 [2, 256, 4096], P(None, ('parts', 'query')), parts along dimension 1
The draws below stay inside these ranges and needn't reach their ends.
There are 2 independent parts, one for each index of `parts`. The reference program is written for one: setup_inputs(seed, part) draws one part's arguments, and reference() takes and returns one part's arrays. A program takes and returns all parts, laid end to end along the dimension named above; an argument that names none is the same for every part. Nothing has to cross between parts.
Inputs may be any that keep to these rules, and one draw needn't show every extreme that they name: `slot_list`: the entries are distinct slots; slot p belongs to device p // 4 of the query axis. Every device holds 4 tiles.
All inputs are finite; a program needn't handle non-finite values.
Results may differ from the reference program's by a relative error of at most 0.0071.
Values may be sent and summed in bfloat16 or wider, within the bound.
No kernel may reach another device: no remote copies, remote signals or barrier semaphores. Data moves between devices by JAX's collectives and lax.ppermute only.
A program may use at most 192 MiB of HBM per device.

```python
import math
import jax
import jax.numpy as jnp
import numpy as np
from jax import lax

D = 4096
FF = 12288
LAYERS = 2
TILE_A = 128
TILE_S = 64
SLOTS = 4
SEQS = 4
QUERIES = 16
QLEN = 16
TOKENS = 128
QT = 256
SLOT_TOTAL = 64
N_QUERY = 16


def draw_slot_list(key, part):
    key = jax.random.fold_in(key, 7)
    key_owner, key_order, key_shuffle = jax.random.split(key, 3)
    slot_count = N_QUERY * SLOTS
    full_owner = jax.random.randint(key_owner, (), 0, N_QUERY)
    order = jax.random.permutation(key_order, slot_count)
    owners = jnp.arange(slot_count, dtype=jnp.int32) // SLOTS
    ranking = order + jnp.where(owners == full_owner, -slot_count, 0)
    picked = jnp.argsort(ranking, stable=True)[:LAYERS * D // TILE_A]
    return jax.random.permutation(key_shuffle, picked).astype(jnp.int32)


def steps_of(stream_key, extent, cuts, low, high):
    factor_of = 1.0
    for position, parts in cuts:
        steps = jax.random.uniform(jax.random.fold_in(jax.random.fold_in(stream_key, 6), position), (parts,), jnp.float32, low / len(cuts), high / len(cuts))
        factor_of = factor_of * jnp.repeat(jnp.exp(steps), extent[position] // parts).reshape((-1,) + (1,) * (len(extent) - 1 - position))
    return factor_of


def profile(amount, total, most, skew):
    loads = [(1 << 20) // math.isqrt(standing ** skew) + 1 for standing in range(2, amount + 1)]
    surplus, holding = total - most - (amount - 1), [1] * (amount - 1)
    while surplus > 0:
        free = [i for i in range(amount - 1) if holding[i] < most]
        pool, remaining = sum([loads[i] for i in free]), surplus
        for i in free:
            addition = min(most - holding[i], max(1, remaining * loads[i] // pool), surplus)
            holding[i] = holding[i] + addition
            surplus = surplus - addition
    return np.array([most] + holding)


def uneven_parts(rng, number_of, total, limit, skew):
    if number_of == 2:
        one = jax.random.randint(rng, (), max(1, total - limit), min(limit, total - 1) + 1)
        return jnp.stack([one, total - one])
    tallies = jnp.asarray(profile(number_of, total, limit, skew), jnp.int32)
    couples = (number_of - 1) // 2
    donor, sink = tallies[1:1 + 2 * couples:2], tallies[2:2 + 2 * couples:2]
    margin = jnp.minimum(donor - 1, limit - sink)
    moved = jax.random.randint(jax.random.fold_in(rng, 1), (couples,), 0, 1 << 20) % (margin + 1)
    tallies = tallies.at[1:1 + 2 * couples:2].set(donor - moved).at[2:2 + 2 * couples:2].set(sink + moved)
    return tallies[jax.random.permutation(jax.random.fold_in(rng, 2), number_of)]


def noise(stream_key, dims, deviation, most, pieces=(), kind=jnp.bfloat16):
    result = jax.random.normal(stream_key, dims, jnp.float32) * deviation
    if len(pieces) > 0:
        result = steps_of(stream_key, dims, pieces, -0.22, 0.18) * result
    return jnp.clip(result, min=-most, max=most).astype(kind)


def setup_inputs(seed: int = 0, part: int = 0) -> dict:
    splits = jax.random.split(jax.random.key(seed), 10)
    part_keys = jax.random.split(jax.random.fold_in(splits[9], part), 10)
    return {
        "train_inputs": noise(part_keys[0], (LAYERS, TOKENS, D), 1.0, 6.0, ((1, 16),)),
        "train_outgrads": noise(part_keys[1], (LAYERS, TOKENS, FF), 0.0007, 0.0039978027, ((2, 16),)),
        "sequence_ids": jnp.searchsorted(jnp.cumsum(uneven_parts(part_keys[2], SEQS, TOKENS, TOKENS // 2, 2)), jnp.arange(TOKENS), side="right").astype(jnp.int32),
        "query_inputs": noise(splits[3], (LAYERS, QT, D), 1.0, 6.0, ((1, 16),)),
        "query_outgrads": noise(splits[4], (LAYERS, QT, FF), 0.0007, 0.0039978027, ((2, 16),)),
        "eigenvalues": jnp.clip(jnp.exp(math.log(10.0) - 6.9077553 * jax.random.uniform(splits[5], (LAYERS, FF, D), jnp.float32) ** steps_of(splits[5], (LAYERS, FF, D), ((1, 16),), -0.2, 0.2)), 0.01, 10.0),
        "input_basis": noise(splits[6], (SLOT_TOTAL, TILE_A, TILE_A), TILE_A ** -0.5, 0.5, ((0, 16),)),
        "slot_list": draw_slot_list(jax.random.fold_in(splits[9], 71), part),
        "output_basis": noise(splits[8], (LAYERS, FF // TILE_S, TILE_S, TILE_S), TILE_S ** -0.5, 0.75, ((1, 16),)),
    }


damping = 0.05


def keep_rounded(values):
    return lax.optimization_barrier(values.astype(jnp.bfloat16)).astype(jnp.float32)


def reference(train_inputs, train_outgrads, sequence_ids, query_inputs, query_outgrads, eigenvalues, input_basis, slot_list, output_basis):
    basis_tiles = input_basis[slot_list].astype(jnp.float32).reshape(LAYERS, D // TILE_A, TILE_A, TILE_A)
    out_tiles = output_basis.astype(jnp.float32)

    def rotate_inputs(rows):
        blocks = rows.astype(jnp.float32).reshape(LAYERS, rows.shape[1], D // TILE_A, TILE_A)
        turned = jnp.einsum('lrbi,lbij->lrbj', blocks, basis_tiles)
        return turned.reshape(LAYERS, rows.shape[1], D).astype(jnp.bfloat16)

    def rotate_grads(rows):
        blocks = rows.astype(jnp.float32).reshape(LAYERS, rows.shape[1], FF // TILE_S, TILE_S)
        turned = jnp.einsum('lrbi,lbij->lrbj', blocks, out_tiles)
        return turned.reshape(LAYERS, rows.shape[1], FF).astype(jnp.bfloat16)

    rotated_train = rotate_inputs(train_inputs)
    rotated_query = rotate_inputs(query_inputs)
    grads_rot = rotate_grads(train_outgrads)
    query_rot = rotate_grads(query_outgrads)
    train_f = keep_rounded(rotated_train)
    query_f = keep_rounded(rotated_query)
    grads_f = keep_rounded(grads_rot)
    qgrads_f = keep_rounded(query_rot)
    onehot = (sequence_ids[:, None] == jnp.arange(SEQS, dtype=jnp.int32)[None, :]).astype(jnp.float32)
    totals = jnp.zeros((SEQS, QUERIES * QLEN), jnp.float32)
    block_span = FF // 8
    for layer_index in range(LAYERS):
        for block_index in range(8):
            block_start = block_index * block_span
            grad_block = grads_f[layer_index][:, block_start:block_start + block_span]
            masked = onehot[:, :, None] * grad_block[:, None, :]
            gram_block = jnp.einsum('tsi,tj->sij', masked, train_f[layer_index])
            weights = 1.0 / (eigenvalues[layer_index, block_start:block_start + block_span] + damping)
            scaled = keep_rounded(gram_block * weights[None])
            projected = jnp.einsum('sij,uj->siu', scaled, query_f[layer_index])
            totals = totals + jnp.einsum('siu,ui->su', projected, qgrads_f[layer_index][:, block_start:block_start + block_span])
    scores = jnp.sum(totals.reshape(SEQS, QUERIES, QLEN), axis=2).T
    return scores, rotated_train
```

```python
import jax
import jax.numpy as jnp
from jax import lax
from jax.experimental import pallas as pl
from jax.experimental.pallas import tpu as pltpu
from jax.sharding import PartitionSpec as P

D = 4096
LAYERS = 2
TILE_A = 128
TILE_S = 64
SEQS = 4
QUERIES = 16
QLEN = 16


damping = 0.05


def rotate_blocks(rows, block_tiles, width):
    layer_count, row_count, feature_count = rows.shape
    blocks = rows.reshape(layer_count, row_count, feature_count // width, width)
    shaped = block_tiles.reshape(layer_count, feature_count // width, width, width)
    turned = jnp.einsum("lrbi,lbij->lrbj", blocks, shaped, preferred_element_type=jnp.float32)
    return turned.reshape(layer_count, row_count, feature_count).astype(jnp.bfloat16)


def general_body(
    train_inputs,
    train_outgrads,
    sequence_ids,
    query_inputs,
    query_outgrads,
    eigenvalues,
    input_basis,
    slot_list,
    output_basis,
):
    every_slot = lax.all_gather(input_basis, "query", axis=0, tiled=True)
    basis_tiles = jnp.take(every_slot, slot_list, axis=0)
    rotated_out = rotate_blocks(train_inputs, basis_tiles, TILE_A)
    own_query = rotate_blocks(query_inputs, basis_tiles, TILE_A)
    rotated_train, rotated_query = (
        lax.all_gather(rotated_out, "query", axis=1, tiled=True),
        lax.all_gather(own_query, "query", axis=1, tiled=True),
    )
    grads_rot = rotate_blocks(train_outgrads, output_basis, TILE_S)
    query_rot = rotate_blocks(query_outgrads, output_basis, TILE_S)
    token_count = grads_rot.shape[1]
    slab_width = grads_rot.shape[2]
    weights = 1.0 / (eigenvalues + damping)
    onehot = (sequence_ids[:, None] == jnp.arange(SEQS, dtype=jnp.int32)[None, :]).astype(
        jnp.bfloat16
    )
    totals = jnp.zeros((SEQS, QUERIES * QLEN), jnp.float32)
    for layer_index in range(LAYERS):
        masked = (onehot[:, :, None] * grads_rot[layer_index][:, None, :]).reshape(
            token_count, SEQS * slab_width
        )
        gram_block = lax.dot_general(
            masked,
            rotated_train[layer_index],
            (((0,), (0,)), ((), ())),
            preferred_element_type=jnp.float32,
        )
        scaled = (gram_block.reshape(SEQS, slab_width, D) * weights[layer_index][None]).astype(
            jnp.bfloat16
        )
        projected = jnp.einsum(
            "sij,uj->siu", scaled, rotated_query[layer_index], preferred_element_type=jnp.float32
        )
        totals = totals + jnp.einsum(
            "siu,ui->su", projected, query_rot[layer_index].astype(jnp.float32)
        )
    partial_value = jnp.sum(totals.reshape(SEQS, QUERIES, QLEN), axis=2).T
    scores = lax.psum(partial_value, "query")
    return (scores, rotated_out)


NQ = 16
HALF = 32
UNIT = 40
SWAP = [(0, 1), (1, 0)]


def hop(value, bits):
    return lax.ppermute(value, "query", [(i, i ^ bits) for i in range(NQ)])


def score_kernel(info, *refs):
    units = refs[:NQ]
    grads, query_grads, codes, eigen, totals, own_rows, held, rows, acc, sems = refs[NQ:]
    step = pl.program_id(0)
    me = info[0]

    @pl.when(step == 0)
    def _():
        copies = [
            pltpu.make_async_copy(units[d], held.at[me ^ d], sems.at[d]) for d in range(NQ)
        ]
        for copy in copies:
            copy.start()
        acc[...] = jnp.zeros_like(acc)
        for copy in copies:
            copy.wait()

    layer = info[1 + step]
    owner = step // 2
    slot = step % 2
    basis = held[owner, pl.ds(HALF + 4 * slot, 4)].reshape(TILE_A, TILE_A)
    tile = held[:, step]
    train = tile[:, :16].reshape(256, TILE_A)
    query = tile[:, 16:].reshape(256, TILE_A)
    turned = jnp.dot(train, basis, preferred_element_type=jnp.float32)
    rows[...] = turned.astype(jnp.bfloat16)
    own_rows[0] = rows[pl.ds(pl.multiple_of(me * 16, 16), 16), :]
    train_t = turned.T.astype(jnp.bfloat16)
    query_t = (
        jnp.dot(query, basis, preferred_element_type=jnp.float32).T.astype(jnp.bfloat16)
    ).astype(jnp.float32)
    weights = 1.0 / (eigen[0].T + damping)
    code = codes[...]
    zero = jnp.zeros_like(train_t)
    left = jnp.concatenate(
        [jnp.where(code == s, train_t, zero) for s in range(2 * SEQS)], axis=0
    )
    projected = None
    for c in range(3):
        cols = pl.ds(c * 256, 256)
        gram = jnp.dot(left, grads[layer, :, cols], preferred_element_type=jnp.float32)
        w = weights[:, c * 256 : (c + 1) * 256]
        scaled = (gram.reshape(2 * SEQS, TILE_A, 256) * w[None]).astype(jnp.bfloat16)
        term = jnp.dot(
            scaled.reshape(2 * SEQS * TILE_A, 256),
            query_grads[layer, cols, :],
            preferred_element_type=jnp.float32,
        )
        projected = term if projected is None else projected + term
    product = projected.reshape(2 * SEQS, TILE_A, 256) * query_t[None]
    acc[...] += jnp.sum(product.reshape(2 * SEQS, TILE_A // 8, 8, 256), axis=1)

    @pl.when(step == pl.num_programs(0) - 1)
    def _():
        totals[...] = jnp.sum(acc[...], axis=1)


def paired_body(
    train_inputs,
    train_outgrads,
    sequence_ids,
    query_inputs,
    query_outgrads,
    eigenvalues,
    input_basis,
    slot_list,
    output_basis,
):
    x = lax.axis_index("parts")
    me = lax.axis_index("query")
    ids = jnp.arange(64, dtype=jnp.int32)
    tile_of = jnp.sum(jnp.where(slot_list[None, :] == ids[:, None], ids[None, :], 0), axis=1)
    by_half = tile_of.reshape(NQ, 2, 2)
    mine = lax.dynamic_index_in_dim(by_half, x, 1, False).reshape(HALF)
    theirs = lax.dynamic_index_in_dim(by_half, 1 - x, 1, False).reshape(HALF)

    def tiles(rows):
        return rows.reshape(LAYERS, rows.shape[1], 32, TILE_A).transpose(0, 2, 1, 3).reshape(
            64, rows.shape[1], TILE_A
        )

    train_tiles = tiles(train_inputs)
    train_mine = jnp.take(train_tiles, mine, axis=0, mode="clip")
    train_theirs = jnp.take(train_tiles, theirs, axis=0, mode="clip")
    train_other = lax.ppermute(train_theirs, "parts", SWAP)
    query_mine = jnp.take(tiles(query_inputs), mine, axis=0, mode="clip")
    first = jnp.where(x == 0, train_mine, train_other)
    second = jnp.where(x == 0, train_other, train_mine)
    basis_mine = lax.dynamic_slice_in_dim(input_basis, 2 * x, 2, 0).reshape(8, 32, TILE_A)
    unit = jnp.concatenate(
        [jnp.concatenate([first, second, query_mine], axis=1), basis_mine], axis=0
    )
    units = [None] * NQ
    units[0] = unit
    for d in (4, 12, 8):
        units[d] = hop(unit, d)
    for d in (0, 4, 12, 8):
        units[d ^ 2] = hop(units[d], 2)
    for d in (0, 2, 4, 6, 12, 14, 8, 10):
        units[d ^ 1] = hop(units[d], 1)

    id_block = jnp.broadcast_to(
        sequence_ids.astype(jnp.bfloat16)[None, :, None], (LAYERS, 128, TILE_A)
    )
    sent = jnp.concatenate([train_outgrads, id_block], axis=2)
    other = lax.ppermute(sent, "parts", SWAP)
    both = jnp.stack(
        [jnp.where(x == 0, sent, other), jnp.where(x == 0, other, sent)], axis=0
    ).reshape(2, LAYERS, NQ, 8, 896)
    both = both.transpose(1, 2, 0, 3, 4).reshape(LAYERS, 256, 896)
    part_of = (jnp.arange(256, dtype=jnp.int32) // 8) % 2
    codes = (both[0, :, 768].astype(jnp.int32) + SEQS * part_of).reshape(1, 256)
    grads_rot = rotate_blocks(both[:, :, :768], output_basis, TILE_S)
    query_rot = rotate_blocks(query_outgrads, output_basis, TILE_S).transpose(0, 2, 1)

    info = jnp.concatenate([me.reshape(1).astype(jnp.int32), mine // 32, mine % 32])
    any_spec = pl.BlockSpec(memory_space=pl.ANY)

    def whole(shape):
        return pl.BlockSpec(shape, lambda n, s: (0,) * len(shape))

    totals, own_rows = pl.pallas_call(
        score_kernel,
        grid_spec=pltpu.PrefetchScalarGridSpec(
            num_scalar_prefetch=1,
            grid=(HALF,),
            in_specs=[any_spec] * NQ
            + [
                whole((LAYERS, 256, 768)),
                whole((LAYERS, 768, 256)),
                whole((1, 256)),
                pl.BlockSpec((1, 768, TILE_A), lambda n, s: (s[1 + n], 0, s[1 + HALF + n])),
            ],
            out_specs=[
                whole((2 * SEQS, 256)),
                pl.BlockSpec((1, 16, TILE_A), lambda n, s: (n, 0, 0)),
            ],
            scratch_shapes=[
                pltpu.VMEM((NQ, UNIT, 32, TILE_A), jnp.bfloat16),
                pltpu.VMEM((256, TILE_A), jnp.bfloat16),
                pltpu.VMEM((2 * SEQS, 8, 256), jnp.float32),
                pltpu.SemaphoreType.DMA((NQ,)),
            ],
        ),
        out_shape=[
            jax.ShapeDtypeStruct((2 * SEQS, 256), jnp.float32),
            jax.ShapeDtypeStruct((HALF, 16, TILE_A), jnp.bfloat16),
        ],
        compiler_params=pltpu.CompilerParams(vmem_limit_bytes=40 * 1024 * 1024),
        cost_estimate=pl.CostEstimate(
            flops=26 * 10**9, bytes_accessed=19 * 10**6, transcendentals=0
        ),
    )(info, *units, grads_rot, query_rot, codes, eigenvalues)

    halves = totals.reshape(2, SEQS, 256)
    keep = lax.dynamic_index_in_dim(halves, x, 0, False)
    give = lax.dynamic_index_in_dim(halves, 1 - x, 0, False)
    total = keep + lax.ppermute(give, "parts", SWAP)
    for bits in (1, 2, 4, 8):
        total = total + hop(total, bits)
    scores = jnp.sum(total.reshape(SEQS, QUERIES, QLEN), axis=2).T

    pair = own_rows.reshape(HALF, 2, 8, TILE_A)
    kept = lax.dynamic_index_in_dim(pair, x, 1, False)
    came = lax.ppermute(lax.dynamic_index_in_dim(pair, 1 - x, 1, False), "parts", SWAP)
    low = jnp.where(x == 0, kept, came).reshape(NQ, 1, 2, 8, TILE_A)
    high = jnp.where(x == 0, came, kept).reshape(NQ, 1, 2, 8, TILE_A)
    by_slot = jnp.concatenate([low, high], axis=1).reshape(64, 8, TILE_A)
    ordered = jnp.take(by_slot, slot_list, axis=0, mode="clip")
    rotated_out = (
        ordered.reshape(LAYERS, 32, 8, TILE_A).transpose(0, 2, 1, 3).reshape(LAYERS, 8, D)
    )
    return (scores, rotated_out)


def solution(mesh):
    paired = mesh.shape["parts"] == 2 and mesh.shape["query"] == NQ
    return jax.shard_map(
        paired_body if paired else general_body,
        mesh=mesh,
        in_specs=(
            P(None, ("parts", "query"), None),
            P(None, "parts", "query"),
            P("parts"),
            P(None, "query", None),
            P(None, None, "query"),
            P(None, "query", None),
            P("query", None, None),
            P(),
            P(None, "query", None, None),
        ),
        out_specs=(P(None, "parts"), P(None, ("parts", "query"), None)),
        check_vma=False,
    )
```

```python
import jax
import jax.numpy as jnp
from jax import lax
from jax.experimental import pallas as pl
from jax.experimental.pallas import tpu as pltpu
from jax.sharding import PartitionSpec as P

D = 4096
LAYERS = 2
TILE_A = 128
TILE_S = 64
SEQS = 4
QUERIES = 16
QLEN = 16


damping = 0.05


def rotate_blocks(rows, block_tiles, width):
    layer_count, row_count, feature_count = rows.shape
    blocks = rows.reshape(layer_count, row_count, feature_count // width, width)
    shaped = block_tiles.reshape(layer_count, feature_count // width, width, width)
    turned = jnp.einsum("lrbi,lbij->lrbj", blocks, shaped, preferred_element_type=jnp.float32)
    return turned.reshape(layer_count, row_count, feature_count).astype(jnp.bfloat16)


def general_body(
    train_inputs,
    train_outgrads,
    sequence_ids,
    query_inputs,
    query_outgrads,
    eigenvalues,
    input_basis,
    slot_list,
    output_basis,
):
    every_slot = lax.all_gather(input_basis, "query", axis=0, tiled=True)
    basis_tiles = jnp.take(every_slot, slot_list, axis=0)
    rotated_out = rotate_blocks(train_inputs, basis_tiles, TILE_A)
    own_query = rotate_blocks(query_inputs, basis_tiles, TILE_A)
    rotated_train, rotated_query = (
        lax.all_gather(rotated_out, "query", axis=1, tiled=True),
        lax.all_gather(own_query, "query", axis=1, tiled=True),
    )
    grads_rot = rotate_blocks(train_outgrads, output_basis, TILE_S)
    query_rot = rotate_blocks(query_outgrads, output_basis, TILE_S)
    token_count = grads_rot.shape[1]
    slab_width = grads_rot.shape[2]
    weights = 1.0 / (eigenvalues + damping)
    onehot = (sequence_ids[:, None] == jnp.arange(SEQS, dtype=jnp.int32)[None, :]).astype(
        jnp.bfloat16
    )
    totals = jnp.zeros((SEQS, QUERIES * QLEN), jnp.float32)
    for layer_index in range(LAYERS):
        masked = (onehot[:, :, None] * grads_rot[layer_index][:, None, :]).reshape(
            token_count, SEQS * slab_width
        )
        gram_block = lax.dot_general(
            masked,
            rotated_train[layer_index],
            (((0,), (0,)), ((), ())),
            preferred_element_type=jnp.float32,
        )
        scaled = (gram_block.reshape(SEQS, slab_width, D) * weights[layer_index][None]).astype(
            jnp.bfloat16
        )
        projected = jnp.einsum(
            "sij,uj->siu", scaled, rotated_query[layer_index], preferred_element_type=jnp.float32
        )
        totals = totals + jnp.einsum(
            "siu,ui->su", projected, query_rot[layer_index].astype(jnp.float32)
        )
    partial_value = jnp.sum(totals.reshape(SEQS, QUERIES, QLEN), axis=2).T
    scores = lax.psum(partial_value, "query")
    return (scores, rotated_out)


NQ = 16
WAVES = 2
GROUPS = 2 * SEQS
TOKENS = 256
UNIT = 20
SWAP = [(0, 1), (1, 0)]
BF = jnp.bfloat16


def hop(value, bits):
    return lax.ppermute(value, "query", [(i, i ^ bits) for i in range(NQ)])


def pack_kernel(info, own, other, query, basis, *units):
    x = info[0]

    for wave in range(WAVES):
        unit = units[wave]

        @pl.loop(0, NQ)
        def _(owner):
            tile = info[1 + wave * NQ + owner]
            layer = tile // 32
            cols = pl.ds(pl.multiple_of((tile % 32) * TILE_A, TILE_A), TILE_A)
            mine = own[layer, :, cols].astype(jnp.float32)
            came = other[layer, :, cols].astype(jnp.float32)
            first = jnp.where(x == 0, mine, came)
            second = jnp.where(x == 0, came, mine)
            unit[owner, :16, :] = jnp.concatenate([first, second], axis=0).astype(BF)
            unit[owner, 16:, :] = query[layer, :, cols]

        unit[NQ:] = basis[2 * x + wave].reshape(4, 32, TILE_A)


def score_kernel(wave, info, *refs):
    units = refs[:NQ]
    grads, query_grads, codes, eigen, before, totals, own_rows = refs[NQ : NQ + 7]
    held, turned_rows, train_t, query_t, eig, scaled0, scaled1, weights, acc = refs[NQ + 7 : NQ + 16]
    unit_sems, eig_sems = refs[NQ + 16 :]
    scaled = (scaled0, scaled1)
    me = info[0]
    copies = [
        pltpu.make_async_copy(units[d], held.at[me ^ d], unit_sems.at[d]) for d in range(NQ)
    ]
    for copy in copies:
        copy.start()

    def eig_copy(n):
        tile = info[1 + wave * NQ + n]
        cols = pl.ds(pl.multiple_of((tile % 32) * TILE_A, TILE_A), TILE_A)
        return pltpu.make_async_copy(eigen.at[tile // 32, :, cols], eig.at[n], eig_sems.at[n])

    for n in range(NQ):
        eig_copy(n).start()
    acc[...] = jnp.zeros_like(acc)
    for copy in copies:
        copy.wait()

    @pl.loop(0, NQ)
    def _(n):
        basis = held[n, NQ:].reshape(TILE_A, TILE_A)
        tile = held[:, n]
        train = tile[:, :16].reshape(TOKENS, TILE_A)
        query = tile[:, 16:].reshape(TOKENS, TILE_A)
        turned = jnp.dot(train, basis, preferred_element_type=jnp.float32)
        turned_rows[...] = turned.astype(BF)
        own_rows[n] = turned_rows[pl.ds(pl.multiple_of(me * 16, 16), 16), :]
        train_t[n] = turned.T.astype(BF)
        query_t[n] = jnp.dot(query, basis, preferred_element_type=jnp.float32).T.astype(BF)

    def weigh(n, k):
        weights[k] = 1.0 / (eig[n].T + damping)

    def gram(n, k):
        layer = info[1 + wave * NQ + n] // 32
        code = codes[...]
        rows = train_t[n]
        zero = jnp.zeros_like(rows)
        for h in range(2):
            left = jnp.concatenate(
                [jnp.where(code == s, rows, zero) for s in range(4 * h, 4 * h + 4)], axis=0
            )
            for c in range(3):
                cols = slice(c * 256, (c + 1) * 256)
                part = jnp.dot(left, grads[layer, :, cols], preferred_element_type=jnp.float32)
                part = part.reshape(4, TILE_A, 256) * weights[k, :, cols][None]
                scaled[k][h * 512 : (h + 1) * 512, cols] = part.astype(BF).reshape(512, 256)

    def project(n, k):
        layer = info[1 + wave * NQ + n] // 32
        query = query_t[n].astype(jnp.float32)
        for h in range(2):
            part = jnp.dot(
                scaled[k][h * 512 : (h + 1) * 512, :],
                query_grads[layer],
                preferred_element_type=jnp.float32,
            )
            part = part.reshape(4, TILE_A, TOKENS) * query[None]
            acc[4 * h : 4 * h + 4] += jnp.sum(part.reshape(4, TILE_A // 8, 8, TOKENS), axis=1)

    eig_copy(0).wait()
    weigh(0, 0)
    eig_copy(1).wait()
    weigh(1, 1)
    gram(0, 0)

    @pl.loop(0, NQ - 2, step=2)
    def _(n):
        eig_copy(n + 2).wait()
        eig_copy(n + 3).wait()
        gram(n + 1, 1)
        project(n, 0)
        weigh(n + 2, 0)
        gram(n + 2, 0)
        project(n + 1, 1)
        weigh(n + 3, 1)

    gram(NQ - 1, 1)
    project(NQ - 2, 0)
    project(NQ - 1, 1)
    totals[...] = before[...] + jnp.sum(acc[...], axis=1)


VMEM = pl.BlockSpec(memory_space=pltpu.VMEM)
SMEM = pl.BlockSpec(memory_space=pltpu.SMEM)
ANY = pl.BlockSpec(memory_space=pl.ANY)


def score_wave(wave, info, units, grads, query_grads, codes, eigenvalues, before):
    width = grads.shape[2]

    def kernel(*refs):
        score_kernel(wave, *refs)

    return pl.pallas_call(
        kernel,
        in_specs=[SMEM] + [ANY] * NQ + [VMEM, VMEM, VMEM, ANY, VMEM],
        out_specs=[VMEM, VMEM],
        out_shape=[
            jax.ShapeDtypeStruct((GROUPS, TOKENS), jnp.float32),
            jax.ShapeDtypeStruct((NQ, 16, TILE_A), BF),
        ],
        scratch_shapes=[
            pltpu.VMEM((NQ, UNIT, 32, TILE_A), BF),
            pltpu.VMEM((TOKENS, TILE_A), BF),
            pltpu.VMEM((NQ, TILE_A, TOKENS), BF),
            pltpu.VMEM((NQ, TILE_A, TOKENS), BF),
            pltpu.VMEM((NQ, width, TILE_A), jnp.float32),
            pltpu.VMEM((GROUPS * TILE_A, width), BF),
            pltpu.VMEM((GROUPS * TILE_A, width), BF),
            pltpu.VMEM((2, TILE_A, width), jnp.float32),
            pltpu.VMEM((GROUPS, 8, TOKENS), jnp.float32),
            pltpu.SemaphoreType.DMA((NQ,)),
            pltpu.SemaphoreType.DMA((NQ,)),
        ],
        compiler_params=pltpu.CompilerParams(vmem_limit_bytes=40 * 1024 * 1024),
        cost_estimate=pl.CostEstimate(
            flops=20 * 10**9, bytes_accessed=10 * 10**6, transcendentals=0
        ),
    )(info, *units, grads, query_grads, codes, eigenvalues, before)


def gather_units(unit):
    units = [None] * NQ
    units[0] = unit
    for d in (4, 12, 8):
        units[d] = hop(unit, d)
    for d in (0, 4, 12, 8):
        units[d ^ 2] = hop(units[d], 2)
    for d in (0, 2, 4, 6, 12, 14, 8, 10):
        units[d ^ 1] = hop(units[d], 1)
    return units


def paired_body(
    train_inputs,
    train_outgrads,
    sequence_ids,
    query_inputs,
    query_outgrads,
    eigenvalues,
    input_basis,
    slot_list,
    output_basis,
):
    x = lax.axis_index("parts")
    me = lax.axis_index("query")
    train_other = lax.ppermute(train_inputs, "parts", SWAP)
    ids = jnp.arange(64, dtype=jnp.int32)
    tile_of = jnp.sum(jnp.where(slot_list[None, :] == ids[:, None], ids[None, :], 0), axis=1)
    mine = lax.dynamic_index_in_dim(tile_of.reshape(NQ, 2, WAVES), x, 1, False)
    mine = mine.T.reshape(WAVES * NQ)

    packed = pl.pallas_call(
        pack_kernel,
        in_specs=[SMEM, VMEM, VMEM, VMEM, VMEM],
        out_specs=[VMEM] * WAVES,
        out_shape=[jax.ShapeDtypeStruct((UNIT, 32, TILE_A), BF)] * WAVES,
    )(
        jnp.concatenate([x.reshape(1).astype(jnp.int32), mine]),
        train_inputs,
        train_other,
        query_inputs,
        input_basis,
    )
    waves = [gather_units(unit) for unit in packed]

    slab = train_outgrads.shape[2]
    id_block = jnp.broadcast_to(sequence_ids.astype(BF)[None, :, None], (LAYERS, 128, TILE_A))
    sent = jnp.concatenate([train_outgrads, id_block], axis=2)
    other = lax.ppermute(sent, "parts", SWAP)
    both = jnp.stack(
        [jnp.where(x == 0, sent, other), jnp.where(x == 0, other, sent)], axis=0
    ).reshape(2, LAYERS, NQ, 8, slab + TILE_A)
    both = both.transpose(1, 2, 0, 3, 4).reshape(LAYERS, TOKENS, slab + TILE_A)
    part_of = (jnp.arange(TOKENS, dtype=jnp.int32) // 8) % 2
    codes = (both[0, :, slab].astype(jnp.int32) + SEQS * part_of).reshape(1, TOKENS)
    grads_rot = rotate_blocks(both[:, :, :slab], output_basis, TILE_S)
    query_rot = rotate_blocks(query_outgrads, output_basis, TILE_S).transpose(0, 2, 1)

    info = jnp.concatenate([me.reshape(1).astype(jnp.int32), mine])
    totals = jnp.zeros((GROUPS, TOKENS), jnp.float32)
    own_rows = [None] * WAVES
    for wave in range(WAVES):
        totals, own_rows[wave] = score_wave(
            wave, info, waves[wave], grads_rot, query_rot, codes, eigenvalues, totals
        )

    halves = totals.reshape(2, SEQS, TOKENS)
    keep = lax.dynamic_index_in_dim(halves, x, 0, False)
    give = lax.dynamic_index_in_dim(halves, 1 - x, 0, False)
    total = keep + lax.ppermute(give, "parts", SWAP)
    for bits in (1, 2, 4, 8):
        total = total + hop(total, bits)
    scores = jnp.sum(total.reshape(SEQS, QUERIES, QLEN), axis=2).T

    slots = [None] * 4
    for wave in range(WAVES):
        pair = own_rows[wave].reshape(NQ, 2, 8, TILE_A)
        kept = lax.dynamic_index_in_dim(pair, x, 1, False)
        came = lax.ppermute(lax.dynamic_index_in_dim(pair, 1 - x, 1, False), "parts", SWAP)
        slots[wave] = jnp.where(x == 0, kept, came)
        slots[2 + wave] = jnp.where(x == 0, came, kept)
    by_slot = jnp.stack(slots, axis=1).reshape(64, 8, TILE_A)
    ordered = jnp.take(by_slot, slot_list, axis=0, mode="clip")
    rotated_out = (
        ordered.reshape(LAYERS, 32, 8, TILE_A).transpose(0, 2, 1, 3).reshape(LAYERS, 8, D)
    )
    return (scores, rotated_out)


def solution(mesh):
    paired = mesh.shape["parts"] == 2 and mesh.shape["query"] == NQ
    return jax.shard_map(
        paired_body if paired else general_body,
        mesh=mesh,
        in_specs=(
            P(None, ("parts", "query"), None),
            P(None, "parts", "query"),
            P("parts"),
            P(None, "query", None),
            P(None, None, "query"),
            P(None, "query", None),
            P("query", None, None),
            P(),
            P(None, "query", None, None),
        ),
        out_specs=(P(None, "parts"), P(None, ("parts", "query"), None)),
        check_vma=False,
    )
```

```python
import jax
import jax.numpy as jnp
from jax import lax
from jax.experimental import pallas as pl
from jax.experimental.pallas import tpu as pltpu
from jax.sharding import PartitionSpec as P

D = 4096
LAYERS = 2
TILE_A = 128
TILE_S = 64
SEQS = 4
QUERIES = 16
QLEN = 16


damping = 0.05


def rotate_blocks(rows, block_tiles, width):
    layer_count, row_count, feature_count = rows.shape
    blocks = rows.reshape(layer_count, row_count, feature_count // width, width)
    shaped = block_tiles.reshape(layer_count, feature_count // width, width, width)
    turned = jnp.einsum("lrbi,lbij->lrbj", blocks, shaped, preferred_element_type=jnp.float32)
    return turned.reshape(layer_count, row_count, feature_count).astype(jnp.bfloat16)


def general_body(
    train_inputs,
    train_outgrads,
    sequence_ids,
    query_inputs,
    query_outgrads,
    eigenvalues,
    input_basis,
    slot_list,
    output_basis,
):
    every_slot = lax.all_gather(input_basis, "query", axis=0, tiled=True)
    basis_tiles = jnp.take(every_slot, slot_list, axis=0)
    rotated_out = rotate_blocks(train_inputs, basis_tiles, TILE_A)
    own_query = rotate_blocks(query_inputs, basis_tiles, TILE_A)
    rotated_train, rotated_query = (
        lax.all_gather(rotated_out, "query", axis=1, tiled=True),
        lax.all_gather(own_query, "query", axis=1, tiled=True),
    )
    grads_rot = rotate_blocks(train_outgrads, output_basis, TILE_S)
    query_rot = rotate_blocks(query_outgrads, output_basis, TILE_S)
    token_count = grads_rot.shape[1]
    slab_width = grads_rot.shape[2]
    weights = 1.0 / (eigenvalues + damping)
    onehot = (sequence_ids[:, None] == jnp.arange(SEQS, dtype=jnp.int32)[None, :]).astype(
        jnp.bfloat16
    )
    totals = jnp.zeros((SEQS, QUERIES * QLEN), jnp.float32)
    for layer_index in range(LAYERS):
        masked = (onehot[:, :, None] * grads_rot[layer_index][:, None, :]).reshape(
            token_count, SEQS * slab_width
        )
        gram_block = lax.dot_general(
            masked,
            rotated_train[layer_index],
            (((0,), (0,)), ((), ())),
            preferred_element_type=jnp.float32,
        )
        scaled = (gram_block.reshape(SEQS, slab_width, D) * weights[layer_index][None]).astype(
            jnp.bfloat16
        )
        projected = jnp.einsum(
            "sij,uj->siu", scaled, rotated_query[layer_index], preferred_element_type=jnp.float32
        )
        totals = totals + jnp.einsum(
            "siu,ui->su", projected, query_rot[layer_index].astype(jnp.float32)
        )
    partial_value = jnp.sum(totals.reshape(SEQS, QUERIES, QLEN), axis=2).T
    scores = lax.psum(partial_value, "query")
    return (scores, rotated_out)


NQ = 16
WAVES = 2
GROUPS = 2 * SEQS
TOKENS = 256
UNIT = 20
SWAP = [(0, 1), (1, 0)]
BF = jnp.bfloat16


def hop(value, bits):
    return lax.ppermute(value, "query", [(i, i ^ bits) for i in range(NQ)])


def pack_kernel(info, own, other, query, basis, *units):
    x = info[0]

    for wave in range(WAVES):
        unit = units[wave]

        @pl.loop(0, NQ)
        def _(owner):
            tile = info[1 + wave * NQ + owner]
            layer = tile // 32
            cols = pl.ds(pl.multiple_of((tile % 32) * TILE_A, TILE_A), TILE_A)
            mine = own[layer, :, cols].astype(jnp.float32)
            came = other[layer, :, cols].astype(jnp.float32)
            first = jnp.where(x == 0, mine, came)
            second = jnp.where(x == 0, came, mine)
            unit[owner, :16, :] = jnp.concatenate([first, second], axis=0).astype(BF)
            unit[owner, 16:, :] = query[layer, :, cols]

        unit[NQ:] = basis[2 * x + wave].reshape(4, 32, TILE_A)


def prepare_kernel(info, own, other, query, block, block_t, grads, query_grads):
    x = info[0]
    for layer in range(LAYERS):
        for c in range(block.shape[1]):
            cols = slice(c * TILE_A, (c + 1) * TILE_A)
            tile = block[layer, c]
            mine = jnp.dot(own[layer, :, cols], tile, preferred_element_type=jnp.float32)
            came = jnp.dot(other[layer, :, cols], tile, preferred_element_type=jnp.float32)
            first = jnp.where(x == 0, mine, came).reshape(NQ, 1, 8, TILE_A)
            second = jnp.where(x == 0, came, mine).reshape(NQ, 1, 8, TILE_A)
            rows = jnp.concatenate([first, second], axis=1).reshape(TOKENS, TILE_A)
            grads[layer, :, cols] = rows.astype(BF)
            query_grads[layer, cols, :] = across(block_t[layer, c], query[layer, :, cols]).astype(BF)


def across(left, right):
    return lax.dot_general(
        left, right, (((1,), (1,)), ((), ())), preferred_element_type=jnp.float32
    )


def score_kernel(base, count, info, *refs):
    units = refs[:NQ]
    grads, query_grads, codes, eigen, before, totals, own_rows = refs[NQ : NQ + 7]
    held, turned_rows, train_t, query_t, eig, scaled0, scaled1, weights, acc = refs[NQ + 7 : NQ + 16]
    unit_sems, eig_sems = refs[NQ + 16 :]
    scaled = (scaled0, scaled1)
    me = info[0]
    start = base % NQ
    wave = base // NQ
    copies = []
    for d in range(NQ):
        unit, which = units[d]
        source = unit if which is None else unit.at[which]
        into = held.at[me ^ d]
        copies.append(
            pltpu.make_async_copy(
                source.at[pl.ds(start, count)], into.at[pl.ds(0, count)], unit_sems.at[d]
            )
        )
        copies.append(
            pltpu.make_async_copy(
                source.at[pl.ds(NQ, 4)], into.at[pl.ds(NQ, 4)], unit_sems.at[NQ + d]
            )
        )
    for copy in copies:
        copy.start()

    def eig_copy(n):
        tile = info[1 + base + n]
        cols = pl.ds(pl.multiple_of((tile % 32) * TILE_A, TILE_A), TILE_A)
        return pltpu.make_async_copy(eigen.at[tile // 32, :, cols], eig.at[n], eig_sems.at[n])

    for n in range(count):
        eig_copy(n).start()
    acc[...] = jnp.zeros_like(acc)
    for copy in copies:
        copy.wait()

    def rotate(n):
        basis = held[start + n, NQ:].reshape(TILE_A, TILE_A)
        basis_t = basis.astype(jnp.float32).T.astype(BF)
        tile = held[:, n]
        train = tile[:, :16].reshape(TOKENS, TILE_A)
        query = tile[:, 16:].reshape(TOKENS, TILE_A)
        mine = held[me, n, :16]
        own_rows[n] = jnp.dot(mine, basis, preferred_element_type=jnp.float32).astype(BF)
        train_t[n] = across(basis_t, train).astype(BF)
        query_t[n] = across(basis_t, query).astype(BF)

    def weigh(n, k):
        weights[k] = 1.0 / (eig[n].T + damping)

    def gram(n, k):
        layer = info[1 + base + n] // 32
        code = codes[...]
        rows = train_t[n]
        zero = jnp.zeros_like(rows)
        for h in range(2):
            left = jnp.concatenate(
                [jnp.where(code == s, rows, zero) for s in range(4 * h, 4 * h + 4)], axis=0
            )
            for c in range(3):
                cols = slice(c * 256, (c + 1) * 256)
                part = jnp.dot(left, grads[layer, :, cols], preferred_element_type=jnp.float32)
                part = part.reshape(4, TILE_A, 256) * weights[k, :, cols][None]
                scaled[k][h * 512 : (h + 1) * 512, cols] = part.astype(BF).reshape(512, 256)

    def project(n, k):
        layer = info[1 + base + n] // 32
        query = query_t[n].astype(jnp.float32)
        for h in range(2):
            part = jnp.dot(
                scaled[k][h * 512 : (h + 1) * 512, :],
                query_grads[layer],
                preferred_element_type=jnp.float32,
            )
            part = part.reshape(4, TILE_A, TOKENS) * query[None]
            acc[4 * h : 4 * h + 4] += jnp.sum(part.reshape(4, TILE_A // 8, 8, TOKENS), axis=1)

    rotate(0)
    rotate(1)
    eig_copy(0).wait()
    weigh(0, 0)
    eig_copy(1).wait()
    weigh(1, 1)
    gram(0, 0)

    @pl.loop(0, count - 2, step=2)
    def _(n):
        eig_copy(n + 2).wait()
        eig_copy(n + 3).wait()
        gram(n + 1, 1)
        rotate(n + 2)
        project(n, 0)
        weigh(n + 2, 0)
        gram(n + 2, 0)
        rotate(n + 3)
        project(n + 1, 1)
        weigh(n + 3, 1)

    gram(count - 1, 1)
    project(count - 2, 0)
    project(count - 1, 1)
    totals[...] = before[...] + jnp.sum(acc[...], axis=1)


VMEM = pl.BlockSpec(memory_space=pltpu.VMEM)
SMEM = pl.BlockSpec(memory_space=pltpu.SMEM)
HBM = pl.BlockSpec(memory_space=pltpu.HBM)


def score_tiles(base, count, info, arrays, places, grads, query_grads, codes, eigenvalues, before):
    width = grads.shape[2]

    def kernel(info_ref, *refs):
        held = refs[: len(arrays)]
        units = [(held[a], which) for a, which in places]
        score_kernel(base, count, info_ref, *units, *refs[len(arrays) :])

    return pl.pallas_call(
        kernel,
        in_specs=[SMEM] + [HBM] * len(arrays) + [VMEM, VMEM, VMEM, HBM, VMEM],
        out_specs=[VMEM, VMEM],
        out_shape=[
            jax.ShapeDtypeStruct((GROUPS, TOKENS), jnp.float32),
            jax.ShapeDtypeStruct((count, 16, TILE_A), BF),
        ],
        scratch_shapes=[
            pltpu.VMEM((NQ, UNIT, 32, TILE_A), BF),
            pltpu.VMEM((TOKENS, TILE_A), BF),
            pltpu.VMEM((count, TILE_A, TOKENS), BF),
            pltpu.VMEM((count, TILE_A, TOKENS), BF),
            pltpu.VMEM((count, width, TILE_A), jnp.float32),
            pltpu.VMEM((GROUPS * TILE_A, width), BF),
            pltpu.VMEM((GROUPS * TILE_A, width), BF),
            pltpu.VMEM((2, TILE_A, width), jnp.float32),
            pltpu.VMEM((GROUPS, 8, TOKENS), jnp.float32),
            pltpu.SemaphoreType.DMA((2 * NQ,)),
            pltpu.SemaphoreType.DMA((count,)),
        ],
        compiler_params=pltpu.CompilerParams(vmem_limit_bytes=62 * 1024 * 1024),
        cost_estimate=pl.CostEstimate(
            flops=count * 10**9, bytes_accessed=count * 10**6 // 2, transcendentals=0
        ),
    )(info, *arrays, grads, query_grads, codes, eigenvalues, before)


def after(value, *others):
    return lax.optimization_barrier((value, *others))[0]


def paired_body(
    train_inputs,
    train_outgrads,
    sequence_ids,
    query_inputs,
    query_outgrads,
    eigenvalues,
    input_basis,
    slot_list,
    output_basis,
):
    x = lax.axis_index("parts")
    me = lax.axis_index("query")
    train_other = lax.ppermute(train_inputs, "parts", SWAP)
    ids = jnp.arange(64, dtype=jnp.int32)
    tile_of = jnp.sum(jnp.where(slot_list[None, :] == ids[:, None], ids[None, :], 0), axis=1)
    mine = lax.dynamic_index_in_dim(tile_of.reshape(NQ, 2, WAVES), x, 1, False)
    mine = mine.T.reshape(WAVES * NQ)
    side = x.reshape(1).astype(jnp.int32)

    packed = pl.pallas_call(
        pack_kernel,
        in_specs=[SMEM, VMEM, VMEM, VMEM, VMEM],
        out_specs=[VMEM] * WAVES,
        out_shape=[jax.ShapeDtypeStruct((UNIT, 32, TILE_A), BF)] * WAVES,
    )(jnp.concatenate([side, mine]), train_inputs, train_other, query_inputs, input_basis)

    units = [None] * NQ
    units[0] = packed[0]
    for d in (4, 12, 8):
        units[d] = hop(packed[0], d)
    for d in (0, 4, 12, 8):
        units[d ^ 2] = hop(units[d], 2)
    for d in (0, 2, 4, 6, 12, 14, 8, 10):
        units[d ^ 1] = hop(units[d], 1)
    places0 = [(d, None) for d in range(NQ)]

    ids_other = lax.ppermute(sequence_ids, "parts", SWAP)
    out_other = lax.ppermute(after(train_outgrads, packed[0]), "parts", SWAP)
    id_pair = jnp.where(
        x == 0, jnp.stack([sequence_ids, ids_other]), jnp.stack([ids_other, sequence_ids])
    )
    id_pair = id_pair + SEQS * jnp.arange(2, dtype=jnp.int32)[:, None]
    codes = id_pair.reshape(2, NQ, 8).transpose(1, 0, 2).reshape(1, TOKENS)
    slab = train_outgrads.shape[2]
    pairs = output_basis.reshape(LAYERS, slab // TILE_A, 2, TILE_S, TILE_S)
    blank = jnp.zeros_like(pairs[:, :, 0])
    block = jnp.concatenate(
        [
            jnp.concatenate([pairs[:, :, 0], blank], axis=3),
            jnp.concatenate([blank, pairs[:, :, 1]], axis=3),
        ],
        axis=2,
    )
    grads, query_grads = pl.pallas_call(
        prepare_kernel,
        in_specs=[SMEM] + [VMEM] * 5,
        out_specs=[VMEM, VMEM],
        out_shape=[
            jax.ShapeDtypeStruct((LAYERS, TOKENS, slab), BF),
            jax.ShapeDtypeStruct((LAYERS, slab, TOKENS), BF),
        ],
    )(side, train_outgrads, out_other, query_outgrads, block, block.transpose(0, 1, 3, 2))

    info = jnp.concatenate([me.reshape(1).astype(jnp.int32), mine])
    zero = jnp.zeros((GROUPS, TOKENS), jnp.float32)
    common = (grads, query_grads, codes, eigenvalues)
    part0, rows0 = score_tiles(0, 8, info, units, places0, *common, zero)

    second = after(packed[1], units[8])
    along = [second] + [hop(second, d) for d in (4, 12, 8)]
    line = jnp.stack(lax.optimization_barrier((*along, part0))[:4])
    beside = hop(line, 2)
    part1, rows1 = score_tiles(8, 8, info, units, places0, *common, part0)
    beside = after(beside, part1)
    line_core, beside_core = hop(line, 1), hop(beside, 1)
    order = {0: 0, 4: 1, 12: 2, 8: 3}
    places1 = [((d & 2) // 2 + 2 * (d & 1), order[d & 12]) for d in range(NQ)]
    totals, rows2 = score_tiles(
        16, 16, info, [line, beside, line_core, beside_core], places1, *common, part1
    )

    halves = totals.reshape(2, SEQS, TOKENS)
    keep = lax.dynamic_index_in_dim(halves, x, 0, False)
    give = lax.dynamic_index_in_dim(halves, 1 - x, 0, False)
    total = keep + lax.ppermute(give, "parts", SWAP)
    for bits in (1, 2, 4, 8):
        total = total + hop(total, bits)
    scores = jnp.sum(total.reshape(SEQS, QUERIES, QLEN), axis=2).T

    slots = [None] * 4
    for wave, rows in enumerate((jnp.concatenate([rows0, rows1], axis=0), rows2)):
        pair = rows.reshape(NQ, 2, 8, TILE_A)
        kept = lax.dynamic_index_in_dim(pair, x, 1, False)
        came = lax.ppermute(lax.dynamic_index_in_dim(pair, 1 - x, 1, False), "parts", SWAP)
        slots[wave] = jnp.where(x == 0, kept, came)
        slots[2 + wave] = jnp.where(x == 0, came, kept)
    by_slot = jnp.stack(slots, axis=1).reshape(64, 8, TILE_A)
    ordered = jnp.take(by_slot, slot_list, axis=0, mode="clip")
    rotated_out = (
        ordered.reshape(LAYERS, 32, 8, TILE_A).transpose(0, 2, 1, 3).reshape(LAYERS, 8, D)
    )
    return (scores, rotated_out)


def solution(mesh):
    paired = mesh.shape["parts"] == 2 and mesh.shape["query"] == NQ
    return jax.shard_map(
        paired_body if paired else general_body,
        mesh=mesh,
        in_specs=(
            P(None, ("parts", "query"), None),
            P(None, "parts", "query"),
            P("parts"),
            P(None, "query", None),
            P(None, None, "query"),
            P(None, "query", None),
            P("query", None, None),
            P(),
            P(None, "query", None, None),
        ),
        out_specs=(P(None, "parts"), P(None, ("parts", "query"), None)),
        check_vma=False,
    )
```

```python
import jax
import jax.numpy as jnp
from jax import lax
from jax.experimental import pallas as pl
from jax.experimental.pallas import tpu as pltpu
from jax.sharding import PartitionSpec as P

D = 4096
LAYERS = 2
TILE_A = 128
TILE_S = 64
SEQS = 4
QUERIES = 16
QLEN = 16


damping = 0.05


def rotate_blocks(rows, block_tiles, width):
    layer_count, row_count, feature_count = rows.shape
    blocks = rows.reshape(layer_count, row_count, feature_count // width, width)
    shaped = block_tiles.reshape(layer_count, feature_count // width, width, width)
    turned = jnp.einsum("lrbi,lbij->lrbj", blocks, shaped, preferred_element_type=jnp.float32)
    return turned.reshape(layer_count, row_count, feature_count).astype(jnp.bfloat16)


def general_body(
    train_inputs,
    train_outgrads,
    sequence_ids,
    query_inputs,
    query_outgrads,
    eigenvalues,
    input_basis,
    slot_list,
    output_basis,
):
    every_slot = lax.all_gather(input_basis, "query", axis=0, tiled=True)
    basis_tiles = jnp.take(every_slot, slot_list, axis=0)
    rotated_out = rotate_blocks(train_inputs, basis_tiles, TILE_A)
    own_query = rotate_blocks(query_inputs, basis_tiles, TILE_A)
    rotated_train, rotated_query = (
        lax.all_gather(rotated_out, "query", axis=1, tiled=True),
        lax.all_gather(own_query, "query", axis=1, tiled=True),
    )
    grads_rot = rotate_blocks(train_outgrads, output_basis, TILE_S)
    query_rot = rotate_blocks(query_outgrads, output_basis, TILE_S)
    token_count = grads_rot.shape[1]
    slab_width = grads_rot.shape[2]
    weights = 1.0 / (eigenvalues + damping)
    onehot = (sequence_ids[:, None] == jnp.arange(SEQS, dtype=jnp.int32)[None, :]).astype(
        jnp.bfloat16
    )
    totals = jnp.zeros((SEQS, QUERIES * QLEN), jnp.float32)
    for layer_index in range(LAYERS):
        masked = (onehot[:, :, None] * grads_rot[layer_index][:, None, :]).reshape(
            token_count, SEQS * slab_width
        )
        gram_block = lax.dot_general(
            masked,
            rotated_train[layer_index],
            (((0,), (0,)), ((), ())),
            preferred_element_type=jnp.float32,
        )
        scaled = (gram_block.reshape(SEQS, slab_width, D) * weights[layer_index][None]).astype(
            jnp.bfloat16
        )
        projected = jnp.einsum(
            "sij,uj->siu", scaled, rotated_query[layer_index], preferred_element_type=jnp.float32
        )
        totals = totals + jnp.einsum(
            "siu,ui->su", projected, query_rot[layer_index].astype(jnp.float32)
        )
    partial_value = jnp.sum(totals.reshape(SEQS, QUERIES, QLEN), axis=2).T
    scores = lax.psum(partial_value, "query")
    return (scores, rotated_out)


NQ = 16
WAVES = 2
GROUPS = 2 * SEQS
TOKENS = 256
UNIT = 20
SWAP = [(0, 1), (1, 0)]
BF = jnp.bfloat16


def hop(value, bits):
    return lax.ppermute(value, "query", [(i, i ^ bits) for i in range(NQ)])


def pack_kernel(info, own, other, query, basis, *units):
    x = info[0]

    for wave in range(WAVES):
        unit = units[wave]

        @pl.loop(0, NQ)
        def _(owner):
            tile = info[1 + wave * NQ + owner]
            layer = tile // 32
            cols = pl.ds(pl.multiple_of((tile % 32) * TILE_A, TILE_A), TILE_A)
            mine = own[layer, :, cols].astype(jnp.float32)
            came = other[layer, :, cols].astype(jnp.float32)
            first = jnp.where(x == 0, mine, came)
            second = jnp.where(x == 0, came, mine)
            unit[owner, :16, :] = jnp.concatenate([first, second], axis=0).astype(BF)
            unit[owner, 16:, :] = query[layer, :, cols]

        unit[NQ:] = basis[2 * x + wave].reshape(4, 32, TILE_A)


def prepare_kernel(info, own, other, query, block, block_t, grads, query_grads):
    x = info[0]
    for layer in range(LAYERS):
        for c in range(block.shape[1]):
            cols = slice(c * TILE_A, (c + 1) * TILE_A)
            tile = block[layer, c]
            mine = jnp.dot(own[layer, :, cols], tile, preferred_element_type=jnp.float32)
            came = jnp.dot(other[layer, :, cols], tile, preferred_element_type=jnp.float32)
            first = jnp.where(x == 0, mine, came).reshape(NQ, 1, 8, TILE_A)
            second = jnp.where(x == 0, came, mine).reshape(NQ, 1, 8, TILE_A)
            rows = jnp.concatenate([first, second], axis=1).reshape(TOKENS, TILE_A)
            grads[layer, :, cols] = rows.astype(BF)
            query_grads[layer, cols, :] = across(block_t[layer, c], query[layer, :, cols]).astype(BF)


def across(left, right):
    return lax.dot_general(
        left, right, (((1,), (1,)), ((), ())), preferred_element_type=jnp.float32
    )


def score_kernel(base, count, last, info, *refs):
    units = refs[:NQ]
    grads, query_grads, codes, eigen, before = refs[NQ : NQ + 5]
    outs = refs[NQ + 5 : NQ + (9 if last else 8)]
    rows_kept, rows_given = outs[-2:]
    bases, train, query, train_t, query_t, eig, scaled0, scaled1, weights, acc, sems = refs[
        NQ + 5 + len(outs) :
    ]
    scaled = (scaled0, scaled1)
    me = info[0]
    x = info[1 + WAVES * NQ]
    start = base % NQ

    def piece(d, index):
        unit, which = units[d]
        return unit[index] if which is None else unit[which, index]

    def eig_copy(n):
        tile = info[1 + base + n]
        cols = pl.ds(pl.multiple_of((tile % 32) * TILE_A, TILE_A), TILE_A)
        return pltpu.make_async_copy(eigen.at[tile // 32, :, cols], eig.at[n], sems.at[n])

    for n in range(count):
        eig_copy(n).start()
    acc[...] = jnp.zeros_like(acc)
    for d in range(NQ):
        bases[me ^ d] = piece(d, slice(NQ, NQ + 4))

    def rotate(n):
        basis = bases[start + n].reshape(TILE_A, TILE_A)
        basis_t = basis.astype(jnp.float32).T.astype(BF)
        for d in range(NQ):
            rows = piece(d, start + n)
            place = pl.ds(pl.multiple_of((me ^ d) * 16, 16), 16)
            train[place, :] = rows[:16]
            query[place, :] = rows[16:]
        own = jnp.dot(piece(0, start + n)[:16], basis, preferred_element_type=jnp.float32)
        rows_kept[n] = jnp.where(x == 0, own[:8], own[8:]).astype(BF)
        rows_given[n] = jnp.where(x == 0, own[8:], own[:8]).astype(BF)
        train_t[n] = across(basis_t, train[...]).astype(BF)
        query_t[n] = across(basis_t, query[...]).astype(BF)

    def weigh(n, k):
        weights[k] = 1.0 / (eig[n].T + damping)

    def gram(n, k):
        layer = info[1 + base + n] // 32
        code = codes[...]
        rows = train_t[n]
        zero = jnp.zeros_like(rows)
        for h in range(2):
            left = jnp.concatenate(
                [jnp.where(code == s, rows, zero) for s in range(4 * h, 4 * h + 4)], axis=0
            )
            for c in range(3):
                cols = slice(c * 256, (c + 1) * 256)
                part = jnp.dot(left, grads[layer, :, cols], preferred_element_type=jnp.float32)
                part = part.reshape(4, TILE_A, 256) * weights[k, :, cols][None]
                scaled[k][h * 512 : (h + 1) * 512, cols] = part.astype(BF).reshape(512, 256)

    def project(n, k):
        layer = info[1 + base + n] // 32
        query = query_t[n].astype(jnp.float32)
        for h in range(2):
            part = jnp.dot(
                scaled[k][h * 512 : (h + 1) * 512, :],
                query_grads[layer],
                preferred_element_type=jnp.float32,
            )
            part = part.reshape(4, TILE_A, TOKENS) * query[None]
            acc[4 * h : 4 * h + 4] += jnp.sum(part.reshape(4, TILE_A // 8, 8, TOKENS), axis=1)

    rotate(0)
    rotate(1)
    eig_copy(0).wait()
    weigh(0, 0)
    eig_copy(1).wait()
    weigh(1, 1)
    gram(0, 0)

    @pl.loop(0, count - 2, step=2)
    def _(n):
        eig_copy(n + 2).wait()
        eig_copy(n + 3).wait()
        gram(n + 1, 1)
        rotate(n + 2)
        project(n, 0)
        weigh(n + 2, 0)
        gram(n + 2, 0)
        rotate(n + 3)
        project(n + 1, 1)
        weigh(n + 3, 1)

    gram(count - 1, 1)
    project(count - 2, 0)
    project(count - 1, 1)
    total = before[...] + jnp.sum(acc[...], axis=1)
    if last:
        outs[0][...] = jnp.where(x == 0, total[:SEQS], total[SEQS:])
        outs[1][...] = jnp.where(x == 0, total[SEQS:], total[:SEQS])
    else:
        outs[0][...] = total


VMEM = pl.BlockSpec(memory_space=pltpu.VMEM)
SMEM = pl.BlockSpec(memory_space=pltpu.SMEM)
HBM = pl.BlockSpec(memory_space=pltpu.HBM)


def score_tiles(base, count, last, info, arrays, places, grads, query_grads, codes, eigenvalues, before):
    width = grads.shape[2]

    def kernel(info_ref, *refs):
        held = refs[: len(arrays)]
        units = [(held[a], which) for a, which in places]
        score_kernel(base, count, last, info_ref, *units, *refs[len(arrays) :])

    sums = (
        [jax.ShapeDtypeStruct((SEQS, TOKENS), jnp.float32)] * 2
        if last
        else [jax.ShapeDtypeStruct((GROUPS, TOKENS), jnp.float32)]
    )
    rows = [jax.ShapeDtypeStruct((count, 8, TILE_A), BF)] * 2
    return pl.pallas_call(
        kernel,
        in_specs=[SMEM] + [VMEM] * len(arrays) + [VMEM, VMEM, VMEM, HBM, VMEM],
        out_specs=[VMEM] * len(sums + rows),
        out_shape=sums + rows,
        scratch_shapes=[
            pltpu.VMEM((NQ, 4, 32, TILE_A), BF),
            pltpu.VMEM((TOKENS, TILE_A), BF),
            pltpu.VMEM((TOKENS, TILE_A), BF),
            pltpu.VMEM((count, TILE_A, TOKENS), BF),
            pltpu.VMEM((count, TILE_A, TOKENS), BF),
            pltpu.VMEM((count, width, TILE_A), jnp.float32),
            pltpu.VMEM((GROUPS * TILE_A, width), BF),
            pltpu.VMEM((GROUPS * TILE_A, width), BF),
            pltpu.VMEM((2, TILE_A, width), jnp.float32),
            pltpu.VMEM((GROUPS, 8, TOKENS), jnp.float32),
            pltpu.SemaphoreType.DMA((count,)),
        ],
        compiler_params=pltpu.CompilerParams(vmem_limit_bytes=42 * 1024 * 1024),
        cost_estimate=pl.CostEstimate(
            flops=count * 10**9, bytes_accessed=count * 10**6 // 2, transcendentals=0
        ),
    )(info, *arrays, grads, query_grads, codes, eigenvalues, before)


def unpack_kernel(tiles, kept0, came0, kept1, came1, out):
    for half, pair in enumerate(((kept0, kept1), (came0, came1))):
        for wave in range(WAVES):
            source = pair[wave]

            @pl.loop(0, NQ)
            def _(owner):
                tile = tiles[half * WAVES * NQ + wave * NQ + owner]
                cols = pl.ds(pl.multiple_of((tile % 32) * TILE_A, TILE_A), TILE_A)
                out[tile // 32, :, cols] = source[owner]


def after(value, *others):
    return lax.optimization_barrier((value, *others))[0]


def paired_body(
    train_inputs,
    train_outgrads,
    sequence_ids,
    query_inputs,
    query_outgrads,
    eigenvalues,
    input_basis,
    slot_list,
    output_basis,
):
    x = lax.axis_index("parts")
    me = lax.axis_index("query")
    train_other = lax.ppermute(train_inputs, "parts", SWAP)
    ids = jnp.arange(64, dtype=jnp.int32)
    tile_of = jnp.sum(jnp.where(slot_list[None, :] == ids[:, None], ids[None, :], 0), axis=1)
    by_half = tile_of.reshape(NQ, 2, WAVES).transpose(1, 2, 0).reshape(2, WAVES * NQ)
    mine = jnp.where(x == 0, by_half[0], by_half[1])
    theirs = jnp.where(x == 0, by_half[1], by_half[0])
    side = x.reshape(1).astype(jnp.int32)

    packed = pl.pallas_call(
        pack_kernel,
        in_specs=[SMEM, VMEM, VMEM, VMEM, VMEM],
        out_specs=[VMEM] * WAVES,
        out_shape=[jax.ShapeDtypeStruct((UNIT, 32, TILE_A), BF)] * WAVES,
    )(jnp.concatenate([side, mine]), train_inputs, train_other, query_inputs, input_basis)

    ids_other = lax.ppermute(sequence_ids, "parts", SWAP)
    out_other = lax.ppermute(after(train_outgrads, train_other), "parts", SWAP)
    id_pair = jnp.where(
        x == 0, jnp.stack([sequence_ids, ids_other]), jnp.stack([ids_other, sequence_ids])
    )
    id_pair = id_pair + SEQS * jnp.arange(2, dtype=jnp.int32)[:, None]
    codes = id_pair.reshape(2, NQ, 8).transpose(1, 0, 2).reshape(1, TOKENS)
    slab = train_outgrads.shape[2]
    pairs = output_basis.reshape(LAYERS, slab // TILE_A, 2, TILE_S, TILE_S)
    blank = jnp.zeros_like(pairs[:, :, 0])
    block = jnp.concatenate(
        [
            jnp.concatenate([pairs[:, :, 0], blank], axis=3),
            jnp.concatenate([blank, pairs[:, :, 1]], axis=3),
        ],
        axis=2,
    )
    grads, query_grads = pl.pallas_call(
        prepare_kernel,
        in_specs=[SMEM] + [VMEM] * 5,
        out_specs=[VMEM, VMEM],
        out_shape=[
            jax.ShapeDtypeStruct((LAYERS, TOKENS, slab), BF),
            jax.ShapeDtypeStruct((LAYERS, slab, TOKENS), BF),
        ],
    )(side, train_outgrads, out_other, query_outgrads, block, block.transpose(0, 1, 3, 2))

    units = [None] * NQ
    units[0] = packed[0]
    for d in (4, 12, 8):
        units[d] = hop(packed[0], d)
    for d in (0, 4, 12):
        units[d ^ 2] = hop(units[d], 2)
    units[10] = hop(after(units[8], grads), 2)
    for d in (0, 2, 4, 6, 12, 14, 8, 10):
        units[d ^ 1] = hop(units[d], 1)
    places0 = [(d, None) for d in range(NQ)]

    info = jnp.concatenate([me.reshape(1).astype(jnp.int32), mine, side])
    zero = jnp.zeros((GROUPS, TOKENS), jnp.float32)
    common = (grads, query_grads, codes, eigenvalues)
    part0, kept_a, given_a = score_tiles(0, 8, False, info, units, places0, *common, zero)

    second = after(packed[1], units[8])
    along = [hop(second, d) for d in (4, 12, 8)]
    near = hop(second, 2)
    *along, near, _ = lax.optimization_barrier((*along, near, part0))
    line = jnp.stack(along)
    beside = hop(line, 2)
    part1, kept_b, given_b = score_tiles(8, 8, False, info, units, places0, *common, part0)
    beside = after(beside, part1)
    arrays = [second, near, line, beside]
    arrays = arrays + [hop(array, 1) for array in arrays]
    order = {4: 0, 12: 1, 8: 2}
    places1 = []
    for d in range(NQ):
        across_y = (d & 2) // 2 + 4 * (d & 1)
        far = d & 12
        places1.append((across_y + 2, order[far]) if far else (across_y, None))
    kept0 = jnp.concatenate([kept_a, kept_b], axis=0)
    came0 = lax.ppermute(jnp.concatenate([given_a, given_b], axis=0), "parts", SWAP)
    keep, give, kept1, given1 = score_tiles(
        16, 16, True, info, arrays, places1, *common, after(part1, came0)
    )

    total = keep + lax.ppermute(give, "parts", SWAP)
    came1 = lax.ppermute(given1, "parts", SWAP)
    rotated_out = pl.pallas_call(
        unpack_kernel,
        in_specs=[SMEM] + [VMEM] * 4,
        out_specs=VMEM,
        out_shape=jax.ShapeDtypeStruct(train_inputs.shape, BF),
    )(jnp.concatenate([mine, theirs]), kept0, came0, kept1, came1)
    for bits in (1, 2, 4):
        total = total + hop(total, bits)
    total = after(total, rotated_out)
    total = total + hop(total, 8)
    scores = jnp.sum(total.reshape(SEQS, QUERIES, QLEN), axis=2).T
    return (scores, rotated_out)


def solution(mesh):
    paired = mesh.shape["parts"] == 2 and mesh.shape["query"] == NQ
    return jax.shard_map(
        paired_body if paired else general_body,
        mesh=mesh,
        in_specs=(
            P(None, ("parts", "query"), None),
            P(None, "parts", "query"),
            P("parts"),
            P(None, "query", None),
            P(None, None, "query"),
            P(None, "query", None),
            P("query", None, None),
            P(),
            P(None, "query", None, None),
        ),
        out_specs=(P(None, "parts"), P(None, ("parts", "query"), None)),
        check_vma=False,
    )
```

```python
import jax
import jax.numpy as jnp
from jax import lax
from jax.experimental import pallas as pl
from jax.experimental.pallas import tpu as pltpu
from jax.sharding import PartitionSpec as P

D = 4096
LAYERS = 2
TILE_A = 128
TILE_S = 64
SEQS = 4
QUERIES = 16
QLEN = 16


damping = 0.05


def rotate_blocks(rows, block_tiles, width):
    layer_count, row_count, feature_count = rows.shape
    blocks = rows.reshape(layer_count, row_count, feature_count // width, width)
    shaped = block_tiles.reshape(layer_count, feature_count // width, width, width)
    turned = jnp.einsum("lrbi,lbij->lrbj", blocks, shaped, preferred_element_type=jnp.float32)
    return turned.reshape(layer_count, row_count, feature_count).astype(jnp.bfloat16)


def general_body(
    train_inputs,
    train_outgrads,
    sequence_ids,
    query_inputs,
    query_outgrads,
    eigenvalues,
    input_basis,
    slot_list,
    output_basis,
):
    every_slot = lax.all_gather(input_basis, "query", axis=0, tiled=True)
    basis_tiles = jnp.take(every_slot, slot_list, axis=0)
    rotated_out = rotate_blocks(train_inputs, basis_tiles, TILE_A)
    own_query = rotate_blocks(query_inputs, basis_tiles, TILE_A)
    rotated_train, rotated_query = (
        lax.all_gather(rotated_out, "query", axis=1, tiled=True),
        lax.all_gather(own_query, "query", axis=1, tiled=True),
    )
    grads_rot = rotate_blocks(train_outgrads, output_basis, TILE_S)
    query_rot = rotate_blocks(query_outgrads, output_basis, TILE_S)
    token_count = grads_rot.shape[1]
    slab_width = grads_rot.shape[2]
    weights = 1.0 / (eigenvalues + damping)
    onehot = (sequence_ids[:, None] == jnp.arange(SEQS, dtype=jnp.int32)[None, :]).astype(
        jnp.bfloat16
    )
    totals = jnp.zeros((SEQS, QUERIES * QLEN), jnp.float32)
    for layer_index in range(LAYERS):
        masked = (onehot[:, :, None] * grads_rot[layer_index][:, None, :]).reshape(
            token_count, SEQS * slab_width
        )
        gram_block = lax.dot_general(
            masked,
            rotated_train[layer_index],
            (((0,), (0,)), ((), ())),
            preferred_element_type=jnp.float32,
        )
        scaled = (gram_block.reshape(SEQS, slab_width, D) * weights[layer_index][None]).astype(
            jnp.bfloat16
        )
        projected = jnp.einsum(
            "sij,uj->siu", scaled, rotated_query[layer_index], preferred_element_type=jnp.float32
        )
        totals = totals + jnp.einsum(
            "siu,ui->su", projected, query_rot[layer_index].astype(jnp.float32)
        )
    partial_value = jnp.sum(totals.reshape(SEQS, QUERIES, QLEN), axis=2).T
    scores = lax.psum(partial_value, "query")
    return (scores, rotated_out)


NQ = 16
WAVES = 2
GROUPS = 2 * SEQS
TOKENS = 256
UNIT = 20
SWAP = [(0, 1), (1, 0)]
BF = jnp.bfloat16


def hop(value, bits):
    return lax.ppermute(value, "query", [(i, i ^ bits) for i in range(NQ)])


def pack_kernel(info, own, other, query, basis, *units):
    x = info[0]

    for wave in range(WAVES):
        unit = units[wave]

        for owner in range(NQ):
            tile = info[1 + wave * NQ + owner]
            layer = tile // 32
            cols = pl.ds(pl.multiple_of((tile % 32) * TILE_A, TILE_A), TILE_A)
            mine = own[layer, :, cols].astype(jnp.float32)
            came = other[layer, :, cols].astype(jnp.float32)
            first = jnp.where(x == 0, mine, came)
            second = jnp.where(x == 0, came, mine)
            unit[owner, :16, :] = jnp.concatenate([first, second], axis=0).astype(BF)
            unit[owner, 16:, :] = query[layer, :, cols]

        unit[NQ:] = basis[2 * x + wave].reshape(4, 32, TILE_A)


def prepare_kernel(info, own, other, query, tiles, grads, query_grads):
    x = info[0]
    blank = jnp.zeros((TILE_S, TILE_S), jnp.float32)
    for layer in range(LAYERS):
        for c in range(tiles.shape[1] // 2):
            cols = slice(c * TILE_A, (c + 1) * TILE_A)
            upper = jnp.concatenate([tiles[layer, 2 * c].astype(jnp.float32), blank], axis=1)
            lower = jnp.concatenate([blank, tiles[layer, 2 * c + 1].astype(jnp.float32)], axis=1)
            block = jnp.concatenate([upper, lower], axis=0)
            tile = block.astype(BF)
            mine = jnp.dot(own[layer, :, cols], tile, preferred_element_type=jnp.float32)
            came = jnp.dot(other[layer, :, cols], tile, preferred_element_type=jnp.float32)
            first = jnp.where(x == 0, mine, came).reshape(NQ, 1, 8, TILE_A)
            second = jnp.where(x == 0, came, mine).reshape(NQ, 1, 8, TILE_A)
            rows = jnp.concatenate([first, second], axis=1).reshape(TOKENS, TILE_A)
            grads[layer, :, cols] = rows.astype(BF)
            query_grads[layer, cols, :] = across(block.T.astype(BF), query[layer, :, cols]).astype(BF)


def across(left, right):
    return lax.dot_general(
        left, right, (((1,), (1,)), ((), ())), preferred_element_type=jnp.float32
    )


def score_kernel(base, count, last, info, *refs):
    units = refs[:NQ]
    grads, query_grads, codes, eigen, before = refs[NQ : NQ + 5]
    outs = refs[NQ + 5 : NQ + (9 if last else 8)]
    rows_kept, rows_given = outs[-2:]
    bases, train, query, train_t, query_t, eig, scaled0, scaled1, weights, acc, sems = refs[
        NQ + 5 + len(outs) :
    ]
    scaled = (scaled0, scaled1)
    me = info[0]
    x = info[1 + WAVES * NQ]
    start = base % NQ

    def piece(d, index):
        unit, which = units[d]
        return unit[index] if which is None else unit[which, index]

    def eig_copy(n):
        tile = info[1 + base + n]
        cols = pl.ds(pl.multiple_of((tile % 32) * TILE_A, TILE_A), TILE_A)
        return pltpu.make_async_copy(eigen.at[tile // 32, :, cols], eig.at[n], sems.at[n])

    for n in range(count):
        eig_copy(n).start()
    acc[...] = jnp.zeros_like(acc)
    for d in range(NQ):
        bases[me ^ d] = piece(d, slice(NQ, NQ + 4))

    def rotate(n):
        basis = bases[start + n].reshape(TILE_A, TILE_A)
        basis_t = basis.astype(jnp.float32).T.astype(BF)
        for d in range(NQ):
            rows = piece(d, start + n)
            place = pl.ds(pl.multiple_of((me ^ d) * 16, 16), 16)
            train[place, :] = rows[:16]
            query[place, :] = rows[16:]
        own = jnp.dot(piece(0, start + n)[:16], basis, preferred_element_type=jnp.float32)
        rows_kept[n] = jnp.where(x == 0, own[:8], own[8:]).astype(BF)
        rows_given[n] = jnp.where(x == 0, own[8:], own[:8]).astype(BF)
        train_t[n] = across(basis_t, train[...]).astype(BF)
        query_t[n] = across(basis_t, query[...]).astype(BF)

    def weigh(n, k):
        weights[k] = 1.0 / (eig[n].T + damping)

    def gram(n, k):
        layer = info[1 + base + n] // 32
        code = codes[...]
        rows = train_t[n]
        zero = jnp.zeros_like(rows)
        for h in range(2):
            left = jnp.concatenate(
                [jnp.where(code == s, rows, zero) for s in range(4 * h, 4 * h + 4)], axis=0
            )
            for c in range(3):
                cols = slice(c * 256, (c + 1) * 256)
                part = jnp.dot(left, grads[layer, :, cols], preferred_element_type=jnp.float32)
                part = part.reshape(4, TILE_A, 256) * weights[k, :, cols][None]
                scaled[k][h * 512 : (h + 1) * 512, cols] = part.astype(BF).reshape(512, 256)

    def project(n, k):
        layer = info[1 + base + n] // 32
        query = query_t[n].astype(jnp.float32)
        for h in range(2):
            part = jnp.dot(
                scaled[k][h * 512 : (h + 1) * 512, :],
                query_grads[layer],
                preferred_element_type=jnp.float32,
            )
            part = part.reshape(4, TILE_A, TOKENS) * query[None]
            acc[4 * h : 4 * h + 4] += jnp.sum(part.reshape(4, TILE_A // 8, 8, TOKENS), axis=1)

    rotate(0)
    rotate(1)
    eig_copy(0).wait()
    weigh(0, 0)
    eig_copy(1).wait()
    weigh(1, 1)
    gram(0, 0)

    @pl.loop(0, count - 2, step=2)
    def _(n):
        eig_copy(n + 2).wait()
        eig_copy(n + 3).wait()
        gram(n + 1, 1)
        rotate(n + 2)
        project(n, 0)
        weigh(n + 2, 0)
        gram(n + 2, 0)
        rotate(n + 3)
        project(n + 1, 1)
        weigh(n + 3, 1)

    gram(count - 1, 1)
    project(count - 2, 0)
    project(count - 1, 1)
    total = before[...] + jnp.sum(acc[...], axis=1)
    if last:
        outs[0][...] = jnp.where(x == 0, total[:SEQS], total[SEQS:])
        outs[1][...] = jnp.where(x == 0, total[SEQS:], total[:SEQS])
    else:
        outs[0][...] = total


VMEM = pl.BlockSpec(memory_space=pltpu.VMEM)
SMEM = pl.BlockSpec(memory_space=pltpu.SMEM)
HBM = pl.BlockSpec(memory_space=pltpu.HBM)


def score_tiles(base, count, last, info, arrays, places, grads, query_grads, codes, eigenvalues, before):
    width = grads.shape[2]

    def kernel(info_ref, *refs):
        held = refs[: len(arrays)]
        units = [(held[a], which) for a, which in places]
        score_kernel(base, count, last, info_ref, *units, *refs[len(arrays) :])

    sums = (
        [jax.ShapeDtypeStruct((SEQS, TOKENS), jnp.float32)] * 2
        if last
        else [jax.ShapeDtypeStruct((GROUPS, TOKENS), jnp.float32)]
    )
    rows = [jax.ShapeDtypeStruct((count, 8, TILE_A), BF)] * 2
    return pl.pallas_call(
        kernel,
        in_specs=[SMEM] + [VMEM] * len(arrays) + [VMEM, VMEM, VMEM, HBM, VMEM],
        out_specs=[VMEM] * len(sums + rows),
        out_shape=sums + rows,
        scratch_shapes=[
            pltpu.VMEM((NQ, 4, 32, TILE_A), BF),
            pltpu.VMEM((TOKENS, TILE_A), BF),
            pltpu.VMEM((TOKENS, TILE_A), BF),
            pltpu.VMEM((count, TILE_A, TOKENS), BF),
            pltpu.VMEM((count, TILE_A, TOKENS), BF),
            pltpu.VMEM((count, width, TILE_A), jnp.float32),
            pltpu.VMEM((GROUPS * TILE_A, width), BF),
            pltpu.VMEM((GROUPS * TILE_A, width), BF),
            pltpu.VMEM((2, TILE_A, width), jnp.float32),
            pltpu.VMEM((GROUPS, 8, TOKENS), jnp.float32),
            pltpu.SemaphoreType.DMA((count,)),
        ],
        compiler_params=pltpu.CompilerParams(vmem_limit_bytes=42 * 1024 * 1024),
        cost_estimate=pl.CostEstimate(
            flops=count * 10**7 if base == 0 else count * 10**9, bytes_accessed=count * 10**6 // 2, transcendentals=0
        ),
    )(info, *arrays, grads, query_grads, codes, eigenvalues, before)


def unpack_kernel(tiles, kept_a, kept_b, kept_c, came, out):
    first = kept_a.shape[0]
    both = WAVES * NQ
    for place in range(2 * both):
        half, n = place // both, place % both
        if half:
            rows = came[n]
        elif n < first:
            rows = kept_a[n]
        else:
            rows = kept_b[n - first] if n < NQ else kept_c[n - NQ]
        tile = tiles[place]
        cols = pl.ds(pl.multiple_of((tile % 32) * TILE_A, TILE_A), TILE_A)
        out[tile // 32, :, cols] = rows


def after(value, *others):
    return lax.optimization_barrier((value, *others))[0]


def paired_body(
    train_inputs,
    train_outgrads,
    sequence_ids,
    query_inputs,
    query_outgrads,
    eigenvalues,
    input_basis,
    slot_list,
    output_basis,
):
    x = lax.axis_index("parts")
    me = lax.axis_index("query")
    train_other = lax.ppermute(train_inputs, "parts", SWAP)
    ids = jnp.arange(64, dtype=jnp.int32)
    tile_of = jnp.sum(jnp.where(slot_list[None, :] == ids[:, None], ids[None, :], 0), axis=1)
    by_half = tile_of.reshape(NQ, 2, WAVES).transpose(1, 2, 0).reshape(2, WAVES * NQ)
    mine = jnp.where(x == 0, by_half[0], by_half[1])
    theirs = jnp.where(x == 0, by_half[1], by_half[0])
    side = x.reshape(1).astype(jnp.int32)

    packed = pl.pallas_call(
        pack_kernel,
        in_specs=[SMEM, VMEM, VMEM, VMEM, VMEM],
        out_specs=[VMEM] * WAVES,
        out_shape=[jax.ShapeDtypeStruct((UNIT, 32, TILE_A), BF)] * WAVES,
    )(jnp.concatenate([side, mine]), train_inputs, train_other, query_inputs, input_basis)

    ids_other = lax.ppermute(sequence_ids, "parts", SWAP)
    out_other = lax.ppermute(after(train_outgrads, train_other), "parts", SWAP)
    id_pair = jnp.where(
        x == 0, jnp.stack([sequence_ids, ids_other]), jnp.stack([ids_other, sequence_ids])
    )
    id_pair = id_pair + SEQS * jnp.arange(2, dtype=jnp.int32)[:, None]
    codes = id_pair.reshape(2, NQ, 8).transpose(1, 0, 2).reshape(1, TOKENS)
    slab = train_outgrads.shape[2]
    grads, query_grads = pl.pallas_call(
        prepare_kernel,
        in_specs=[SMEM] + [VMEM] * 4,
        out_specs=[VMEM, VMEM],
        out_shape=[
            jax.ShapeDtypeStruct((LAYERS, TOKENS, slab), BF),
            jax.ShapeDtypeStruct((LAYERS, slab, TOKENS), BF),
        ],
    )(side, train_outgrads, out_other, query_outgrads, output_basis)

    units = [None] * NQ
    units[0] = packed[0]
    units[4] = hop(packed[0], 4)
    units[12] = hop(packed[0], 12)
    units[8] = hop(after(packed[0], units[4], units[12]), 8)
    for d in (0, 4, 12):
        units[d ^ 2] = hop(units[d], 2)
    units[10] = hop(after(units[8], grads, units[2], units[6], units[14]), 2)
    for d in (0, 2, 4, 6, 12, 14, 8, 10):
        units[d ^ 1] = hop(units[d], 1)
    places0 = [(d, None) for d in range(NQ)]

    info = jnp.concatenate([me.reshape(1).astype(jnp.int32), mine, side])
    zero = jnp.zeros((GROUPS, TOKENS), jnp.float32)
    common = (grads, query_grads, codes, eigenvalues)
    part0, kept_a, given_a = score_tiles(0, 8, False, info, units, places0, *common, zero)

    second = after(packed[1], units[8])
    along = [hop(second, d) for d in (4, 12, 8)]
    near = hop(second, 2)
    *along, near, _ = lax.optimization_barrier((*along, near, part0))
    line = jnp.stack(along)
    beside = hop(line, 2)
    part1, kept_b, given_b = score_tiles(8, 8, False, info, units, places0, *common, part0)
    beside = after(beside, part1)
    arrays = [second, near, line, beside]
    arrays = arrays + [hop(array, 1) for array in arrays]
    order = {4: 0, 12: 1, 8: 2}
    places1 = []
    for d in range(NQ):
        across_y = (d & 2) // 2 + 4 * (d & 1)
        far = d & 12
        places1.append((across_y + 2, order[far]) if far else (across_y, None))
    keep, give, kept1, given1 = score_tiles(
        16, 16, True, info, arrays, places1, *common, part1
    )

    total = keep + lax.ppermute(give, "parts", SWAP)
    came = lax.ppermute(jnp.concatenate([given_a, given_b, given1], axis=0), "parts", SWAP)
    total = after(total, came)
    rotated_out = pl.pallas_call(
        unpack_kernel,
        in_specs=[SMEM] + [VMEM] * 4,
        out_specs=VMEM,
        out_shape=jax.ShapeDtypeStruct(train_inputs.shape, BF),
    )(jnp.concatenate([mine, theirs]), kept_a, kept_b, kept1, came)
    for bits in (1, 2, 4):
        total = total + hop(total, bits)
    total = after(total, rotated_out)
    total = total + hop(total, 8)
    scores = jnp.sum(total.reshape(SEQS, QUERIES, QLEN), axis=2).T
    return (scores, rotated_out)


def solution(mesh):
    paired = mesh.shape["parts"] == 2 and mesh.shape["query"] == NQ
    return jax.shard_map(
        paired_body if paired else general_body,
        mesh=mesh,
        in_specs=(
            P(None, ("parts", "query"), None),
            P(None, "parts", "query"),
            P("parts"),
            P(None, "query", None),
            P(None, None, "query"),
            P(None, "query", None),
            P("query", None, None),
            P(),
            P(None, "query", None, None),
        ),
        out_specs=(P(None, "parts"), P(None, ("parts", "query"), None)),
        check_vma=False,
    )
```

```python
import jax
import jax.numpy as jnp
from jax import lax
from jax.experimental import pallas as pl
from jax.experimental.pallas import tpu as pltpu
from jax.sharding import PartitionSpec as P

D = 4096
LAYERS = 2
TILE_A = 128
TILE_S = 64
SEQS = 4
QUERIES = 16
QLEN = 16


damping = 0.05


def rotate_blocks(rows, block_tiles, width):
    layer_count, row_count, feature_count = rows.shape
    blocks = rows.reshape(layer_count, row_count, feature_count // width, width)
    shaped = block_tiles.reshape(layer_count, feature_count // width, width, width)
    turned = jnp.einsum("lrbi,lbij->lrbj", blocks, shaped, preferred_element_type=jnp.float32)
    return turned.reshape(layer_count, row_count, feature_count).astype(jnp.bfloat16)


def general_body(
    train_inputs,
    train_outgrads,
    sequence_ids,
    query_inputs,
    query_outgrads,
    eigenvalues,
    input_basis,
    slot_list,
    output_basis,
):
    every_slot = lax.all_gather(input_basis, "query", axis=0, tiled=True)
    basis_tiles = jnp.take(every_slot, slot_list, axis=0)
    rotated_out = rotate_blocks(train_inputs, basis_tiles, TILE_A)
    own_query = rotate_blocks(query_inputs, basis_tiles, TILE_A)
    rotated_train, rotated_query = (
        lax.all_gather(rotated_out, "query", axis=1, tiled=True),
        lax.all_gather(own_query, "query", axis=1, tiled=True),
    )
    grads_rot = rotate_blocks(train_outgrads, output_basis, TILE_S)
    query_rot = rotate_blocks(query_outgrads, output_basis, TILE_S)
    token_count = grads_rot.shape[1]
    slab_width = grads_rot.shape[2]
    weights = 1.0 / (eigenvalues + damping)
    onehot = (sequence_ids[:, None] == jnp.arange(SEQS, dtype=jnp.int32)[None, :]).astype(
        jnp.bfloat16
    )
    totals = jnp.zeros((SEQS, QUERIES * QLEN), jnp.float32)
    for layer_index in range(LAYERS):
        masked = (onehot[:, :, None] * grads_rot[layer_index][:, None, :]).reshape(
            token_count, SEQS * slab_width
        )
        gram_block = lax.dot_general(
            masked,
            rotated_train[layer_index],
            (((0,), (0,)), ((), ())),
            preferred_element_type=jnp.float32,
        )
        scaled = (gram_block.reshape(SEQS, slab_width, D) * weights[layer_index][None]).astype(
            jnp.bfloat16
        )
        projected = jnp.einsum(
            "sij,uj->siu", scaled, rotated_query[layer_index], preferred_element_type=jnp.float32
        )
        totals = totals + jnp.einsum(
            "siu,ui->su", projected, query_rot[layer_index].astype(jnp.float32)
        )
    partial_value = jnp.sum(totals.reshape(SEQS, QUERIES, QLEN), axis=2).T
    scores = lax.psum(partial_value, "query")
    return (scores, rotated_out)


NQ = 16
WAVES = 2
GROUPS = 2 * SEQS
TOKENS = 256
UNIT = 20
SWAP = [(0, 1), (1, 0)]
BF = jnp.bfloat16


def hop(value, bits):
    return lax.ppermute(value, "query", [(i, i ^ bits) for i in range(NQ)])


def pack_kernel(info, own, other, query, basis, *units):
    x = info[1 + WAVES * NQ]

    for wave in range(WAVES):
        unit = units[wave]

        for owner in range(NQ):
            tile = info[1 + wave * NQ + owner]
            layer = tile // 32
            cols = pl.ds(pl.multiple_of((tile % 32) * TILE_A, TILE_A), TILE_A)
            mine = own[layer, :, cols].astype(jnp.float32)
            came = other[layer, :, cols].astype(jnp.float32)
            first = jnp.where(x == 0, mine, came)
            second = jnp.where(x == 0, came, mine)
            unit[owner, :16, :] = jnp.concatenate([first, second], axis=0).astype(BF)
            unit[owner, 16:, :] = query[layer, :, cols]

        unit[NQ:] = basis[2 * x + wave].reshape(4, 32, TILE_A)


def prepare_kernel(info, own, other, query, tiles, grads, query_grads):
    x = info[1 + WAVES * NQ]
    blank = jnp.zeros((TILE_S, TILE_S), jnp.float32)
    for layer in range(LAYERS):
        for c in range(tiles.shape[1] // 2):
            cols = slice(c * TILE_A, (c + 1) * TILE_A)
            upper = jnp.concatenate([tiles[layer, 2 * c].astype(jnp.float32), blank], axis=1)
            lower = jnp.concatenate([blank, tiles[layer, 2 * c + 1].astype(jnp.float32)], axis=1)
            block = jnp.concatenate([upper, lower], axis=0)
            tile = block.astype(BF)
            mine = jnp.dot(own[layer, :, cols], tile, preferred_element_type=jnp.float32)
            came = jnp.dot(other[layer, :, cols], tile, preferred_element_type=jnp.float32)
            first = jnp.where(x == 0, mine, came).reshape(NQ, 1, 8, TILE_A)
            second = jnp.where(x == 0, came, mine).reshape(NQ, 1, 8, TILE_A)
            rows = jnp.concatenate([first, second], axis=1).reshape(TOKENS, TILE_A)
            grads[layer, :, cols] = rows.astype(BF)
            query_grads[layer, cols, :] = across(block.T.astype(BF), query[layer, :, cols]).astype(BF)


def across(left, right):
    return lax.dot_general(
        left, right, (((1,), (1,)), ((), ())), preferred_element_type=jnp.float32
    )


def score_kernel(base, count, last, info, *refs):
    units = refs[:NQ]
    grads, query_grads, codes, eigen, before = refs[NQ : NQ + 5]
    outs = refs[NQ + 5 : NQ + (9 if last else 8)]
    rows_kept, rows_given = outs[-2:]
    bases, train, query, train_t, query_t, eig, scaled0, scaled1, weights, acc, sems = refs[
        NQ + 5 + len(outs) :
    ]
    scaled = (scaled0, scaled1)
    me = info[0]
    x = info[1 + WAVES * NQ]
    start = base % NQ

    def piece(d, index):
        unit, which = units[d]
        return unit[index] if which is None else unit[which, index]

    def eig_copy(n):
        tile = info[1 + base + n]
        cols = pl.ds(pl.multiple_of((tile % 32) * TILE_A, TILE_A), TILE_A)
        return pltpu.make_async_copy(eigen.at[tile // 32, :, cols], eig.at[n], sems.at[n])

    for n in range(count):
        eig_copy(n).start()
    acc[...] = jnp.zeros_like(acc)
    for d in range(NQ):
        bases[me ^ d] = piece(d, slice(NQ, NQ + 4))

    def rotate(n):
        basis = bases[start + n].reshape(TILE_A, TILE_A)
        basis_t = basis.astype(jnp.float32).T.astype(BF)
        for d in range(NQ):
            rows = piece(d, start + n)
            place = pl.ds(pl.multiple_of((me ^ d) * 16, 16), 16)
            train[place, :] = rows[:16]
            query[place, :] = rows[16:]
        own = jnp.dot(piece(0, start + n)[:16], basis, preferred_element_type=jnp.float32)
        rows_kept[n] = jnp.where(x == 0, own[:8], own[8:]).astype(BF)
        rows_given[n] = jnp.where(x == 0, own[8:], own[:8]).astype(BF)
        train_t[n] = across(basis_t, train[...]).astype(BF)
        query_t[n] = across(basis_t, query[...]).astype(BF)

    def weigh(n, k):
        weights[k] = 1.0 / (eig[n].T + damping)

    def gram(n, k):
        layer = info[1 + base + n] // 32
        code = codes[...]
        rows = train_t[n]
        zero = jnp.zeros_like(rows)
        for h in range(2):
            left = jnp.concatenate(
                [jnp.where(code == s, rows, zero) for s in range(4 * h, 4 * h + 4)], axis=0
            )
            for c in range(3):
                cols = slice(c * 256, (c + 1) * 256)
                part = jnp.dot(left, grads[layer, :, cols], preferred_element_type=jnp.float32)
                part = part.reshape(4, TILE_A, 256) * weights[k, :, cols][None]
                scaled[k][h * 512 : (h + 1) * 512, cols] = part.astype(BF).reshape(512, 256)

    def project(n, k):
        layer = info[1 + base + n] // 32
        query = query_t[n].astype(jnp.float32)
        for h in range(2):
            part = jnp.dot(
                scaled[k][h * 512 : (h + 1) * 512, :],
                query_grads[layer],
                preferred_element_type=jnp.float32,
            )
            part = part.reshape(4, TILE_A, TOKENS) * query[None]
            acc[4 * h : 4 * h + 4] += jnp.sum(part.reshape(4, TILE_A // 8, 8, TOKENS), axis=1)

    rotate(0)
    rotate(1)
    eig_copy(0).wait()
    weigh(0, 0)
    eig_copy(1).wait()
    weigh(1, 1)
    gram(0, 0)

    @pl.loop(0, count - 2, step=2)
    def _(n):
        eig_copy(n + 2).wait()
        eig_copy(n + 3).wait()
        gram(n + 1, 1)
        rotate(n + 2)
        project(n, 0)
        weigh(n + 2, 0)
        gram(n + 2, 0)
        rotate(n + 3)
        project(n + 1, 1)
        weigh(n + 3, 1)

    gram(count - 1, 1)
    project(count - 2, 0)
    project(count - 1, 1)
    total = before[...] + jnp.sum(acc[...], axis=1)
    if last:
        outs[0][...] = jnp.where(x == 0, total[:SEQS], total[SEQS:])
        outs[1][...] = jnp.where(x == 0, total[SEQS:], total[:SEQS])
    else:
        outs[0][...] = total


VMEM = pl.BlockSpec(memory_space=pltpu.VMEM)
SMEM = pl.BlockSpec(memory_space=pltpu.SMEM)
HBM = pl.BlockSpec(memory_space=pltpu.HBM)


def score_tiles(base, count, last, info, arrays, places, grads, query_grads, codes, eigenvalues, before):
    width = grads.shape[2]

    def kernel(info_ref, *refs):
        held = refs[: len(arrays)]
        units = [(held[a], which) for a, which in places]
        score_kernel(base, count, last, info_ref, *units, *refs[len(arrays) :])

    sums = (
        [jax.ShapeDtypeStruct((SEQS, TOKENS), jnp.float32)] * 2
        if last
        else [jax.ShapeDtypeStruct((GROUPS, TOKENS), jnp.float32)]
    )
    rows = [jax.ShapeDtypeStruct((count, 8, TILE_A), BF)] * 2
    return pl.pallas_call(
        kernel,
        in_specs=[SMEM] + [VMEM] * len(arrays) + [VMEM, VMEM, VMEM, HBM, VMEM],
        out_specs=[VMEM] * len(sums + rows),
        out_shape=sums + rows,
        scratch_shapes=[
            pltpu.VMEM((NQ, 4, 32, TILE_A), BF),
            pltpu.VMEM((TOKENS, TILE_A), BF),
            pltpu.VMEM((TOKENS, TILE_A), BF),
            pltpu.VMEM((count, TILE_A, TOKENS), BF),
            pltpu.VMEM((count, TILE_A, TOKENS), BF),
            pltpu.VMEM((count, width, TILE_A), jnp.float32),
            pltpu.VMEM((GROUPS * TILE_A, width), BF),
            pltpu.VMEM((GROUPS * TILE_A, width), BF),
            pltpu.VMEM((2, TILE_A, width), jnp.float32),
            pltpu.VMEM((GROUPS, 8, TOKENS), jnp.float32),
            pltpu.SemaphoreType.DMA((count,)),
        ],
        compiler_params=pltpu.CompilerParams(vmem_limit_bytes=42 * 1024 * 1024),
        cost_estimate=pl.CostEstimate(
            flops=count * 10**7 if base == 0 else count * 10**9, bytes_accessed=count * 10**6 // 2, transcendentals=0
        ),
    )(info, *arrays, grads, query_grads, codes, eigenvalues, before)


def unpack_kernel(info, kept_a, kept_b, kept_c, came, out):
    first = kept_a.shape[0]
    both = WAVES * NQ
    for place in range(2 * both):
        half, n = place // both, place % both
        if half:
            rows = came[n]
        elif n < first:
            rows = kept_a[n]
        else:
            rows = kept_b[n - first] if n < NQ else kept_c[n - NQ]
        tile = info[1 + n + (both + 1 if half else 0)]
        cols = pl.ds(pl.multiple_of((tile % 32) * TILE_A, TILE_A), TILE_A)
        out[tile // 32, :, cols] = rows


def after(value, *others):
    return lax.optimization_barrier((value, *others))[0]


def paired_body(
    train_inputs,
    train_outgrads,
    sequence_ids,
    query_inputs,
    query_outgrads,
    eigenvalues,
    input_basis,
    slot_list,
    output_basis,
):
    x = lax.axis_index("parts")
    me = lax.axis_index("query")
    train_other = lax.ppermute(train_inputs, "parts", SWAP)
    ids = jnp.arange(64, dtype=jnp.int32)
    tile_of = jnp.sum(jnp.where(slot_list[None, :] == ids[:, None], ids[None, :], 0), axis=1)
    by_half = tile_of.reshape(NQ, 2, WAVES).transpose(1, 2, 0).reshape(2, WAVES * NQ)
    mine = jnp.where(x == 0, by_half[0], by_half[1])
    theirs = jnp.where(x == 0, by_half[1], by_half[0])
    ids_other = lax.ppermute(after(sequence_ids, mine), "parts", SWAP)
    side = x.reshape(1).astype(jnp.int32)
    info = jnp.concatenate([me.reshape(1).astype(jnp.int32), mine, side, theirs])

    packed = pl.pallas_call(
        pack_kernel,
        in_specs=[SMEM, VMEM, VMEM, VMEM, VMEM],
        out_specs=[VMEM] * WAVES,
        out_shape=[jax.ShapeDtypeStruct((UNIT, 32, TILE_A), BF)] * WAVES,
    )(after(info, ids_other), train_inputs, train_other, query_inputs, input_basis)

    out_other = lax.ppermute(after(train_outgrads, train_other), "parts", SWAP)
    id_pair = jnp.where(
        x == 0, jnp.stack([sequence_ids, ids_other]), jnp.stack([ids_other, sequence_ids])
    )
    id_pair = id_pair + SEQS * jnp.arange(2, dtype=jnp.int32)[:, None]
    codes = id_pair.reshape(2, NQ, 8).transpose(1, 0, 2).reshape(1, TOKENS)
    slab = train_outgrads.shape[2]
    grads, query_grads = pl.pallas_call(
        prepare_kernel,
        in_specs=[SMEM] + [VMEM] * 4,
        out_specs=[VMEM, VMEM],
        out_shape=[
            jax.ShapeDtypeStruct((LAYERS, TOKENS, slab), BF),
            jax.ShapeDtypeStruct((LAYERS, slab, TOKENS), BF),
        ],
    )(info, train_outgrads, out_other, query_outgrads, output_basis)

    units = [None] * NQ
    units[0] = packed[0]
    units[4] = hop(packed[0], 4)
    units[12] = hop(packed[0], 12)
    units[8] = hop(after(packed[0], units[4], units[12]), 8)
    units[2] = hop(units[0], 2)
    units[6] = hop(units[4], 2)
    units[14] = hop(after(units[12], grads), 2)
    units[10] = hop(after(units[8], units[2], units[6]), 2)
    for d in (0, 2, 4, 6, 12, 14, 8, 10):
        units[d ^ 1] = hop(units[d], 1)
    places0 = [(d, None) for d in range(NQ)]

    zero = jnp.zeros((GROUPS, TOKENS), jnp.float32)
    common = (grads, query_grads, codes, eigenvalues)
    part0, kept_a, given_a = score_tiles(0, 8, False, info, units, places0, *common, zero)

    second = after(packed[1], units[8])
    along = [hop(second, d) for d in (4, 12, 8)]
    near = hop(second, 2)
    *along, near, _ = lax.optimization_barrier((*along, near, part0))
    line = jnp.stack(along)
    beside = hop(line, 2)
    part1, kept_b, given_b = score_tiles(8, 8, False, info, units, places0, *common, part0)
    beside = after(beside, part1)
    arrays = [second, near, line, beside]
    arrays = arrays + [hop(array, 1) for array in arrays]
    order = {4: 0, 12: 1, 8: 2}
    places1 = []
    for d in range(NQ):
        across_y = (d & 2) // 2 + 4 * (d & 1)
        far = d & 12
        places1.append((across_y + 2, order[far]) if far else (across_y, None))
    keep, give, kept1, given1 = score_tiles(
        16, 16, True, info, arrays, places1, *common, part1
    )

    total = keep + lax.ppermute(give, "parts", SWAP)
    came = lax.ppermute(jnp.concatenate([given_a, given_b, given1], axis=0), "parts", SWAP)
    total = after(total, came)
    rotated_out = pl.pallas_call(
        unpack_kernel,
        in_specs=[SMEM] + [VMEM] * 4,
        out_specs=VMEM,
        out_shape=jax.ShapeDtypeStruct(train_inputs.shape, BF),
    )(info, kept_a, kept_b, kept1, came)
    for bits in (1, 2, 4):
        total = total + hop(total, bits)
    total = after(total, rotated_out)
    total = total + hop(total, 8)
    scores = jnp.sum(total.reshape(SEQS, QUERIES, QLEN), axis=2).T
    return (scores, rotated_out)


def solution(mesh):
    paired = mesh.shape["parts"] == 2 and mesh.shape["query"] == NQ
    return jax.shard_map(
        paired_body if paired else general_body,
        mesh=mesh,
        in_specs=(
            P(None, ("parts", "query"), None),
            P(None, "parts", "query"),
            P("parts"),
            P(None, "query", None),
            P(None, None, "query"),
            P(None, "query", None),
            P("query", None, None),
            P(),
            P(None, "query", None, None),
        ),
        out_specs=(P(None, "parts"), P(None, ("parts", "query"), None)),
        check_vma=False,
    )
```

```python
import jax
import jax.numpy as jnp
from jax import lax
from jax.experimental import pallas as pl
from jax.experimental.pallas import tpu as pltpu
from jax.sharding import PartitionSpec as P

D = 4096
LAYERS = 2
TILE_A = 128
TILE_S = 64
SEQS = 4
QUERIES = 16
QLEN = 16


damping = 0.05


def rotate_blocks(rows, block_tiles, width):
    layer_count, row_count, feature_count = rows.shape
    blocks = rows.reshape(layer_count, row_count, feature_count // width, width)
    shaped = block_tiles.reshape(layer_count, feature_count // width, width, width)
    turned = jnp.einsum("lrbi,lbij->lrbj", blocks, shaped, preferred_element_type=jnp.float32)
    return turned.reshape(layer_count, row_count, feature_count).astype(jnp.bfloat16)


def general_body(
    train_inputs,
    train_outgrads,
    sequence_ids,
    query_inputs,
    query_outgrads,
    eigenvalues,
    input_basis,
    slot_list,
    output_basis,
):
    every_slot = lax.all_gather(input_basis, "query", axis=0, tiled=True)
    basis_tiles = jnp.take(every_slot, slot_list, axis=0)
    rotated_out = rotate_blocks(train_inputs, basis_tiles, TILE_A)
    own_query = rotate_blocks(query_inputs, basis_tiles, TILE_A)
    rotated_train, rotated_query = (
        lax.all_gather(rotated_out, "query", axis=1, tiled=True),
        lax.all_gather(own_query, "query", axis=1, tiled=True),
    )
    grads_rot = rotate_blocks(train_outgrads, output_basis, TILE_S)
    query_rot = rotate_blocks(query_outgrads, output_basis, TILE_S)
    token_count = grads_rot.shape[1]
    slab_width = grads_rot.shape[2]
    weights = 1.0 / (eigenvalues + damping)
    onehot = (sequence_ids[:, None] == jnp.arange(SEQS, dtype=jnp.int32)[None, :]).astype(
        jnp.bfloat16
    )
    totals = jnp.zeros((SEQS, QUERIES * QLEN), jnp.float32)
    for layer_index in range(LAYERS):
        masked = (onehot[:, :, None] * grads_rot[layer_index][:, None, :]).reshape(
            token_count, SEQS * slab_width
        )
        gram_block = lax.dot_general(
            masked,
            rotated_train[layer_index],
            (((0,), (0,)), ((), ())),
            preferred_element_type=jnp.float32,
        )
        scaled = (gram_block.reshape(SEQS, slab_width, D) * weights[layer_index][None]).astype(
            jnp.bfloat16
        )
        projected = jnp.einsum(
            "sij,uj->siu", scaled, rotated_query[layer_index], preferred_element_type=jnp.float32
        )
        totals = totals + jnp.einsum(
            "siu,ui->su", projected, query_rot[layer_index].astype(jnp.float32)
        )
    partial_value = jnp.sum(totals.reshape(SEQS, QUERIES, QLEN), axis=2).T
    scores = lax.psum(partial_value, "query")
    return (scores, rotated_out)


NQ = 16
WAVES = 2
GROUPS = 2 * SEQS
TOKENS = 256
UNIT = 20
SWAP = [(0, 1), (1, 0)]
BF = jnp.bfloat16


def hop(value, bits):
    return lax.ppermute(value, "query", [(i, i ^ bits) for i in range(NQ)])


def pack_kernel(info, own, other, query, basis, *units):
    x = info[1 + WAVES * NQ]

    for wave in range(WAVES):
        unit = units[wave]

        for owner in range(NQ):
            tile = info[1 + wave * NQ + owner]
            layer = tile // 32
            cols = pl.ds(pl.multiple_of((tile % 32) * TILE_A, TILE_A), TILE_A)
            mine = own[layer, :, cols].astype(jnp.float32)
            came = other[layer, :, cols].astype(jnp.float32)
            first = jnp.where(x == 0, mine, came)
            second = jnp.where(x == 0, came, mine)
            unit[owner, :16, :] = jnp.concatenate([first, second], axis=0).astype(BF)
            unit[owner, 16:, :] = query[layer, :, cols]

        unit[NQ:] = basis[2 * x + wave].reshape(4, 32, TILE_A)


def prepare_kernel(info, own, other, query, tiles, grads, query_grads):
    x = info[1 + WAVES * NQ]
    blank = jnp.zeros((TILE_S, TILE_S), jnp.float32)
    for layer in range(LAYERS):
        for c in range(tiles.shape[1] // 2):
            cols = slice(c * TILE_A, (c + 1) * TILE_A)
            upper = jnp.concatenate([tiles[layer, 2 * c].astype(jnp.float32), blank], axis=1)
            lower = jnp.concatenate([blank, tiles[layer, 2 * c + 1].astype(jnp.float32)], axis=1)
            block = jnp.concatenate([upper, lower], axis=0)
            tile = block.astype(BF)
            mine = jnp.dot(own[layer, :, cols], tile, preferred_element_type=jnp.float32)
            came = jnp.dot(other[layer, :, cols], tile, preferred_element_type=jnp.float32)
            first = jnp.where(x == 0, mine, came).reshape(NQ, 1, 8, TILE_A)
            second = jnp.where(x == 0, came, mine).reshape(NQ, 1, 8, TILE_A)
            rows = jnp.concatenate([first, second], axis=1).reshape(TOKENS, TILE_A)
            grads[layer, :, cols] = rows.astype(BF)
            query_grads[layer, cols, :] = across(block.T.astype(BF), query[layer, :, cols]).astype(BF)


def across(left, right):
    return lax.dot_general(
        left, right, (((1,), (1,)), ((), ())), preferred_element_type=jnp.float32
    )


def score_kernel(base, count, last, info, *refs):
    units = refs[:NQ]
    grads, query_grads, codes, eigen, before = refs[NQ : NQ + 5]
    outs = refs[NQ + 5 : NQ + (9 if last else 8)]
    rows_kept, rows_given = outs[-2:]
    bases, train, query, train_t, query_t, eig, scaled0, scaled1, weights, acc, sems = refs[
        NQ + 5 + len(outs) :
    ]
    scaled = (scaled0, scaled1)
    me = info[0]
    x = info[1 + WAVES * NQ]
    start = base % NQ

    def piece(d, index):
        unit, which = units[d]
        return unit[index] if which is None else unit[which, index]

    def eig_copy(n):
        tile = info[1 + base + n]
        cols = pl.ds(pl.multiple_of((tile % 32) * TILE_A, TILE_A), TILE_A)
        return pltpu.make_async_copy(eigen.at[tile // 32, :, cols], eig.at[n], sems.at[n])

    for n in range(count):
        eig_copy(n).start()
    acc[...] = jnp.zeros_like(acc)
    for d in range(NQ):
        bases[me ^ d] = piece(d, slice(NQ, NQ + 4))

    def rotate(n):
        basis = bases[start + n].reshape(TILE_A, TILE_A)
        basis_t = basis.astype(jnp.float32).T.astype(BF)
        for d in range(NQ):
            rows = piece(d, start + n)
            place = pl.ds(pl.multiple_of((me ^ d) * 16, 16), 16)
            train[place, :] = rows[:16]
            query[place, :] = rows[16:]
        own = jnp.dot(piece(0, start + n)[:16], basis, preferred_element_type=jnp.float32)
        rows_kept[n] = jnp.where(x == 0, own[:8], own[8:]).astype(BF)
        rows_given[n] = jnp.where(x == 0, own[8:], own[:8]).astype(BF)
        train_t[n] = across(basis_t, train[...]).astype(BF)
        query_t[n] = across(basis_t, query[...]).astype(BF)

    def weigh(n, k):
        weights[k] = 1.0 / (eig[n].T + damping)

    def gram(n, k):
        layer = info[1 + base + n] // 32
        code = codes[...]
        rows = train_t[n]
        zero = jnp.zeros_like(rows)
        for h in range(2):
            left = jnp.concatenate(
                [jnp.where(code == s, rows, zero) for s in range(4 * h, 4 * h + 4)], axis=0
            )
            for c in range(3):
                cols = slice(c * 256, (c + 1) * 256)
                part = jnp.dot(left, grads[layer, :, cols], preferred_element_type=jnp.float32)
                part = part.reshape(4, TILE_A, 256) * weights[k, :, cols][None]
                scaled[k][h * 512 : (h + 1) * 512, cols] = part.astype(BF).reshape(512, 256)

    def project(n, k):
        layer = info[1 + base + n] // 32
        query = query_t[n].astype(jnp.float32)
        for h in range(2):
            part = jnp.dot(
                scaled[k][h * 512 : (h + 1) * 512, :],
                query_grads[layer],
                preferred_element_type=jnp.float32,
            )
            part = part.reshape(4, TILE_A, TOKENS) * query[None]
            acc[4 * h : 4 * h + 4] += jnp.sum(part.reshape(4, TILE_A // 8, 8, TOKENS), axis=1)

    rotate(0)
    rotate(1)
    eig_copy(0).wait()
    weigh(0, 0)
    eig_copy(1).wait()
    weigh(1, 1)
    gram(0, 0)

    @pl.loop(0, count - 2, step=2)
    def _(n):
        eig_copy(n + 2).wait()
        eig_copy(n + 3).wait()
        gram(n + 1, 1)
        rotate(n + 2)
        project(n, 0)
        weigh(n + 2, 0)
        gram(n + 2, 0)
        rotate(n + 3)
        project(n + 1, 1)
        weigh(n + 3, 1)

    gram(count - 1, 1)
    project(count - 2, 0)
    project(count - 1, 1)
    total = before[...] + jnp.sum(acc[...], axis=1)
    if last:
        outs[0][...] = jnp.where(x == 0, total[:SEQS], total[SEQS:])
        outs[1][...] = jnp.where(x == 0, total[SEQS:], total[:SEQS])
    else:
        outs[0][...] = total


VMEM = pl.BlockSpec(memory_space=pltpu.VMEM)
SMEM = pl.BlockSpec(memory_space=pltpu.SMEM)
HBM = pl.BlockSpec(memory_space=pltpu.HBM)


def score_tiles(base, count, last, info, arrays, places, grads, query_grads, codes, eigenvalues, before):
    width = grads.shape[2]

    def kernel(info_ref, *refs):
        held = refs[: len(arrays)]
        units = [(held[a], which) for a, which in places]
        score_kernel(base, count, last, info_ref, *units, *refs[len(arrays) :])

    sums = (
        [jax.ShapeDtypeStruct((SEQS, TOKENS), jnp.float32)] * 2
        if last
        else [jax.ShapeDtypeStruct((GROUPS, TOKENS), jnp.float32)]
    )
    rows = [jax.ShapeDtypeStruct((count, 8, TILE_A), BF)] * 2
    return pl.pallas_call(
        kernel,
        in_specs=[SMEM] + [VMEM] * len(arrays) + [VMEM, VMEM, VMEM, HBM, VMEM],
        out_specs=[VMEM] * len(sums + rows),
        out_shape=sums + rows,
        scratch_shapes=[
            pltpu.VMEM((NQ, 4, 32, TILE_A), BF),
            pltpu.VMEM((TOKENS, TILE_A), BF),
            pltpu.VMEM((TOKENS, TILE_A), BF),
            pltpu.VMEM((count, TILE_A, TOKENS), BF),
            pltpu.VMEM((count, TILE_A, TOKENS), BF),
            pltpu.VMEM((count, width, TILE_A), jnp.float32),
            pltpu.VMEM((GROUPS * TILE_A, width), BF),
            pltpu.VMEM((GROUPS * TILE_A, width), BF),
            pltpu.VMEM((2, TILE_A, width), jnp.float32),
            pltpu.VMEM((GROUPS, 8, TOKENS), jnp.float32),
            pltpu.SemaphoreType.DMA((count,)),
        ],
        compiler_params=pltpu.CompilerParams(vmem_limit_bytes=42 * 1024 * 1024),
        cost_estimate=pl.CostEstimate(
            flops=count * 10**7 if base == 0 else count * 10**9, bytes_accessed=count * 10**6 // 2, transcendentals=0
        ),
    )(info, *arrays, grads, query_grads, codes, eigenvalues, before)


def unpack_kernel(info, kept_a, kept_b, kept_c, came, out):
    first = kept_a.shape[0]
    both = WAVES * NQ
    for place in range(2 * both):
        half, n = place // both, place % both
        if half:
            rows = came[n]
        elif n < first:
            rows = kept_a[n]
        else:
            rows = kept_b[n - first] if n < NQ else kept_c[n - NQ]
        tile = info[1 + n + (both + 1 if half else 0)]
        cols = pl.ds(pl.multiple_of((tile % 32) * TILE_A, TILE_A), TILE_A)
        out[tile // 32, :, cols] = rows


def after(value, *others):
    return lax.optimization_barrier((value, *others))[0]


def paired_body(
    train_inputs,
    train_outgrads,
    sequence_ids,
    query_inputs,
    query_outgrads,
    eigenvalues,
    input_basis,
    slot_list,
    output_basis,
):
    x = lax.axis_index("parts")
    me = lax.axis_index("query")
    train_other = lax.ppermute(train_inputs, "parts", SWAP)
    ids = jnp.arange(64, dtype=jnp.int32)
    tile_of = jnp.sum(jnp.where(slot_list[None, :] == ids[:, None], ids[None, :], 0), axis=1)
    by_half = tile_of.reshape(NQ, 2, WAVES).transpose(1, 2, 0).reshape(2, WAVES * NQ)
    mine = jnp.where(x == 0, by_half[0], by_half[1])
    theirs = jnp.where(x == 0, by_half[1], by_half[0])
    ids_other = lax.ppermute(after(sequence_ids, mine), "parts", SWAP)
    side = x.reshape(1).astype(jnp.int32)
    info = jnp.concatenate([me.reshape(1).astype(jnp.int32), mine, side, theirs])

    packed = pl.pallas_call(
        pack_kernel,
        in_specs=[SMEM, VMEM, VMEM, VMEM, VMEM],
        out_specs=[VMEM] * WAVES,
        out_shape=[jax.ShapeDtypeStruct((UNIT, 32, TILE_A), BF)] * WAVES,
    )(after(info, ids_other), train_inputs, train_other, query_inputs, input_basis)

    out_other = lax.ppermute(after(train_outgrads, train_other), "parts", SWAP)
    id_pair = jnp.where(
        x == 0, jnp.stack([sequence_ids, ids_other]), jnp.stack([ids_other, sequence_ids])
    )
    id_pair = id_pair + SEQS * jnp.arange(2, dtype=jnp.int32)[:, None]
    codes = id_pair.reshape(2, NQ, 8).transpose(1, 0, 2).reshape(1, TOKENS)
    slab = train_outgrads.shape[2]
    grads, query_grads = pl.pallas_call(
        prepare_kernel,
        in_specs=[SMEM] + [VMEM] * 4,
        out_specs=[VMEM, VMEM],
        out_shape=[
            jax.ShapeDtypeStruct((LAYERS, TOKENS, slab), BF),
            jax.ShapeDtypeStruct((LAYERS, slab, TOKENS), BF),
        ],
    )(info, train_outgrads, out_other, query_outgrads, output_basis)

    units = [None] * NQ
    units[0] = packed[0]
    units[4] = hop(packed[0], 4)
    units[12] = hop(packed[0], 12)
    units[8] = hop(after(packed[0], units[4], units[12], grads), 8)
    units[2] = hop(units[0], 2)
    units[6] = hop(units[4], 2)
    units[14] = hop(units[12], 2)
    units[10] = hop(after(units[8], units[2], units[6], units[14]), 2)
    for d in (0, 2, 4, 6, 12, 14, 8, 10):
        units[d ^ 1] = hop(units[d], 1)
    places0 = [(d, None) for d in range(NQ)]

    zero = jnp.zeros((GROUPS, TOKENS), jnp.float32)
    common = (grads, query_grads, codes, eigenvalues)
    part0, kept_a, given_a = score_tiles(0, 8, False, info, units, places0, *common, zero)

    second = after(packed[1], units[8])
    along = [hop(second, d) for d in (4, 12, 8)]
    near = hop(second, 2)
    *along, near, _ = lax.optimization_barrier((*along, near, part0))
    line = jnp.stack(along)
    beside = hop(line, 2)
    part1, kept_b, given_b = score_tiles(8, 8, False, info, units, places0, *common, part0)
    beside = after(beside, part1)
    arrays = [second, near, line, beside]
    arrays = arrays + [hop(array, 1) for array in arrays]
    order = {4: 0, 12: 1, 8: 2}
    places1 = []
    for d in range(NQ):
        across_y = (d & 2) // 2 + 4 * (d & 1)
        far = d & 12
        places1.append((across_y + 2, order[far]) if far else (across_y, None))
    keep, give, kept1, given1 = score_tiles(
        16, 16, True, info, arrays, places1, *common, part1
    )

    total = keep + lax.ppermute(give, "parts", SWAP)
    came = lax.ppermute(jnp.concatenate([given_a, given_b, given1], axis=0), "parts", SWAP)
    total = after(total, came)
    rotated_out = pl.pallas_call(
        unpack_kernel,
        in_specs=[SMEM] + [VMEM] * 4,
        out_specs=VMEM,
        out_shape=jax.ShapeDtypeStruct(train_inputs.shape, BF),
    )(info, kept_a, kept_b, kept1, came)
    for bits in (1, 2, 4):
        total = total + hop(total, bits)
    total = after(total, rotated_out)
    total = total + hop(total, 8)
    scores = jnp.sum(total.reshape(SEQS, QUERIES, QLEN), axis=2).T
    return (scores, rotated_out)


def solution(mesh):
    paired = mesh.shape["parts"] == 2 and mesh.shape["query"] == NQ
    return jax.shard_map(
        paired_body if paired else general_body,
        mesh=mesh,
        in_specs=(
            P(None, ("parts", "query"), None),
            P(None, "parts", "query"),
            P("parts"),
            P(None, "query", None),
            P(None, None, "query"),
            P(None, "query", None),
            P("query", None, None),
            P(),
            P(None, "query", None, None),
        ),
        out_specs=(P(None, "parts"), P(None, ("parts", "query"), None)),
        check_vma=False,
    )
```

```python
import jax
import jax.numpy as jnp
from jax import lax
from jax.experimental import pallas as pl
from jax.experimental.pallas import tpu as pltpu
from jax.sharding import PartitionSpec as P

D = 4096
LAYERS = 2
TILE_A = 128
TILE_S = 64
SEQS = 4
QUERIES = 16
QLEN = 16


damping = 0.05


def rotate_blocks(rows, block_tiles, width):
    layer_count, row_count, feature_count = rows.shape
    blocks = rows.reshape(layer_count, row_count, feature_count // width, width)
    shaped = block_tiles.reshape(layer_count, feature_count // width, width, width)
    turned = jnp.einsum("lrbi,lbij->lrbj", blocks, shaped, preferred_element_type=jnp.float32)
    return turned.reshape(layer_count, row_count, feature_count).astype(jnp.bfloat16)


def general_body(
    train_inputs,
    train_outgrads,
    sequence_ids,
    query_inputs,
    query_outgrads,
    eigenvalues,
    input_basis,
    slot_list,
    output_basis,
):
    every_slot = lax.all_gather(input_basis, "query", axis=0, tiled=True)
    basis_tiles = jnp.take(every_slot, slot_list, axis=0)
    rotated_out = rotate_blocks(train_inputs, basis_tiles, TILE_A)
    own_query = rotate_blocks(query_inputs, basis_tiles, TILE_A)
    rotated_train, rotated_query = (
        lax.all_gather(rotated_out, "query", axis=1, tiled=True),
        lax.all_gather(own_query, "query", axis=1, tiled=True),
    )
    grads_rot = rotate_blocks(train_outgrads, output_basis, TILE_S)
    query_rot = rotate_blocks(query_outgrads, output_basis, TILE_S)
    token_count = grads_rot.shape[1]
    slab_width = grads_rot.shape[2]
    weights = 1.0 / (eigenvalues + damping)
    onehot = (sequence_ids[:, None] == jnp.arange(SEQS, dtype=jnp.int32)[None, :]).astype(
        jnp.bfloat16
    )
    totals = jnp.zeros((SEQS, QUERIES * QLEN), jnp.float32)
    for layer_index in range(LAYERS):
        masked = (onehot[:, :, None] * grads_rot[layer_index][:, None, :]).reshape(
            token_count, SEQS * slab_width
        )
        gram_block = lax.dot_general(
            masked,
            rotated_train[layer_index],
            (((0,), (0,)), ((), ())),
            preferred_element_type=jnp.float32,
        )
        scaled = (gram_block.reshape(SEQS, slab_width, D) * weights[layer_index][None]).astype(
            jnp.bfloat16
        )
        projected = jnp.einsum(
            "sij,uj->siu", scaled, rotated_query[layer_index], preferred_element_type=jnp.float32
        )
        totals = totals + jnp.einsum(
            "siu,ui->su", projected, query_rot[layer_index].astype(jnp.float32)
        )
    partial_value = jnp.sum(totals.reshape(SEQS, QUERIES, QLEN), axis=2).T
    scores = lax.psum(partial_value, "query")
    return (scores, rotated_out)


NQ = 16
WAVES = 2
GROUPS = 2 * SEQS
TOKENS = 256
UNIT = 20
SWAP = [(0, 1), (1, 0)]
BF = jnp.bfloat16


def hop(value, bits):
    return lax.ppermute(value, "query", [(i, i ^ bits) for i in range(NQ)])


def pack_kernel(info, own, other, query, basis, *units):
    x = info[1 + WAVES * NQ]

    for wave in range(WAVES):
        unit = units[wave]

        for owner in range(NQ):
            tile = info[1 + wave * NQ + owner]
            layer = tile // 32
            cols = pl.ds(pl.multiple_of((tile % 32) * TILE_A, TILE_A), TILE_A)
            mine = own[layer, :, cols].astype(jnp.float32)
            came = other[layer, :, cols].astype(jnp.float32)
            first = jnp.where(x == 0, mine, came)
            second = jnp.where(x == 0, came, mine)
            unit[owner, :16, :] = jnp.concatenate([first, second], axis=0).astype(BF)
            unit[owner, 16:, :] = query[layer, :, cols]

        unit[NQ:] = basis[2 * x + wave].reshape(4, 32, TILE_A)


def prepare_kernel(info, own, other, query, tiles, grads, query_grads):
    x = info[1 + WAVES * NQ]
    blank = jnp.zeros((TILE_S, TILE_S), jnp.float32)
    for layer in range(LAYERS):
        for c in range(tiles.shape[1] // 2):
            cols = slice(c * TILE_A, (c + 1) * TILE_A)
            upper = jnp.concatenate([tiles[layer, 2 * c].astype(jnp.float32), blank], axis=1)
            lower = jnp.concatenate([blank, tiles[layer, 2 * c + 1].astype(jnp.float32)], axis=1)
            block = jnp.concatenate([upper, lower], axis=0)
            tile = block.astype(BF)
            mine = jnp.dot(own[layer, :, cols], tile, preferred_element_type=jnp.float32)
            came = jnp.dot(other[layer, :, cols], tile, preferred_element_type=jnp.float32)
            first = jnp.where(x == 0, mine, came).reshape(NQ, 1, 8, TILE_A)
            second = jnp.where(x == 0, came, mine).reshape(NQ, 1, 8, TILE_A)
            rows = jnp.concatenate([first, second], axis=1).reshape(TOKENS, TILE_A)
            grads[layer, :, cols] = rows.astype(BF)
            query_grads[layer, cols, :] = across(block.T.astype(BF), query[layer, :, cols]).astype(BF)


def across(left, right):
    return lax.dot_general(
        left, right, (((1,), (1,)), ((), ())), preferred_element_type=jnp.float32
    )


def score_kernel(base, count, last, info, *refs):
    units = refs[:NQ]
    grads, query_grads, codes, eigen, before = refs[NQ : NQ + 5]
    outs = refs[NQ + 5 : NQ + (9 if last else 8)]
    rows_kept, rows_given = outs[-2:]
    bases, train, query, train_t, query_t, eig, scaled0, scaled1, weights, acc, sems = refs[
        NQ + 5 + len(outs) :
    ]
    scaled = (scaled0, scaled1)
    me = info[0]
    x = info[1 + WAVES * NQ]
    start = base % NQ

    def piece(d, index):
        unit, which = units[d]
        return unit[index] if which is None else unit[which, index]

    def eig_copy(n):
        tile = info[1 + base + n]
        cols = pl.ds(pl.multiple_of((tile % 32) * TILE_A, TILE_A), TILE_A)
        return pltpu.make_async_copy(eigen.at[tile // 32, :, cols], eig.at[n], sems.at[n])

    for n in range(count):
        eig_copy(n).start()
    acc[...] = jnp.zeros_like(acc)
    for d in range(NQ):
        bases[me ^ d] = piece(d, slice(NQ, NQ + 4))

    def rotate(n):
        basis = bases[start + n].reshape(TILE_A, TILE_A)
        basis_t = basis.astype(jnp.float32).T.astype(BF)
        for d in range(NQ):
            rows = piece(d, start + n)
            place = pl.ds(pl.multiple_of((me ^ d) * 16, 16), 16)
            train[place, :] = rows[:16]
            query[place, :] = rows[16:]
        own = jnp.dot(piece(0, start + n)[:16], basis, preferred_element_type=jnp.float32)
        rows_kept[n] = jnp.where(x == 0, own[:8], own[8:]).astype(BF)
        rows_given[n] = jnp.where(x == 0, own[8:], own[:8]).astype(BF)
        train_t[n] = across(basis_t, train[...]).astype(BF)
        query_t[n] = across(basis_t, query[...]).astype(BF)

    def weigh(n, k):
        weights[k] = 1.0 / (eig[n].T + damping)

    def gram(n, k):
        layer = info[1 + base + n] // 32
        code = codes[...]
        rows = train_t[n]
        zero = jnp.zeros_like(rows)
        for h in range(2):
            left = jnp.concatenate(
                [jnp.where(code == s, rows, zero) for s in range(4 * h, 4 * h + 4)], axis=0
            )
            for c in range(3):
                cols = slice(c * 256, (c + 1) * 256)
                part = jnp.dot(left, grads[layer, :, cols], preferred_element_type=jnp.float32)
                part = part.reshape(4, TILE_A, 256) * weights[k, :, cols][None]
                scaled[k][h * 512 : (h + 1) * 512, cols] = part.astype(BF).reshape(512, 256)

    def project(n, k):
        layer = info[1 + base + n] // 32
        query = query_t[n].astype(jnp.float32)
        for h in range(2):
            part = jnp.dot(
                scaled[k][h * 512 : (h + 1) * 512, :],
                query_grads[layer],
                preferred_element_type=jnp.float32,
            )
            part = part.reshape(4, TILE_A, TOKENS) * query[None]
            acc[4 * h : 4 * h + 4] += jnp.sum(part.reshape(4, TILE_A // 8, 8, TOKENS), axis=1)

    rotate(0)
    rotate(1)
    eig_copy(0).wait()
    weigh(0, 0)
    eig_copy(1).wait()
    weigh(1, 1)
    gram(0, 0)

    @pl.loop(0, count - 2, step=2)
    def _(n):
        eig_copy(n + 2).wait()
        eig_copy(n + 3).wait()
        gram(n + 1, 1)
        rotate(n + 2)
        project(n, 0)
        weigh(n + 2, 0)
        gram(n + 2, 0)
        rotate(n + 3)
        project(n + 1, 1)
        weigh(n + 3, 1)

    gram(count - 1, 1)
    project(count - 2, 0)
    project(count - 1, 1)
    total = before[...] + jnp.sum(acc[...], axis=1)
    if last:
        outs[0][...] = jnp.where(x == 0, total[:SEQS], total[SEQS:])
        outs[1][...] = jnp.where(x == 0, total[SEQS:], total[:SEQS])
    else:
        outs[0][...] = total


VMEM = pl.BlockSpec(memory_space=pltpu.VMEM)
SMEM = pl.BlockSpec(memory_space=pltpu.SMEM)
HBM = pl.BlockSpec(memory_space=pltpu.HBM)


def score_tiles(base, count, last, info, arrays, places, grads, query_grads, codes, eigenvalues, before):
    width = grads.shape[2]

    def kernel(info_ref, *refs):
        held = refs[: len(arrays)]
        units = [(held[a], which) for a, which in places]
        score_kernel(base, count, last, info_ref, *units, *refs[len(arrays) :])

    sums = (
        [jax.ShapeDtypeStruct((SEQS, TOKENS), jnp.float32)] * 2
        if last
        else [jax.ShapeDtypeStruct((GROUPS, TOKENS), jnp.float32)]
    )
    rows = [jax.ShapeDtypeStruct((count, 8, TILE_A), BF)] * 2
    return pl.pallas_call(
        kernel,
        in_specs=[SMEM] + [VMEM] * len(arrays) + [VMEM, VMEM, VMEM, HBM, VMEM],
        out_specs=[VMEM] * len(sums + rows),
        out_shape=sums + rows,
        scratch_shapes=[
            pltpu.VMEM((NQ, 4, 32, TILE_A), BF),
            pltpu.VMEM((TOKENS, TILE_A), BF),
            pltpu.VMEM((TOKENS, TILE_A), BF),
            pltpu.VMEM((count, TILE_A, TOKENS), BF),
            pltpu.VMEM((count, TILE_A, TOKENS), BF),
            pltpu.VMEM((count, width, TILE_A), jnp.float32),
            pltpu.VMEM((GROUPS * TILE_A, width), BF),
            pltpu.VMEM((GROUPS * TILE_A, width), BF),
            pltpu.VMEM((2, TILE_A, width), jnp.float32),
            pltpu.VMEM((GROUPS, 8, TOKENS), jnp.float32),
            pltpu.SemaphoreType.DMA((count,)),
        ],
        compiler_params=pltpu.CompilerParams(vmem_limit_bytes=42 * 1024 * 1024),
        cost_estimate=pl.CostEstimate(
            flops=count * 10**7 if base == 0 else count * 10**9, bytes_accessed=count * 10**6 // 2, transcendentals=0
        ),
    )(info, *arrays, grads, query_grads, codes, eigenvalues, before)


def unpack_kernel(info, kept_a, kept_b, kept_c, came, out):
    first = kept_a.shape[0]
    both = WAVES * NQ
    for place in range(2 * both):
        half, n = place // both, place % both
        if half:
            rows = came[n]
        elif n < first:
            rows = kept_a[n]
        else:
            rows = kept_b[n - first] if n < NQ else kept_c[n - NQ]
        tile = info[1 + n + (both + 1 if half else 0)]
        cols = pl.ds(pl.multiple_of((tile % 32) * TILE_A, TILE_A), TILE_A)
        out[tile // 32, :, cols] = rows


def after(value, *others):
    return lax.optimization_barrier((value, *others))[0]


def paired_body(
    train_inputs,
    train_outgrads,
    sequence_ids,
    query_inputs,
    query_outgrads,
    eigenvalues,
    input_basis,
    slot_list,
    output_basis,
):
    x = lax.axis_index("parts")
    me = lax.axis_index("query")
    train_other = lax.ppermute(train_inputs, "parts", SWAP)
    ids = jnp.arange(64, dtype=jnp.int32)
    tile_of = jnp.sum(jnp.where(slot_list[None, :] == ids[:, None], ids[None, :], 0), axis=1)
    by_half = tile_of.reshape(NQ, 2, WAVES).transpose(1, 2, 0).reshape(2, WAVES * NQ)
    mine = jnp.where(x == 0, by_half[0], by_half[1])
    theirs = jnp.where(x == 0, by_half[1], by_half[0])
    ids_other = lax.ppermute(after(sequence_ids, mine), "parts", SWAP)
    side = x.reshape(1).astype(jnp.int32)
    info = jnp.concatenate([me.reshape(1).astype(jnp.int32), mine, side, theirs])

    packed = pl.pallas_call(
        pack_kernel,
        in_specs=[SMEM, VMEM, VMEM, VMEM, VMEM],
        out_specs=[VMEM] * WAVES,
        out_shape=[jax.ShapeDtypeStruct((UNIT, 32, TILE_A), BF)] * WAVES,
        compiler_params=pltpu.CompilerParams(vmem_limit_bytes=8 * 1024 * 1024),
    )(after(info, ids_other), train_inputs, train_other, query_inputs, input_basis)

    out_other = lax.ppermute(after(train_outgrads, train_other), "parts", SWAP)
    id_pair = jnp.where(
        x == 0, jnp.stack([sequence_ids, ids_other]), jnp.stack([ids_other, sequence_ids])
    )
    id_pair = id_pair + SEQS * jnp.arange(2, dtype=jnp.int32)[:, None]
    codes = id_pair.reshape(2, NQ, 8).transpose(1, 0, 2).reshape(1, TOKENS)
    slab = train_outgrads.shape[2]
    grads, query_grads = pl.pallas_call(
        prepare_kernel,
        in_specs=[SMEM] + [VMEM] * 4,
        out_specs=[VMEM, VMEM],
        out_shape=[
            jax.ShapeDtypeStruct((LAYERS, TOKENS, slab), BF),
            jax.ShapeDtypeStruct((LAYERS, slab, TOKENS), BF),
        ],
        compiler_params=pltpu.CompilerParams(vmem_limit_bytes=16 * 1024 * 1024),
    )(info, train_outgrads, out_other, query_outgrads, output_basis)

    units = [None] * NQ
    units[0] = packed[0]
    units[4] = hop(packed[0], 4)
    units[12] = hop(packed[0], 12)
    units[8] = hop(after(packed[0], units[4], units[12], grads), 8)
    units[2] = hop(units[0], 2)
    units[6] = hop(units[4], 2)
    units[14] = hop(units[12], 2)
    units[10] = hop(after(units[8], units[2], units[6], units[14]), 2)
    for d in (0, 2, 4, 6, 12, 14, 8, 10):
        units[d ^ 1] = hop(units[d], 1)
    places0 = [(d, None) for d in range(NQ)]

    zero = jnp.zeros((GROUPS, TOKENS), jnp.float32)
    common = (grads, query_grads, codes, eigenvalues)
    part0, kept_a, given_a = score_tiles(0, 8, False, info, units, places0, *common, zero)

    second = after(packed[1], units[8])
    along = [hop(second, d) for d in (4, 12, 8)]
    near = hop(second, 2)
    *along, near, _ = lax.optimization_barrier((*along, near, part0))
    line = jnp.stack(along)
    beside = hop(line, 2)
    part1, kept_b, given_b = score_tiles(8, 8, False, info, units, places0, *common, part0)
    beside = after(beside, part1)
    arrays = [second, near, line, beside]
    arrays = arrays + [hop(array, 1) for array in arrays]
    order = {4: 0, 12: 1, 8: 2}
    places1 = []
    for d in range(NQ):
        across_y = (d & 2) // 2 + 4 * (d & 1)
        far = d & 12
        places1.append((across_y + 2, order[far]) if far else (across_y, None))
    keep, give, kept1, given1 = score_tiles(
        16, 16, True, info, arrays, places1, *common, part1
    )

    total = keep + lax.ppermute(give, "parts", SWAP)
    came = lax.ppermute(jnp.concatenate([given_a, given_b, given1], axis=0), "parts", SWAP)
    total = after(total, came)
    rotated_out = pl.pallas_call(
        unpack_kernel,
        in_specs=[SMEM] + [VMEM] * 4,
        out_specs=VMEM,
        out_shape=jax.ShapeDtypeStruct(train_inputs.shape, BF),
        compiler_params=pltpu.CompilerParams(vmem_limit_bytes=8 * 1024 * 1024),
    )(info, kept_a, kept_b, kept1, came)
    for bits in (1, 2, 4):
        total = total + hop(total, bits)
    total = after(total, rotated_out)
    total = total + hop(total, 8)
    scores = jnp.sum(total.reshape(SEQS, QUERIES, QLEN), axis=2).T
    return (scores, rotated_out)


def solution(mesh):
    paired = mesh.shape["parts"] == 2 and mesh.shape["query"] == NQ
    return jax.shard_map(
        paired_body if paired else general_body,
        mesh=mesh,
        in_specs=(
            P(None, ("parts", "query"), None),
            P(None, "parts", "query"),
            P("parts"),
            P(None, "query", None),
            P(None, None, "query"),
            P(None, "query", None),
            P("query", None, None),
            P(),
            P(None, "query", None, None),
        ),
        out_specs=(P(None, "parts"), P(None, ("parts", "query"), None)),
        check_vma=False,
    )
```

```python
import jax
import jax.numpy as jnp
from jax import lax
from jax.experimental import pallas as pl
from jax.experimental.pallas import tpu as pltpu
from jax.sharding import PartitionSpec as P

D = 4096
LAYERS = 2
TILE_A = 128
TILE_S = 64
SEQS = 4
QUERIES = 16
QLEN = 16


damping = 0.05


def rotate_blocks(rows, block_tiles, width):
    layer_count, row_count, feature_count = rows.shape
    blocks = rows.reshape(layer_count, row_count, feature_count // width, width)
    shaped = block_tiles.reshape(layer_count, feature_count // width, width, width)
    turned = jnp.einsum("lrbi,lbij->lrbj", blocks, shaped, preferred_element_type=jnp.float32)
    return turned.reshape(layer_count, row_count, feature_count).astype(jnp.bfloat16)


def general_body(
    train_inputs,
    train_outgrads,
    sequence_ids,
    query_inputs,
    query_outgrads,
    eigenvalues,
    input_basis,
    slot_list,
    output_basis,
):
    every_slot = lax.all_gather(input_basis, "query", axis=0, tiled=True)
    basis_tiles = jnp.take(every_slot, slot_list, axis=0)
    rotated_out = rotate_blocks(train_inputs, basis_tiles, TILE_A)
    own_query = rotate_blocks(query_inputs, basis_tiles, TILE_A)
    rotated_train, rotated_query = (
        lax.all_gather(rotated_out, "query", axis=1, tiled=True),
        lax.all_gather(own_query, "query", axis=1, tiled=True),
    )
    grads_rot = rotate_blocks(train_outgrads, output_basis, TILE_S)
    query_rot = rotate_blocks(query_outgrads, output_basis, TILE_S)
    token_count = grads_rot.shape[1]
    slab_width = grads_rot.shape[2]
    weights = 1.0 / (eigenvalues + damping)
    onehot = (sequence_ids[:, None] == jnp.arange(SEQS, dtype=jnp.int32)[None, :]).astype(
        jnp.bfloat16
    )
    totals = jnp.zeros((SEQS, QUERIES * QLEN), jnp.float32)
    for layer_index in range(LAYERS):
        masked = (onehot[:, :, None] * grads_rot[layer_index][:, None, :]).reshape(
            token_count, SEQS * slab_width
        )
        gram_block = lax.dot_general(
            masked,
            rotated_train[layer_index],
            (((0,), (0,)), ((), ())),
            preferred_element_type=jnp.float32,
        )
        scaled = (gram_block.reshape(SEQS, slab_width, D) * weights[layer_index][None]).astype(
            jnp.bfloat16
        )
        projected = jnp.einsum(
            "sij,uj->siu", scaled, rotated_query[layer_index], preferred_element_type=jnp.float32
        )
        totals = totals + jnp.einsum(
            "siu,ui->su", projected, query_rot[layer_index].astype(jnp.float32)
        )
    partial_value = jnp.sum(totals.reshape(SEQS, QUERIES, QLEN), axis=2).T
    scores = lax.psum(partial_value, "query")
    return (scores, rotated_out)


NQ = 16
WAVES = 2
GROUPS = 2 * SEQS
TOKENS = 256
UNIT = 20
SWAP = [(0, 1), (1, 0)]
BF = jnp.bfloat16


def hop(value, bits):
    return lax.ppermute(value, "query", [(i, i ^ bits) for i in range(NQ)])


def pack_kernel(info, own, other, query, basis, *units):
    x = info[1 + WAVES * NQ]

    for wave in range(WAVES):
        unit = units[wave]

        for owner in range(NQ):
            tile = info[1 + wave * NQ + owner]
            layer = tile // 32
            cols = pl.ds(pl.multiple_of((tile % 32) * TILE_A, TILE_A), TILE_A)
            mine = own[layer, :, cols].astype(jnp.float32)
            came = other[layer, :, cols].astype(jnp.float32)
            first = jnp.where(x == 0, mine, came)
            second = jnp.where(x == 0, came, mine)
            unit[owner, :16, :] = jnp.concatenate([first, second], axis=0).astype(BF)
            unit[owner, 16:, :] = query[layer, :, cols]

        unit[NQ:] = basis[2 * x + wave].reshape(4, 32, TILE_A)


def diagonal(tiles, layer, c):
    blank = jnp.zeros((TILE_S, TILE_S), jnp.float32)
    upper = jnp.concatenate([tiles[layer, 2 * c].astype(jnp.float32), blank], axis=1)
    lower = jnp.concatenate([blank, tiles[layer, 2 * c + 1].astype(jnp.float32)], axis=1)
    return jnp.concatenate([upper, lower], axis=0)


def query_kernel(query, tiles, query_grads):
    for layer in range(LAYERS):
        for c in range(tiles.shape[1] // 2):
            cols = slice(c * TILE_A, (c + 1) * TILE_A)
            block_t = diagonal(tiles, layer, c).T.astype(BF)
            query_grads[layer, cols, :] = across(block_t, query[layer, :, cols]).astype(BF)


def train_kernel(info, own, other, ids, ids_other, tiles, grads, codes):
    x = info[1 + WAVES * NQ]
    for layer in range(LAYERS):
        for c in range(tiles.shape[1] // 2):
            cols = slice(c * TILE_A, (c + 1) * TILE_A)
            tile = diagonal(tiles, layer, c).astype(BF)
            mine = jnp.dot(own[layer, :, cols], tile, preferred_element_type=jnp.float32)
            came = jnp.dot(other[layer, :, cols], tile, preferred_element_type=jnp.float32)
            first = jnp.where(x == 0, mine, came).reshape(NQ, 1, 8, TILE_A)
            second = jnp.where(x == 0, came, mine).reshape(NQ, 1, 8, TILE_A)
            rows = jnp.concatenate([first, second], axis=1).reshape(TOKENS, TILE_A)
            grads[layer, :, cols] = rows.astype(BF)
    half = TOKENS // 2
    row = lax.broadcasted_iota(jnp.int32, (half, TOKENS), 0)
    col = lax.broadcasted_iota(jnp.int32, (half, TOKENS), 1)
    hit = row == (col >> 4) * 8 + (col & 7)
    part = (col >> 3) & 1
    own_f, other_f = ids[...].astype(jnp.float32), ids_other[...].astype(jnp.float32)
    mine = jnp.where(hit & (part == x), 1.0, 0.0)
    came = jnp.where(hit & (part != x), 1.0, 0.0)
    placed = jnp.dot(
        jnp.broadcast_to(own_f, (8, half)), mine, preferred_element_type=jnp.float32
    ) + jnp.dot(jnp.broadcast_to(other_f, (8, half)), came, preferred_element_type=jnp.float32)
    codes[...] = (placed[:1] + 0.5).astype(jnp.int32) + SEQS * part[:1]


def across(left, right):
    return lax.dot_general(
        left, right, (((1,), (1,)), ((), ())), preferred_element_type=jnp.float32
    )


def score_kernel(base, count, last, info, *refs):
    units = refs[:NQ]
    grads, query_grads, codes, eigen, before = refs[NQ : NQ + 5]
    outs = refs[NQ + 5 : NQ + (9 if last else 8)]
    rows_kept, rows_given = outs[-2:]
    bases, train, query, train_t, query_t, eig, scaled0, scaled1, weights, acc, sems = refs[
        NQ + 5 + len(outs) :
    ]
    scaled = (scaled0, scaled1)
    me = info[0]
    x = info[1 + WAVES * NQ]
    start = base % NQ

    def piece(d, index):
        unit, which = units[d]
        return unit[index] if which is None else unit[which, index]

    def eig_copy(n):
        tile = info[1 + base + n]
        cols = pl.ds(pl.multiple_of((tile % 32) * TILE_A, TILE_A), TILE_A)
        return pltpu.make_async_copy(eigen.at[tile // 32, :, cols], eig.at[n], sems.at[n])

    for n in range(count):
        eig_copy(n).start()
    acc[...] = jnp.zeros_like(acc)
    for d in range(NQ):
        bases[me ^ d] = piece(d, slice(NQ, NQ + 4))

    def rotate(n):
        basis = bases[start + n].reshape(TILE_A, TILE_A)
        basis_t = basis.astype(jnp.float32).T.astype(BF)
        for d in range(NQ):
            rows = piece(d, start + n)
            place = pl.ds(pl.multiple_of((me ^ d) * 16, 16), 16)
            train[place, :] = rows[:16]
            query[place, :] = rows[16:]
        own = jnp.dot(piece(0, start + n)[:16], basis, preferred_element_type=jnp.float32)
        rows_kept[n] = jnp.where(x == 0, own[:8], own[8:]).astype(BF)
        rows_given[n] = jnp.where(x == 0, own[8:], own[:8]).astype(BF)
        train_t[n] = across(basis_t, train[...]).astype(BF)
        query_t[n] = across(basis_t, query[...]).astype(BF)

    def weigh(n, k):
        weights[k] = 1.0 / (eig[n].T + damping)

    def gram(n, k):
        layer = info[1 + base + n] // 32
        code = codes[...]
        rows = train_t[n]
        zero = jnp.zeros_like(rows)
        for h in range(2):
            left = jnp.concatenate(
                [jnp.where(code == s, rows, zero) for s in range(4 * h, 4 * h + 4)], axis=0
            )
            for c in range(3):
                cols = slice(c * 256, (c + 1) * 256)
                part = jnp.dot(left, grads[layer, :, cols], preferred_element_type=jnp.float32)
                part = part.reshape(4, TILE_A, 256) * weights[k, :, cols][None]
                scaled[k][h * 512 : (h + 1) * 512, cols] = part.astype(BF).reshape(512, 256)

    def project(n, k):
        layer = info[1 + base + n] // 32
        query = query_t[n].astype(jnp.float32)
        for h in range(2):
            part = jnp.dot(
                scaled[k][h * 512 : (h + 1) * 512, :],
                query_grads[layer],
                preferred_element_type=jnp.float32,
            )
            part = part.reshape(4, TILE_A, TOKENS) * query[None]
            acc[4 * h : 4 * h + 4] += jnp.sum(part.reshape(4, TILE_A // 8, 8, TOKENS), axis=1)

    rotate(0)
    rotate(1)
    eig_copy(0).wait()
    weigh(0, 0)
    eig_copy(1).wait()
    weigh(1, 1)
    gram(0, 0)

    @pl.loop(0, count - 2, step=2)
    def _(n):
        eig_copy(n + 2).wait()
        eig_copy(n + 3).wait()
        gram(n + 1, 1)
        rotate(n + 2)
        project(n, 0)
        weigh(n + 2, 0)
        gram(n + 2, 0)
        rotate(n + 3)
        project(n + 1, 1)
        weigh(n + 3, 1)

    gram(count - 1, 1)
    project(count - 2, 0)
    project(count - 1, 1)
    total = before[...] + jnp.sum(acc[...], axis=1)
    if last:
        outs[0][...] = jnp.where(x == 0, total[:SEQS], total[SEQS:])
        outs[1][...] = jnp.where(x == 0, total[SEQS:], total[:SEQS])
    else:
        outs[0][...] = total


VMEM = pl.BlockSpec(memory_space=pltpu.VMEM)
SMEM = pl.BlockSpec(memory_space=pltpu.SMEM)
HBM = pl.BlockSpec(memory_space=pltpu.HBM)


def score_tiles(base, count, last, info, arrays, places, grads, query_grads, codes, eigenvalues, before):
    width = grads.shape[2]

    def kernel(info_ref, *refs):
        held = refs[: len(arrays)]
        units = [(held[a], which) for a, which in places]
        score_kernel(base, count, last, info_ref, *units, *refs[len(arrays) :])

    sums = (
        [jax.ShapeDtypeStruct((SEQS, TOKENS), jnp.float32)] * 2
        if last
        else [jax.ShapeDtypeStruct((GROUPS, TOKENS), jnp.float32)]
    )
    rows = [jax.ShapeDtypeStruct((count, 8, TILE_A), BF)] * 2
    return pl.pallas_call(
        kernel,
        in_specs=[SMEM] + [VMEM] * len(arrays) + [VMEM, VMEM, VMEM, HBM, VMEM],
        out_specs=[VMEM] * len(sums + rows),
        out_shape=sums + rows,
        scratch_shapes=[
            pltpu.VMEM((NQ, 4, 32, TILE_A), BF),
            pltpu.VMEM((TOKENS, TILE_A), BF),
            pltpu.VMEM((TOKENS, TILE_A), BF),
            pltpu.VMEM((count, TILE_A, TOKENS), BF),
            pltpu.VMEM((count, TILE_A, TOKENS), BF),
            pltpu.VMEM((count, width, TILE_A), jnp.float32),
            pltpu.VMEM((GROUPS * TILE_A, width), BF),
            pltpu.VMEM((GROUPS * TILE_A, width), BF),
            pltpu.VMEM((2, TILE_A, width), jnp.float32),
            pltpu.VMEM((GROUPS, 8, TOKENS), jnp.float32),
            pltpu.SemaphoreType.DMA((count,)),
        ],
        compiler_params=pltpu.CompilerParams(vmem_limit_bytes=42 * 1024 * 1024),
        cost_estimate=pl.CostEstimate(
            flops=count * 10**7 if base == 0 else count * 10**9, bytes_accessed=count * 10**6 // 2, transcendentals=0
        ),
    )(info, *arrays, grads, query_grads, codes, eigenvalues, before)


def unpack_kernel(info, kept_a, kept_b, kept_c, came, out):
    first = kept_a.shape[0]
    both = WAVES * NQ
    for place in range(2 * both):
        half, n = place // both, place % both
        if half:
            rows = came[n]
        elif n < first:
            rows = kept_a[n]
        else:
            rows = kept_b[n - first] if n < NQ else kept_c[n - NQ]
        tile = info[1 + n + (both + 1 if half else 0)]
        cols = pl.ds(pl.multiple_of((tile % 32) * TILE_A, TILE_A), TILE_A)
        out[tile // 32, :, cols] = rows


def after(value, *others):
    return lax.optimization_barrier((value, *others))[0]


def paired_body(
    train_inputs,
    train_outgrads,
    sequence_ids,
    query_inputs,
    query_outgrads,
    eigenvalues,
    input_basis,
    slot_list,
    output_basis,
):
    x = lax.axis_index("parts")
    me = lax.axis_index("query")
    train_other = lax.ppermute(train_inputs, "parts", SWAP)
    ids = jnp.arange(64, dtype=jnp.int32)
    tile_of = jnp.sum(jnp.where(slot_list[None, :] == ids[:, None], ids[None, :], 0), axis=1)
    by_half = tile_of.reshape(NQ, 2, WAVES).transpose(1, 2, 0).reshape(2, WAVES * NQ)
    mine = jnp.where(x == 0, by_half[0], by_half[1])
    theirs = jnp.where(x == 0, by_half[1], by_half[0])
    ids = sequence_ids.reshape(1, sequence_ids.shape[0])
    ids_other = lax.ppermute(after(ids, mine), "parts", SWAP)
    side = x.reshape(1).astype(jnp.int32)
    info = jnp.concatenate([me.reshape(1).astype(jnp.int32), mine, side, theirs])

    packed = pl.pallas_call(
        pack_kernel,
        in_specs=[SMEM, VMEM, VMEM, VMEM, VMEM],
        out_specs=[VMEM] * WAVES,
        out_shape=[jax.ShapeDtypeStruct((UNIT, 32, TILE_A), BF)] * WAVES,
        compiler_params=pltpu.CompilerParams(vmem_limit_bytes=8 * 1024 * 1024),
    )(after(info, ids_other), train_inputs, train_other, query_inputs, input_basis)

    out_other = lax.ppermute(after(train_outgrads, train_other), "parts", SWAP)
    slab = train_outgrads.shape[2]
    little = pltpu.CompilerParams(vmem_limit_bytes=16 * 1024 * 1024)
    query_grads = pl.pallas_call(
        query_kernel,
        in_specs=[VMEM] * 2,
        out_specs=VMEM,
        out_shape=jax.ShapeDtypeStruct((LAYERS, slab, TOKENS), BF),
        compiler_params=little,
    )(query_outgrads, output_basis)
    grads, codes = pl.pallas_call(
        train_kernel,
        in_specs=[SMEM] + [VMEM] * 5,
        out_specs=[VMEM, VMEM],
        out_shape=[
            jax.ShapeDtypeStruct((LAYERS, TOKENS, slab), BF),
            jax.ShapeDtypeStruct((1, TOKENS), jnp.int32),
        ],
        compiler_params=little,
    )(info, train_outgrads, out_other, ids, ids_other, output_basis)

    units = [None] * NQ
    units[0] = packed[0]
    units[4] = hop(packed[0], 4)
    units[12] = hop(packed[0], 12)
    units[8] = hop(after(packed[0], units[4], units[12], query_grads), 8)
    units[2] = hop(units[0], 2)
    units[6] = hop(units[4], 2)
    units[14] = hop(units[12], 2)
    units[10] = hop(after(units[8], grads, units[2], units[6], units[14]), 2)
    for d in (0, 2, 4, 6, 12, 14, 8, 10):
        units[d ^ 1] = hop(units[d], 1)
    places0 = [(d, None) for d in range(NQ)]

    zero = jnp.zeros((GROUPS, TOKENS), jnp.float32)
    common = (grads, query_grads, codes, eigenvalues)
    part0, kept_a, given_a = score_tiles(0, 8, False, info, units, places0, *common, zero)

    second = after(packed[1], units[8])
    along = [hop(second, d) for d in (4, 12, 8)]
    near = hop(second, 2)
    *along, near, _ = lax.optimization_barrier((*along, near, part0))
    line = jnp.stack(along)
    beside = hop(line, 2)
    part1, kept_b, given_b = score_tiles(8, 8, False, info, units, places0, *common, part0)
    beside = after(beside, part1)
    arrays = [second, near, line, beside]
    arrays = arrays + [hop(array, 1) for array in arrays]
    order = {4: 0, 12: 1, 8: 2}
    places1 = []
    for d in range(NQ):
        across_y = (d & 2) // 2 + 4 * (d & 1)
        far = d & 12
        places1.append((across_y + 2, order[far]) if far else (across_y, None))
    keep, give, kept1, given1 = score_tiles(
        16, 16, True, info, arrays, places1, *common, part1
    )

    total = keep + lax.ppermute(give, "parts", SWAP)
    came = lax.ppermute(jnp.concatenate([given_a, given_b, given1], axis=0), "parts", SWAP)
    total = after(total, came)
    rotated_out = pl.pallas_call(
        unpack_kernel,
        in_specs=[SMEM] + [VMEM] * 4,
        out_specs=VMEM,
        out_shape=jax.ShapeDtypeStruct(train_inputs.shape, BF),
        compiler_params=pltpu.CompilerParams(vmem_limit_bytes=8 * 1024 * 1024),
    )(info, kept_a, kept_b, kept1, came)
    for bits in (1, 2, 4):
        total = total + hop(total, bits)
    total = after(total, rotated_out)
    total = total + hop(total, 8)
    scores = jnp.sum(total.reshape(SEQS, QUERIES, QLEN), axis=2).T
    return (scores, rotated_out)


def solution(mesh):
    paired = mesh.shape["parts"] == 2 and mesh.shape["query"] == NQ
    return jax.shard_map(
        paired_body if paired else general_body,
        mesh=mesh,
        in_specs=(
            P(None, ("parts", "query"), None),
            P(None, "parts", "query"),
            P("parts"),
            P(None, "query", None),
            P(None, None, "query"),
            P(None, "query", None),
            P("query", None, None),
            P(),
            P(None, "query", None, None),
        ),
        out_specs=(P(None, "parts"), P(None, ("parts", "query"), None)),
        check_vma=False,
    )
```

```python
import jax
import jax.numpy as jnp
from jax import lax
from jax.experimental import pallas as pl
from jax.experimental.pallas import tpu as pltpu
from jax.sharding import PartitionSpec as P

D = 4096
LAYERS = 2
TILE_A = 128
TILE_S = 64
SEQS = 4
QUERIES = 16
QLEN = 16


damping = 0.05


def rotate_blocks(rows, block_tiles, width):
    layer_count, row_count, feature_count = rows.shape
    blocks = rows.reshape(layer_count, row_count, feature_count // width, width)
    shaped = block_tiles.reshape(layer_count, feature_count // width, width, width)
    turned = jnp.einsum("lrbi,lbij->lrbj", blocks, shaped, preferred_element_type=jnp.float32)
    return turned.reshape(layer_count, row_count, feature_count).astype(jnp.bfloat16)


def general_body(
    train_inputs,
    train_outgrads,
    sequence_ids,
    query_inputs,
    query_outgrads,
    eigenvalues,
    input_basis,
    slot_list,
    output_basis,
):
    every_slot = lax.all_gather(input_basis, "query", axis=0, tiled=True)
    basis_tiles = jnp.take(every_slot, slot_list, axis=0)
    rotated_out = rotate_blocks(train_inputs, basis_tiles, TILE_A)
    own_query = rotate_blocks(query_inputs, basis_tiles, TILE_A)
    rotated_train, rotated_query = (
        lax.all_gather(rotated_out, "query", axis=1, tiled=True),
        lax.all_gather(own_query, "query", axis=1, tiled=True),
    )
    grads_rot = rotate_blocks(train_outgrads, output_basis, TILE_S)
    query_rot = rotate_blocks(query_outgrads, output_basis, TILE_S)
    token_count = grads_rot.shape[1]
    slab_width = grads_rot.shape[2]
    weights = 1.0 / (eigenvalues + damping)
    onehot = (sequence_ids[:, None] == jnp.arange(SEQS, dtype=jnp.int32)[None, :]).astype(
        jnp.bfloat16
    )
    totals = jnp.zeros((SEQS, QUERIES * QLEN), jnp.float32)
    for layer_index in range(LAYERS):
        masked = (onehot[:, :, None] * grads_rot[layer_index][:, None, :]).reshape(
            token_count, SEQS * slab_width
        )
        gram_block = lax.dot_general(
            masked,
            rotated_train[layer_index],
            (((0,), (0,)), ((), ())),
            preferred_element_type=jnp.float32,
        )
        scaled = (gram_block.reshape(SEQS, slab_width, D) * weights[layer_index][None]).astype(
            jnp.bfloat16
        )
        projected = jnp.einsum(
            "sij,uj->siu", scaled, rotated_query[layer_index], preferred_element_type=jnp.float32
        )
        totals = totals + jnp.einsum(
            "siu,ui->su", projected, query_rot[layer_index].astype(jnp.float32)
        )
    partial_value = jnp.sum(totals.reshape(SEQS, QUERIES, QLEN), axis=2).T
    scores = lax.psum(partial_value, "query")
    return (scores, rotated_out)


NQ = 16
WAVES = 2
GROUPS = 2 * SEQS
TOKENS = 256
UNIT = 20
SWAP = [(0, 1), (1, 0)]
BF = jnp.bfloat16


def hop(value, bits):
    return lax.ppermute(value, "query", [(i, i ^ bits) for i in range(NQ)])


def pack_kernel(info, own, other, query, basis, *units):
    x = info[1 + WAVES * NQ]

    for wave in range(WAVES):
        unit = units[wave]

        for owner in range(NQ):
            tile = info[1 + wave * NQ + owner]
            layer = tile // 32
            cols = pl.ds(pl.multiple_of((tile % 32) * TILE_A, TILE_A), TILE_A)
            mine = own[layer, :, cols].astype(jnp.float32)
            came = other[layer, :, cols].astype(jnp.float32)
            first = jnp.where(x == 0, mine, came)
            second = jnp.where(x == 0, came, mine)
            unit[owner, :16, :] = jnp.concatenate([first, second], axis=0).astype(BF)
            unit[owner, 16:, :] = query[layer, :, cols]

        unit[NQ:] = basis[2 * x + wave].reshape(4, 32, TILE_A)


def diagonal(tiles, layer, c):
    blank = jnp.zeros((TILE_S, TILE_S), jnp.float32)
    upper = jnp.concatenate([tiles[layer, 2 * c].astype(jnp.float32), blank], axis=1)
    lower = jnp.concatenate([blank, tiles[layer, 2 * c + 1].astype(jnp.float32)], axis=1)
    return jnp.concatenate([upper, lower], axis=0)


def query_kernel(query, tiles, query_grads):
    for layer in range(LAYERS):
        for c in range(tiles.shape[1] // 2):
            cols = slice(c * TILE_A, (c + 1) * TILE_A)
            block_t = diagonal(tiles, layer, c).T.astype(BF)
            query_grads[layer, cols, :] = across(block_t, query[layer, :, cols]).astype(BF)


def train_kernel(info, own, other, ids, ids_other, tiles, grads, codes):
    x = info[1 + WAVES * NQ]
    for layer in range(LAYERS):
        for c in range(tiles.shape[1] // 2):
            cols = slice(c * TILE_A, (c + 1) * TILE_A)
            tile = diagonal(tiles, layer, c).astype(BF)
            mine = jnp.dot(own[layer, :, cols], tile, preferred_element_type=jnp.float32)
            came = jnp.dot(other[layer, :, cols], tile, preferred_element_type=jnp.float32)
            first = jnp.where(x == 0, mine, came).reshape(NQ, 1, 8, TILE_A)
            second = jnp.where(x == 0, came, mine).reshape(NQ, 1, 8, TILE_A)
            rows = jnp.concatenate([first, second], axis=1).reshape(TOKENS, TILE_A)
            grads[layer, :, cols] = rows.astype(BF)
    half = TOKENS // 2
    row = lax.broadcasted_iota(jnp.int32, (half, TOKENS), 0)
    col = lax.broadcasted_iota(jnp.int32, (half, TOKENS), 1)
    hit = row == (col >> 4) * 8 + (col & 7)
    part = (col >> 3) & 1
    own_f, other_f = ids[...].astype(jnp.float32), ids_other[...].astype(jnp.float32)
    mine = jnp.where(hit & (part == x), 1.0, 0.0)
    came = jnp.where(hit & (part != x), 1.0, 0.0)
    placed = jnp.dot(
        jnp.broadcast_to(own_f, (8, half)), mine, preferred_element_type=jnp.float32
    ) + jnp.dot(jnp.broadcast_to(other_f, (8, half)), came, preferred_element_type=jnp.float32)
    codes[...] = (placed[:1] + 0.5).astype(jnp.int32) + SEQS * part[:1]


def across(left, right):
    return lax.dot_general(
        left, right, (((1,), (1,)), ((), ())), preferred_element_type=jnp.float32
    )


def score_kernel(base, count, last, info, *refs):
    units = refs[:NQ]
    grads, query_grads, codes, eigen, before = refs[NQ : NQ + 5]
    outs = refs[NQ + 5 : NQ + (9 if last else 8)]
    rows_kept, rows_given = outs[-2:]
    bases, train, query, train_t, query_t, eig, scaled0, scaled1, weights, acc, sems = refs[
        NQ + 5 + len(outs) :
    ]
    scaled = (scaled0, scaled1)
    me = info[0]
    x = info[1 + WAVES * NQ]
    start = base % NQ

    def piece(d, index):
        unit, which = units[d]
        return unit[index] if which is None else unit[which, index]

    def eig_copy(n):
        tile = info[1 + base + n]
        cols = pl.ds(pl.multiple_of((tile % 32) * TILE_A, TILE_A), TILE_A)
        return pltpu.make_async_copy(eigen.at[tile // 32, :, cols], eig.at[n], sems.at[n])

    for n in range(count):
        eig_copy(n).start()
    acc[...] = jnp.zeros_like(acc)
    for d in range(NQ):
        bases[me ^ d] = piece(d, slice(NQ, NQ + 4))

    def rotate(n):
        basis = bases[start + n].reshape(TILE_A, TILE_A)
        basis_t = basis.astype(jnp.float32).T.astype(BF)
        for d in range(NQ):
            rows = piece(d, start + n)
            place = pl.ds(pl.multiple_of((me ^ d) * 16, 16), 16)
            train[place, :] = rows[:16]
            query[place, :] = rows[16:]
        own = jnp.dot(piece(0, start + n)[:16], basis, preferred_element_type=jnp.float32)
        rows_kept[n] = jnp.where(x == 0, own[:8], own[8:]).astype(BF)
        rows_given[n] = jnp.where(x == 0, own[8:], own[:8]).astype(BF)
        train_t[n] = across(basis_t, train[...]).astype(BF)
        query_t[n] = across(basis_t, query[...]).astype(BF)

    def weigh(n, k):
        weights[k] = 1.0 / (eig[n].T + damping)

    def gram(n, k):
        layer = info[1 + base + n] // 32
        code = codes[...]
        rows = train_t[n]
        zero = jnp.zeros_like(rows)
        for h in range(2):
            left = jnp.concatenate(
                [jnp.where(code == s, rows, zero) for s in range(4 * h, 4 * h + 4)], axis=0
            )
            for c in range(3):
                cols = slice(c * 256, (c + 1) * 256)
                part = jnp.dot(left, grads[layer, :, cols], preferred_element_type=jnp.float32)
                part = part.reshape(4, TILE_A, 256) * weights[k, :, cols][None]
                scaled[k][h * 512 : (h + 1) * 512, cols] = part.astype(BF).reshape(512, 256)

    def project(n, k):
        layer = info[1 + base + n] // 32
        query = query_t[n].astype(jnp.float32)
        for h in range(2):
            part = jnp.dot(
                scaled[k][h * 512 : (h + 1) * 512, :],
                query_grads[layer],
                preferred_element_type=jnp.float32,
            )
            part = part.reshape(4, TILE_A, TOKENS) * query[None]
            acc[4 * h : 4 * h + 4] += jnp.sum(part.reshape(4, TILE_A // 8, 8, TOKENS), axis=1)

    rotate(0)
    rotate(1)
    eig_copy(0).wait()
    weigh(0, 0)
    eig_copy(1).wait()
    weigh(1, 1)
    gram(0, 0)

    @pl.loop(0, count - 2, step=2)
    def _(n):
        eig_copy(n + 2).wait()
        eig_copy(n + 3).wait()
        gram(n + 1, 1)
        rotate(n + 2)
        project(n, 0)
        weigh(n + 2, 0)
        gram(n + 2, 0)
        rotate(n + 3)
        project(n + 1, 1)
        weigh(n + 3, 1)

    gram(count - 1, 1)
    project(count - 2, 0)
    project(count - 1, 1)
    total = before[...] + jnp.sum(acc[...], axis=1)
    if last:
        outs[0][...] = jnp.where(x == 0, total[:SEQS], total[SEQS:])
        outs[1][...] = jnp.where(x == 0, total[SEQS:], total[:SEQS])
    else:
        outs[0][...] = total


VMEM = pl.BlockSpec(memory_space=pltpu.VMEM)
SMEM = pl.BlockSpec(memory_space=pltpu.SMEM)
HBM = pl.BlockSpec(memory_space=pltpu.HBM)


def score_tiles(base, count, last, info, arrays, places, grads, query_grads, codes, eigenvalues, before):
    width = grads.shape[2]

    def kernel(info_ref, *refs):
        held = refs[: len(arrays)]
        units = [(held[a], which) for a, which in places]
        score_kernel(base, count, last, info_ref, *units, *refs[len(arrays) :])

    sums = (
        [jax.ShapeDtypeStruct((SEQS, TOKENS), jnp.float32)] * 2
        if last
        else [jax.ShapeDtypeStruct((GROUPS, TOKENS), jnp.float32)]
    )
    rows = [jax.ShapeDtypeStruct((count, 8, TILE_A), BF)] * 2
    return pl.pallas_call(
        kernel,
        in_specs=[SMEM] + [VMEM] * len(arrays) + [VMEM, VMEM, VMEM, HBM, VMEM],
        out_specs=[VMEM] * len(sums + rows),
        out_shape=sums + rows,
        scratch_shapes=[
            pltpu.VMEM((NQ, 4, 32, TILE_A), BF),
            pltpu.VMEM((TOKENS, TILE_A), BF),
            pltpu.VMEM((TOKENS, TILE_A), BF),
            pltpu.VMEM((count, TILE_A, TOKENS), BF),
            pltpu.VMEM((count, TILE_A, TOKENS), BF),
            pltpu.VMEM((count, width, TILE_A), jnp.float32),
            pltpu.VMEM((GROUPS * TILE_A, width), BF),
            pltpu.VMEM((GROUPS * TILE_A, width), BF),
            pltpu.VMEM((2, TILE_A, width), jnp.float32),
            pltpu.VMEM((GROUPS, 8, TOKENS), jnp.float32),
            pltpu.SemaphoreType.DMA((count,)),
        ],
        compiler_params=pltpu.CompilerParams(vmem_limit_bytes=42 * 1024 * 1024),
        cost_estimate=pl.CostEstimate(
            flops=count * 10**7 if base == 0 else count * 10**9, bytes_accessed=count * 10**6 // 2, transcendentals=0
        ),
    )(info, *arrays, grads, query_grads, codes, eigenvalues, before)


def unpack_kernel(info, kept_a, kept_b, kept_c, came, out):
    first = kept_a.shape[0]
    both = WAVES * NQ
    for place in range(2 * both):
        half, n = place // both, place % both
        if half:
            rows = came[n]
        elif n < first:
            rows = kept_a[n]
        else:
            rows = kept_b[n - first] if n < NQ else kept_c[n - NQ]
        tile = info[1 + n + (both + 1 if half else 0)]
        cols = pl.ds(pl.multiple_of((tile % 32) * TILE_A, TILE_A), TILE_A)
        out[tile // 32, :, cols] = rows


def after(value, *others):
    return lax.optimization_barrier((value, *others))[0]


def paired_body(
    train_inputs,
    train_outgrads,
    sequence_ids,
    query_inputs,
    query_outgrads,
    eigenvalues,
    input_basis,
    slot_list,
    output_basis,
):
    x = lax.axis_index("parts")
    me = lax.axis_index("query")
    train_other = lax.ppermute(train_inputs, "parts", SWAP)
    ids = jnp.arange(64, dtype=jnp.int32)
    tile_of = jnp.sum(jnp.where(slot_list[None, :] == ids[:, None], ids[None, :], 0), axis=1)
    by_half = tile_of.reshape(NQ, 2, WAVES).transpose(1, 2, 0).reshape(2, WAVES * NQ)
    mine = jnp.where(x == 0, by_half[0], by_half[1])
    theirs = jnp.where(x == 0, by_half[1], by_half[0])
    ids = sequence_ids.reshape(1, sequence_ids.shape[0])
    ids_other = lax.ppermute(after(ids, mine), "parts", SWAP)
    side = x.reshape(1).astype(jnp.int32)
    info = jnp.concatenate([me.reshape(1).astype(jnp.int32), mine, side, theirs])

    packed = pl.pallas_call(
        pack_kernel,
        in_specs=[SMEM, VMEM, VMEM, VMEM, VMEM],
        out_specs=[VMEM] * WAVES,
        out_shape=[jax.ShapeDtypeStruct((UNIT, 32, TILE_A), BF)] * WAVES,
        compiler_params=pltpu.CompilerParams(vmem_limit_bytes=8 * 1024 * 1024),
    )(after(info, ids_other), train_inputs, train_other, query_inputs, input_basis)

    out_other = lax.ppermute(after(train_outgrads, packed[0]), "parts", SWAP)
    slab = train_outgrads.shape[2]
    little = pltpu.CompilerParams(vmem_limit_bytes=16 * 1024 * 1024)
    query_grads = pl.pallas_call(
        query_kernel,
        in_specs=[VMEM] * 2,
        out_specs=VMEM,
        out_shape=jax.ShapeDtypeStruct((LAYERS, slab, TOKENS), BF),
        compiler_params=little,
    )(query_outgrads, output_basis)
    grads, codes = pl.pallas_call(
        train_kernel,
        in_specs=[SMEM] + [VMEM] * 5,
        out_specs=[VMEM, VMEM],
        out_shape=[
            jax.ShapeDtypeStruct((LAYERS, TOKENS, slab), BF),
            jax.ShapeDtypeStruct((1, TOKENS), jnp.int32),
        ],
        compiler_params=little,
    )(info, train_outgrads, out_other, ids, ids_other, output_basis)

    units = [None] * NQ
    units[0] = packed[0]
    units[4] = hop(packed[0], 4)
    units[12] = hop(packed[0], 12)
    units[8] = hop(after(packed[0], units[4], units[12], query_grads), 8)
    units[2] = hop(units[0], 2)
    units[6] = hop(units[4], 2)
    units[14] = hop(after(units[12], out_other), 2)
    units[10] = hop(after(units[8], units[2], units[6], units[14]), 2)
    for d in (0, 2, 4, 6, 12, 8, 10):
        units[d ^ 1] = hop(units[d], 1)
    units[15] = hop(after(units[14], grads), 1)
    places0 = [(d, None) for d in range(NQ)]

    zero = jnp.zeros((GROUPS, TOKENS), jnp.float32)
    common = (grads, query_grads, codes, eigenvalues)
    part0, kept_a, given_a = score_tiles(0, 8, False, info, units, places0, *common, zero)

    second = after(packed[1], units[8])
    along = [hop(second, d) for d in (4, 12, 8)]
    near = hop(second, 2)
    *along, near, _ = lax.optimization_barrier((*along, near, part0))
    line = jnp.stack(along)
    beside = hop(line, 2)
    part1, kept_b, given_b = score_tiles(8, 8, False, info, units, places0, *common, part0)
    beside = after(beside, part1)
    arrays = [second, near, line, beside]
    arrays = arrays + [hop(array, 1) for array in arrays]
    order = {4: 0, 12: 1, 8: 2}
    places1 = []
    for d in range(NQ):
        across_y = (d & 2) // 2 + 4 * (d & 1)
        far = d & 12
        places1.append((across_y + 2, order[far]) if far else (across_y, None))
    keep, give, kept1, given1 = score_tiles(
        16, 16, True, info, arrays, places1, *common, part1
    )

    total = keep + lax.ppermute(give, "parts", SWAP)
    came = lax.ppermute(jnp.concatenate([given_a, given_b, given1], axis=0), "parts", SWAP)
    total = after(total, came)
    rotated_out = pl.pallas_call(
        unpack_kernel,
        in_specs=[SMEM] + [VMEM] * 4,
        out_specs=VMEM,
        out_shape=jax.ShapeDtypeStruct(train_inputs.shape, BF),
        compiler_params=pltpu.CompilerParams(vmem_limit_bytes=8 * 1024 * 1024),
    )(info, kept_a, kept_b, kept1, came)
    for bits in (1, 2, 4):
        total = total + hop(total, bits)
    total = after(total, rotated_out)
    total = total + hop(total, 8)
    scores = jnp.sum(total.reshape(SEQS, QUERIES, QLEN), axis=2).T
    return (scores, rotated_out)


def solution(mesh):
    paired = mesh.shape["parts"] == 2 and mesh.shape["query"] == NQ
    return jax.shard_map(
        paired_body if paired else general_body,
        mesh=mesh,
        in_specs=(
            P(None, ("parts", "query"), None),
            P(None, "parts", "query"),
            P("parts"),
            P(None, "query", None),
            P(None, None, "query"),
            P(None, "query", None),
            P("query", None, None),
            P(),
            P(None, "query", None, None),
        ),
        out_specs=(P(None, "parts"), P(None, ("parts", "query"), None)),
        check_vma=False,
    )
```

```python
import jax
import jax.numpy as jnp
from jax import lax
from jax.experimental import pallas as pl
from jax.experimental.pallas import tpu as pltpu
from jax.sharding import PartitionSpec as P

D = 4096
LAYERS = 2
TILE_A = 128
TILE_S = 64
SEQS = 4
QUERIES = 16
QLEN = 16


damping = 0.05


def rotate_blocks(rows, block_tiles, width):
    layer_count, row_count, feature_count = rows.shape
    blocks = rows.reshape(layer_count, row_count, feature_count // width, width)
    shaped = block_tiles.reshape(layer_count, feature_count // width, width, width)
    turned = jnp.einsum("lrbi,lbij->lrbj", blocks, shaped, preferred_element_type=jnp.float32)
    return turned.reshape(layer_count, row_count, feature_count).astype(jnp.bfloat16)


def general_body(
    train_inputs,
    train_outgrads,
    sequence_ids,
    query_inputs,
    query_outgrads,
    eigenvalues,
    input_basis,
    slot_list,
    output_basis,
):
    every_slot = lax.all_gather(input_basis, "query", axis=0, tiled=True)
    basis_tiles = jnp.take(every_slot, slot_list, axis=0)
    rotated_out = rotate_blocks(train_inputs, basis_tiles, TILE_A)
    own_query = rotate_blocks(query_inputs, basis_tiles, TILE_A)
    rotated_train, rotated_query = (
        lax.all_gather(rotated_out, "query", axis=1, tiled=True),
        lax.all_gather(own_query, "query", axis=1, tiled=True),
    )
    grads_rot = rotate_blocks(train_outgrads, output_basis, TILE_S)
    query_rot = rotate_blocks(query_outgrads, output_basis, TILE_S)
    token_count = grads_rot.shape[1]
    slab_width = grads_rot.shape[2]
    weights = 1.0 / (eigenvalues + damping)
    onehot = (sequence_ids[:, None] == jnp.arange(SEQS, dtype=jnp.int32)[None, :]).astype(
        jnp.bfloat16
    )
    totals = jnp.zeros((SEQS, QUERIES * QLEN), jnp.float32)
    for layer_index in range(LAYERS):
        masked = (onehot[:, :, None] * grads_rot[layer_index][:, None, :]).reshape(
            token_count, SEQS * slab_width
        )
        gram_block = lax.dot_general(
            masked,
            rotated_train[layer_index],
            (((0,), (0,)), ((), ())),
            preferred_element_type=jnp.float32,
        )
        scaled = (gram_block.reshape(SEQS, slab_width, D) * weights[layer_index][None]).astype(
            jnp.bfloat16
        )
        projected = jnp.einsum(
            "sij,uj->siu", scaled, rotated_query[layer_index], preferred_element_type=jnp.float32
        )
        totals = totals + jnp.einsum(
            "siu,ui->su", projected, query_rot[layer_index].astype(jnp.float32)
        )
    partial_value = jnp.sum(totals.reshape(SEQS, QUERIES, QLEN), axis=2).T
    scores = lax.psum(partial_value, "query")
    return (scores, rotated_out)


NQ = 16
WAVES = 2
GROUPS = 2 * SEQS
TOKENS = 256
UNIT = 20
SWAP = [(0, 1), (1, 0)]
BF = jnp.bfloat16


def hop(value, bits):
    return lax.ppermute(value, "query", [(i, i ^ bits) for i in range(NQ)])


def pack_kernel(info, own, other, query, basis, *units):
    x = info[1 + WAVES * NQ]

    for wave in range(WAVES):
        unit = units[wave]

        for owner in range(NQ):
            tile = info[1 + wave * NQ + owner]
            layer = tile // 32
            cols = pl.ds(pl.multiple_of((tile % 32) * TILE_A, TILE_A), TILE_A)
            mine = own[layer, :, cols].astype(jnp.float32)
            came = other[layer, :, cols].astype(jnp.float32)
            first = jnp.where(x == 0, mine, came)
            second = jnp.where(x == 0, came, mine)
            unit[owner, :16, :] = jnp.concatenate([first, second], axis=0).astype(BF)
            unit[owner, 16:, :] = query[layer, :, cols]

        unit[NQ:] = basis[2 * x + wave].reshape(4, 32, TILE_A)


def diagonal(tiles, layer, c):
    blank = jnp.zeros((TILE_S, TILE_S), jnp.float32)
    upper = jnp.concatenate([tiles[layer, 2 * c].astype(jnp.float32), blank], axis=1)
    lower = jnp.concatenate([blank, tiles[layer, 2 * c + 1].astype(jnp.float32)], axis=1)
    return jnp.concatenate([upper, lower], axis=0)


def query_kernel(query, tiles, query_grads):
    for layer in range(LAYERS):
        for c in range(tiles.shape[1] // 2):
            cols = slice(c * TILE_A, (c + 1) * TILE_A)
            block_t = diagonal(tiles, layer, c).T.astype(BF)
            query_grads[layer, cols, :] = across(block_t, query[layer, :, cols]).astype(BF)


def train_kernel(info, own, other, ids, ids_other, tiles, grads, codes):
    x = info[1 + WAVES * NQ]
    for layer in range(LAYERS):
        for c in range(tiles.shape[1] // 2):
            cols = slice(c * TILE_A, (c + 1) * TILE_A)
            tile = diagonal(tiles, layer, c).astype(BF)
            mine = jnp.dot(own[layer, :, cols], tile, preferred_element_type=jnp.float32)
            came = jnp.dot(other[layer, :, cols], tile, preferred_element_type=jnp.float32)
            first = jnp.where(x == 0, mine, came).reshape(NQ, 1, 8, TILE_A)
            second = jnp.where(x == 0, came, mine).reshape(NQ, 1, 8, TILE_A)
            rows = jnp.concatenate([first, second], axis=1).reshape(TOKENS, TILE_A)
            grads[layer, :, cols] = rows.astype(BF)
    half = TOKENS // 2
    row = lax.broadcasted_iota(jnp.int32, (half, TOKENS), 0)
    col = lax.broadcasted_iota(jnp.int32, (half, TOKENS), 1)
    hit = row == (col >> 4) * 8 + (col & 7)
    part = (col >> 3) & 1
    own_f, other_f = ids[...].astype(jnp.float32), ids_other[...].astype(jnp.float32)
    mine = jnp.where(hit & (part == x), 1.0, 0.0)
    came = jnp.where(hit & (part != x), 1.0, 0.0)
    placed = jnp.dot(
        jnp.broadcast_to(own_f, (8, half)), mine, preferred_element_type=jnp.float32
    ) + jnp.dot(jnp.broadcast_to(other_f, (8, half)), came, preferred_element_type=jnp.float32)
    codes[...] = (placed[:1] + 0.5).astype(jnp.int32) + SEQS * part[:1]


def across(left, right):
    return lax.dot_general(
        left, right, (((1,), (1,)), ((), ())), preferred_element_type=jnp.float32
    )


def score_kernel(base, count, last, info, *refs):
    units = refs[:NQ]
    grads, query_grads, codes, eigen, before = refs[NQ : NQ + 5]
    outs = refs[NQ + 5 : NQ + (9 if last else 8)]
    rows_kept, rows_given = outs[-2:]
    bases, train, query, train_t, query_t, eig, scaled0, scaled1, weights, acc, sems = refs[
        NQ + 5 + len(outs) :
    ]
    scaled = (scaled0, scaled1)
    me = info[0]
    x = info[1 + WAVES * NQ]
    start = base % NQ

    def piece(d, index):
        unit, which = units[d]
        return unit[index] if which is None else unit[which, index]

    def eig_copy(n):
        tile = info[1 + base + n]
        cols = pl.ds(pl.multiple_of((tile % 32) * TILE_A, TILE_A), TILE_A)
        return pltpu.make_async_copy(eigen.at[tile // 32, :, cols], eig.at[n], sems.at[n])

    for n in range(count):
        eig_copy(n).start()
    acc[...] = jnp.zeros_like(acc)
    for d in range(NQ):
        bases[me ^ d] = piece(d, slice(NQ, NQ + 4))

    def rotate(n):
        basis = bases[start + n].reshape(TILE_A, TILE_A)
        basis_t = basis.astype(jnp.float32).T.astype(BF)
        for d in range(NQ):
            rows = piece(d, start + n)
            place = pl.ds(pl.multiple_of((me ^ d) * 16, 16), 16)
            train[place, :] = rows[:16]
            query[place, :] = rows[16:]
        own = jnp.dot(piece(0, start + n)[:16], basis, preferred_element_type=jnp.float32)
        rows_kept[n] = jnp.where(x == 0, own[:8], own[8:]).astype(BF)
        rows_given[n] = jnp.where(x == 0, own[8:], own[:8]).astype(BF)
        train_t[n] = across(basis_t, train[...]).astype(BF)
        query_t[n] = across(basis_t, query[...]).astype(BF)

    def weigh(n, k):
        weights[k] = 1.0 / (eig[n].T + damping)

    def gram(n, k):
        layer = info[1 + base + n] // 32
        code = codes[...]
        rows = train_t[n]
        zero = jnp.zeros_like(rows)
        for h in range(2):
            left = jnp.concatenate(
                [jnp.where(code == s, rows, zero) for s in range(4 * h, 4 * h + 4)], axis=0
            )
            for c in range(3):
                cols = slice(c * 256, (c + 1) * 256)
                part = jnp.dot(left, grads[layer, :, cols], preferred_element_type=jnp.float32)
                part = part.reshape(4, TILE_A, 256) * weights[k, :, cols][None]
                scaled[k][h * 512 : (h + 1) * 512, cols] = part.astype(BF).reshape(512, 256)

    def project(n, k):
        layer = info[1 + base + n] // 32
        query = query_t[n].astype(jnp.float32)
        for h in range(2):
            part = jnp.dot(
                scaled[k][h * 512 : (h + 1) * 512, :],
                query_grads[layer],
                preferred_element_type=jnp.float32,
            )
            part = part.reshape(4, TILE_A, TOKENS) * query[None]
            acc[4 * h : 4 * h + 4] += jnp.sum(part.reshape(4, TILE_A // 8, 8, TOKENS), axis=1)

    rotate(0)
    rotate(1)
    eig_copy(0).wait()
    weigh(0, 0)
    eig_copy(1).wait()
    weigh(1, 1)
    gram(0, 0)

    @pl.loop(0, count - 2, step=2)
    def _(n):
        eig_copy(n + 2).wait()
        eig_copy(n + 3).wait()
        gram(n + 1, 1)
        rotate(n + 2)
        project(n, 0)
        weigh(n + 2, 0)
        gram(n + 2, 0)
        rotate(n + 3)
        project(n + 1, 1)
        weigh(n + 3, 1)

    gram(count - 1, 1)
    project(count - 2, 0)
    project(count - 1, 1)
    total = before[...] + jnp.sum(acc[...], axis=1)
    if last:
        outs[0][...] = jnp.where(x == 0, total[:SEQS], total[SEQS:])
        outs[1][...] = jnp.where(x == 0, total[SEQS:], total[:SEQS])
    else:
        outs[0][...] = total


VMEM = pl.BlockSpec(memory_space=pltpu.VMEM)
SMEM = pl.BlockSpec(memory_space=pltpu.SMEM)
HBM = pl.BlockSpec(memory_space=pltpu.HBM)


def score_tiles(base, count, last, info, arrays, places, grads, query_grads, codes, eigenvalues, before):
    width = grads.shape[2]

    def kernel(info_ref, *refs):
        held = refs[: len(arrays)]
        units = [(held[a], which) for a, which in places]
        score_kernel(base, count, last, info_ref, *units, *refs[len(arrays) :])

    sums = (
        [jax.ShapeDtypeStruct((SEQS, TOKENS), jnp.float32)] * 2
        if last
        else [jax.ShapeDtypeStruct((GROUPS, TOKENS), jnp.float32)]
    )
    rows = [jax.ShapeDtypeStruct((count, 8, TILE_A), BF)] * 2
    return pl.pallas_call(
        kernel,
        in_specs=[SMEM] + [VMEM] * len(arrays) + [VMEM, VMEM, VMEM, HBM, VMEM],
        out_specs=[VMEM] * len(sums + rows),
        out_shape=sums + rows,
        scratch_shapes=[
            pltpu.VMEM((NQ, 4, 32, TILE_A), BF),
            pltpu.VMEM((TOKENS, TILE_A), BF),
            pltpu.VMEM((TOKENS, TILE_A), BF),
            pltpu.VMEM((count, TILE_A, TOKENS), BF),
            pltpu.VMEM((count, TILE_A, TOKENS), BF),
            pltpu.VMEM((count, width, TILE_A), jnp.float32),
            pltpu.VMEM((GROUPS * TILE_A, width), BF),
            pltpu.VMEM((GROUPS * TILE_A, width), BF),
            pltpu.VMEM((2, TILE_A, width), jnp.float32),
            pltpu.VMEM((GROUPS, 8, TOKENS), jnp.float32),
            pltpu.SemaphoreType.DMA((count,)),
        ],
        compiler_params=pltpu.CompilerParams(vmem_limit_bytes=42 * 1024 * 1024),
        cost_estimate=pl.CostEstimate(
            flops=count * 10**7 if base == 0 else count * 10**9, bytes_accessed=count * 10**6 // 2, transcendentals=0
        ),
    )(info, *arrays, grads, query_grads, codes, eigenvalues, before)


def unpack_kernel(info, kept_a, kept_b, kept_c, came, out):
    first = kept_a.shape[0]
    both = WAVES * NQ
    for place in range(2 * both):
        half, n = place // both, place % both
        if half:
            rows = came[n]
        elif n < first:
            rows = kept_a[n]
        else:
            rows = kept_b[n - first] if n < NQ else kept_c[n - NQ]
        tile = info[1 + n + (both + 1 if half else 0)]
        cols = pl.ds(pl.multiple_of((tile % 32) * TILE_A, TILE_A), TILE_A)
        out[tile // 32, :, cols] = rows


def after(value, *others):
    return lax.optimization_barrier((value, *others))[0]


def paired_body(
    train_inputs,
    train_outgrads,
    sequence_ids,
    query_inputs,
    query_outgrads,
    eigenvalues,
    input_basis,
    slot_list,
    output_basis,
):
    x = lax.axis_index("parts")
    me = lax.axis_index("query")
    train_other = lax.ppermute(train_inputs, "parts", SWAP)
    ids = jnp.arange(64, dtype=jnp.int32)
    tile_of = jnp.sum(jnp.where(slot_list[None, :] == ids[:, None], ids[None, :], 0), axis=1)
    by_half = tile_of.reshape(NQ, 2, WAVES).transpose(1, 2, 0).reshape(2, WAVES * NQ)
    mine = jnp.where(x == 0, by_half[0], by_half[1])
    theirs = jnp.where(x == 0, by_half[1], by_half[0])
    ids = sequence_ids.reshape(1, sequence_ids.shape[0])
    side = x.reshape(1).astype(jnp.int32)
    info = jnp.concatenate([me.reshape(1).astype(jnp.int32), mine, side, theirs])

    packed = pl.pallas_call(
        pack_kernel,
        in_specs=[SMEM, VMEM, VMEM, VMEM, VMEM],
        out_specs=[VMEM] * WAVES,
        out_shape=[jax.ShapeDtypeStruct((UNIT, 32, TILE_A), BF)] * WAVES,
        compiler_params=pltpu.CompilerParams(vmem_limit_bytes=8 * 1024 * 1024),
    )(info, train_inputs, train_other, query_inputs, input_basis)

    units = [None] * NQ
    units[0] = packed[0]
    units[4] = hop(packed[0], 4)
    units[12] = hop(packed[0], 12)

    ids_other = lax.ppermute(after(ids, units[12]), "parts", SWAP)
    out_other = lax.ppermute(after(train_outgrads, packed[0]), "parts", SWAP)
    slab = train_outgrads.shape[2]
    little = pltpu.CompilerParams(vmem_limit_bytes=16 * 1024 * 1024)
    query_grads = pl.pallas_call(
        query_kernel,
        in_specs=[VMEM] * 2,
        out_specs=VMEM,
        out_shape=jax.ShapeDtypeStruct((LAYERS, slab, TOKENS), BF),
        compiler_params=little,
    )(query_outgrads, output_basis)
    grads, codes = pl.pallas_call(
        train_kernel,
        in_specs=[SMEM] + [VMEM] * 5,
        out_specs=[VMEM, VMEM],
        out_shape=[
            jax.ShapeDtypeStruct((LAYERS, TOKENS, slab), BF),
            jax.ShapeDtypeStruct((1, TOKENS), jnp.int32),
        ],
        compiler_params=little,
    )(info, train_outgrads, out_other, ids, ids_other, output_basis)

    units[8] = hop(after(packed[0], units[4], units[12], query_grads), 8)
    units[2] = hop(units[0], 2)
    units[6] = hop(units[4], 2)
    units[14] = hop(after(units[12], out_other), 2)
    units[10] = hop(after(units[8], units[2], units[6], units[14]), 2)
    for d in (0, 2, 4, 6, 12, 8, 10):
        units[d ^ 1] = hop(units[d], 1)
    units[15] = hop(after(units[14], grads), 1)
    places0 = [(d, None) for d in range(NQ)]

    zero = jnp.zeros((GROUPS, TOKENS), jnp.float32)
    common = (grads, query_grads, codes, eigenvalues)
    part0, kept_a, given_a = score_tiles(0, 8, False, info, units, places0, *common, zero)

    second = after(packed[1], units[8])
    along = [hop(second, d) for d in (4, 12, 8)]
    near = hop(second, 2)
    *along, near, _ = lax.optimization_barrier((*along, near, part0))
    line = jnp.stack(along)
    beside = hop(line, 2)
    part1, kept_b, given_b = score_tiles(8, 8, False, info, units, places0, *common, part0)
    beside = after(beside, part1)
    arrays = [second, near, line, beside]
    arrays = arrays + [hop(array, 1) for array in arrays]
    order = {4: 0, 12: 1, 8: 2}
    places1 = []
    for d in range(NQ):
        across_y = (d & 2) // 2 + 4 * (d & 1)
        far = d & 12
        places1.append((across_y + 2, order[far]) if far else (across_y, None))
    keep, give, kept1, given1 = score_tiles(
        16, 16, True, info, arrays, places1, *common, part1
    )

    total = keep + lax.ppermute(give, "parts", SWAP)
    came = lax.ppermute(jnp.concatenate([given_a, given_b, given1], axis=0), "parts", SWAP)
    total = after(total, came)
    rotated_out = pl.pallas_call(
        unpack_kernel,
        in_specs=[SMEM] + [VMEM] * 4,
        out_specs=VMEM,
        out_shape=jax.ShapeDtypeStruct(train_inputs.shape, BF),
        compiler_params=pltpu.CompilerParams(vmem_limit_bytes=8 * 1024 * 1024),
    )(info, kept_a, kept_b, kept1, came)
    for bits in (1, 2, 4):
        total = total + hop(total, bits)
    total = after(total, rotated_out)
    total = total + hop(total, 8)
    scores = jnp.sum(total.reshape(SEQS, QUERIES, QLEN), axis=2).T
    return (scores, rotated_out)


def solution(mesh):
    paired = mesh.shape["parts"] == 2 and mesh.shape["query"] == NQ
    return jax.shard_map(
        paired_body if paired else general_body,
        mesh=mesh,
        in_specs=(
            P(None, ("parts", "query"), None),
            P(None, "parts", "query"),
            P("parts"),
            P(None, "query", None),
            P(None, None, "query"),
            P(None, "query", None),
            P("query", None, None),
            P(),
            P(None, "query", None, None),
        ),
        out_specs=(P(None, "parts"), P(None, ("parts", "query"), None)),
        check_vma=False,
    )
```

```python
import jax
import jax.numpy as jnp
from jax import lax
from jax.experimental import pallas as pl
from jax.experimental.pallas import tpu as pltpu
from jax.sharding import PartitionSpec as P

D = 4096
LAYERS = 2
TILE_A = 128
TILE_S = 64
SEQS = 4
QUERIES = 16
QLEN = 16


damping = 0.05


def rotate_blocks(rows, block_tiles, width):
    layer_count, row_count, feature_count = rows.shape
    blocks = rows.reshape(layer_count, row_count, feature_count // width, width)
    shaped = block_tiles.reshape(layer_count, feature_count // width, width, width)
    turned = jnp.einsum("lrbi,lbij->lrbj", blocks, shaped, preferred_element_type=jnp.float32)
    return turned.reshape(layer_count, row_count, feature_count).astype(jnp.bfloat16)


def general_body(
    train_inputs,
    train_outgrads,
    sequence_ids,
    query_inputs,
    query_outgrads,
    eigenvalues,
    input_basis,
    slot_list,
    output_basis,
):
    every_slot = lax.all_gather(input_basis, "query", axis=0, tiled=True)
    basis_tiles = jnp.take(every_slot, slot_list, axis=0)
    rotated_out = rotate_blocks(train_inputs, basis_tiles, TILE_A)
    own_query = rotate_blocks(query_inputs, basis_tiles, TILE_A)
    rotated_train, rotated_query = (
        lax.all_gather(rotated_out, "query", axis=1, tiled=True),
        lax.all_gather(own_query, "query", axis=1, tiled=True),
    )
    grads_rot = rotate_blocks(train_outgrads, output_basis, TILE_S)
    query_rot = rotate_blocks(query_outgrads, output_basis, TILE_S)
    token_count = grads_rot.shape[1]
    slab_width = grads_rot.shape[2]
    weights = 1.0 / (eigenvalues + damping)
    onehot = (sequence_ids[:, None] == jnp.arange(SEQS, dtype=jnp.int32)[None, :]).astype(
        jnp.bfloat16
    )
    totals = jnp.zeros((SEQS, QUERIES * QLEN), jnp.float32)
    for layer_index in range(LAYERS):
        masked = (onehot[:, :, None] * grads_rot[layer_index][:, None, :]).reshape(
            token_count, SEQS * slab_width
        )
        gram_block = lax.dot_general(
            masked,
            rotated_train[layer_index],
            (((0,), (0,)), ((), ())),
            preferred_element_type=jnp.float32,
        )
        scaled = (gram_block.reshape(SEQS, slab_width, D) * weights[layer_index][None]).astype(
            jnp.bfloat16
        )
        projected = jnp.einsum(
            "sij,uj->siu", scaled, rotated_query[layer_index], preferred_element_type=jnp.float32
        )
        totals = totals + jnp.einsum(
            "siu,ui->su", projected, query_rot[layer_index].astype(jnp.float32)
        )
    partial_value = jnp.sum(totals.reshape(SEQS, QUERIES, QLEN), axis=2).T
    scores = lax.psum(partial_value, "query")
    return (scores, rotated_out)


NQ = 16
WAVES = 2
GROUPS = 2 * SEQS
TOKENS = 256
UNIT = 20
SWAP = [(0, 1), (1, 0)]
BF = jnp.bfloat16


def hop(value, bits):
    return lax.ppermute(value, "query", [(i, i ^ bits) for i in range(NQ)])


def pack_kernel(info, own, other, query, basis, *units):
    x = info[1 + WAVES * NQ]

    for wave in range(WAVES):
        unit = units[wave]

        for owner in range(NQ):
            tile = info[1 + wave * NQ + owner]
            layer = tile // 32
            cols = pl.ds(pl.multiple_of((tile % 32) * TILE_A, TILE_A), TILE_A)
            mine = own[layer, :, cols].astype(jnp.float32)
            came = other[layer, :, cols].astype(jnp.float32)
            first = jnp.where(x == 0, mine, came)
            second = jnp.where(x == 0, came, mine)
            unit[owner, :16, :] = jnp.concatenate([first, second], axis=0).astype(BF)
            unit[owner, 16:, :] = query[layer, :, cols]

        unit[NQ:] = basis[2 * x + wave].reshape(4, 32, TILE_A)


def diagonal(tiles, layer, c):
    blank = jnp.zeros((TILE_S, TILE_S), jnp.float32)
    upper = jnp.concatenate([tiles[layer, 2 * c].astype(jnp.float32), blank], axis=1)
    lower = jnp.concatenate([blank, tiles[layer, 2 * c + 1].astype(jnp.float32)], axis=1)
    return jnp.concatenate([upper, lower], axis=0)


def query_kernel(query, tiles, query_grads):
    for layer in range(LAYERS):
        for c in range(tiles.shape[1] // 2):
            cols = slice(c * TILE_A, (c + 1) * TILE_A)
            block_t = diagonal(tiles, layer, c).T.astype(BF)
            query_grads[layer, cols, :] = across(block_t, query[layer, :, cols]).astype(BF)


def train_kernel(info, own, other, ids, ids_other, tiles, grads, codes):
    x = info[1 + WAVES * NQ]
    for layer in range(LAYERS):
        for c in range(tiles.shape[1] // 2):
            cols = slice(c * TILE_A, (c + 1) * TILE_A)
            tile = diagonal(tiles, layer, c).astype(BF)
            mine = jnp.dot(own[layer, :, cols], tile, preferred_element_type=jnp.float32)
            came = jnp.dot(other[layer, :, cols], tile, preferred_element_type=jnp.float32)
            first = jnp.where(x == 0, mine, came).reshape(NQ, 1, 8, TILE_A)
            second = jnp.where(x == 0, came, mine).reshape(NQ, 1, 8, TILE_A)
            rows = jnp.concatenate([first, second], axis=1).reshape(TOKENS, TILE_A)
            grads[layer, :, cols] = rows.astype(BF)
    half = TOKENS // 2
    row = lax.broadcasted_iota(jnp.int32, (half, TOKENS), 0)
    col = lax.broadcasted_iota(jnp.int32, (half, TOKENS), 1)
    hit = row == (col >> 4) * 8 + (col & 7)
    part = (col >> 3) & 1
    own_f, other_f = ids[...].astype(jnp.float32), ids_other[...].astype(jnp.float32)
    mine = jnp.where(hit & (part == x), 1.0, 0.0)
    came = jnp.where(hit & (part != x), 1.0, 0.0)
    placed = jnp.dot(
        jnp.broadcast_to(own_f, (8, half)), mine, preferred_element_type=jnp.float32
    ) + jnp.dot(jnp.broadcast_to(other_f, (8, half)), came, preferred_element_type=jnp.float32)
    codes[...] = (placed[:1] + 0.5).astype(jnp.int32) + SEQS * part[:1]


def across(left, right):
    return lax.dot_general(
        left, right, (((1,), (1,)), ((), ())), preferred_element_type=jnp.float32
    )


def score_kernel(base, count, last, info, *refs):
    units = refs[:NQ]
    grads, query_grads, codes, eigen, before = refs[NQ : NQ + 5]
    outs = refs[NQ + 5 : NQ + (9 if last else 8)]
    rows_kept, rows_given = outs[-2:]
    bases, train, query, train_t, query_t, eig, scaled0, scaled1, weights, acc, sems = refs[
        NQ + 5 + len(outs) :
    ]
    scaled = (scaled0, scaled1)
    me = info[0]
    x = info[1 + WAVES * NQ]
    start = base % NQ

    def piece(d, index):
        unit, which = units[d]
        return unit[index] if which is None else unit[which, index]

    def eig_copy(n):
        tile = info[1 + base + n]
        cols = pl.ds(pl.multiple_of((tile % 32) * TILE_A, TILE_A), TILE_A)
        return pltpu.make_async_copy(eigen.at[tile // 32, :, cols], eig.at[n], sems.at[n])

    for n in range(count):
        eig_copy(n).start()
    acc[...] = jnp.zeros_like(acc)
    for d in range(NQ):
        bases[me ^ d] = piece(d, slice(NQ, NQ + 4))

    def rotate(n):
        basis = bases[start + n].reshape(TILE_A, TILE_A)
        basis_t = basis.astype(jnp.float32).T.astype(BF)
        for d in range(NQ):
            rows = piece(d, start + n)
            place = pl.ds(pl.multiple_of((me ^ d) * 16, 16), 16)
            train[place, :] = rows[:16]
            query[place, :] = rows[16:]
        own = jnp.dot(piece(0, start + n)[:16], basis, preferred_element_type=jnp.float32)
        rows_kept[n] = jnp.where(x == 0, own[:8], own[8:]).astype(BF)
        rows_given[n] = jnp.where(x == 0, own[8:], own[:8]).astype(BF)
        train_t[n] = across(basis_t, train[...]).astype(BF)
        query_t[n] = across(basis_t, query[...]).astype(BF)

    def weigh(n, k):
        weights[k] = 1.0 / (eig[n].T + damping)

    def gram(n, k):
        layer = info[1 + base + n] // 32
        code = codes[...]
        rows = train_t[n]
        zero = jnp.zeros_like(rows)
        for h in range(2):
            left = jnp.concatenate(
                [jnp.where(code == s, rows, zero) for s in range(4 * h, 4 * h + 4)], axis=0
            )
            for c in range(3):
                cols = slice(c * 256, (c + 1) * 256)
                part = jnp.dot(left, grads[layer, :, cols], preferred_element_type=jnp.float32)
                part = part.reshape(4, TILE_A, 256) * weights[k, :, cols][None]
                scaled[k][h * 512 : (h + 1) * 512, cols] = part.astype(BF).reshape(512, 256)

    def project(n, k):
        layer = info[1 + base + n] // 32
        query = query_t[n].astype(jnp.float32)
        for h in range(2):
            part = jnp.dot(
                scaled[k][h * 512 : (h + 1) * 512, :],
                query_grads[layer],
                preferred_element_type=jnp.float32,
            )
            part = part.reshape(4, TILE_A, TOKENS) * query[None]
            acc[4 * h : 4 * h + 4] += jnp.sum(part.reshape(4, TILE_A // 8, 8, TOKENS), axis=1)

    rotate(0)
    rotate(1)
    eig_copy(0).wait()
    weigh(0, 0)
    eig_copy(1).wait()
    weigh(1, 1)
    gram(0, 0)

    @pl.loop(0, count - 2, step=2)
    def _(n):
        eig_copy(n + 2).wait()
        eig_copy(n + 3).wait()
        gram(n + 1, 1)
        rotate(n + 2)
        project(n, 0)
        weigh(n + 2, 0)
        gram(n + 2, 0)
        rotate(n + 3)
        project(n + 1, 1)
        weigh(n + 3, 1)

    gram(count - 1, 1)
    project(count - 2, 0)
    project(count - 1, 1)
    total = before[...] + jnp.sum(acc[...], axis=1)
    if last:
        outs[0][...] = jnp.where(x == 0, total[:SEQS], total[SEQS:])
        outs[1][...] = jnp.where(x == 0, total[SEQS:], total[:SEQS])
    else:
        outs[0][...] = total


VMEM = pl.BlockSpec(memory_space=pltpu.VMEM)
SMEM = pl.BlockSpec(memory_space=pltpu.SMEM)
HBM = pl.BlockSpec(memory_space=pltpu.HBM)


def score_tiles(base, count, last, info, arrays, places, grads, query_grads, codes, eigenvalues, before):
    width = grads.shape[2]

    def kernel(info_ref, *refs):
        held = refs[: len(arrays)]
        units = [(held[a], which) for a, which in places]
        score_kernel(base, count, last, info_ref, *units, *refs[len(arrays) :])

    sums = (
        [jax.ShapeDtypeStruct((SEQS, TOKENS), jnp.float32)] * 2
        if last
        else [jax.ShapeDtypeStruct((GROUPS, TOKENS), jnp.float32)]
    )
    rows = [jax.ShapeDtypeStruct((count, 8, TILE_A), BF)] * 2
    return pl.pallas_call(
        kernel,
        in_specs=[SMEM] + [VMEM] * len(arrays) + [VMEM, VMEM, VMEM, HBM, VMEM],
        out_specs=[VMEM] * len(sums + rows),
        out_shape=sums + rows,
        scratch_shapes=[
            pltpu.VMEM((NQ, 4, 32, TILE_A), BF),
            pltpu.VMEM((TOKENS, TILE_A), BF),
            pltpu.VMEM((TOKENS, TILE_A), BF),
            pltpu.VMEM((count, TILE_A, TOKENS), BF),
            pltpu.VMEM((count, TILE_A, TOKENS), BF),
            pltpu.VMEM((count, width, TILE_A), jnp.float32),
            pltpu.VMEM((GROUPS * TILE_A, width), BF),
            pltpu.VMEM((GROUPS * TILE_A, width), BF),
            pltpu.VMEM((2, TILE_A, width), jnp.float32),
            pltpu.VMEM((GROUPS, 8, TOKENS), jnp.float32),
            pltpu.SemaphoreType.DMA((count,)),
        ],
        compiler_params=pltpu.CompilerParams(vmem_limit_bytes=42 * 1024 * 1024),
        cost_estimate=pl.CostEstimate(
            flops=count * 10**7 if base == 0 else count * 10**9, bytes_accessed=count * 10**6 // 2, transcendentals=0
        ),
    )(info, *arrays, grads, query_grads, codes, eigenvalues, before)


def unpack_kernel(info, kept_a, kept_b, kept_c, came, out):
    first = kept_a.shape[0]
    both = WAVES * NQ
    for place in range(2 * both):
        half, n = place // both, place % both
        if half:
            rows = came[n]
        elif n < first:
            rows = kept_a[n]
        else:
            rows = kept_b[n - first] if n < NQ else kept_c[n - NQ]
        tile = info[1 + n + (both + 1 if half else 0)]
        cols = pl.ds(pl.multiple_of((tile % 32) * TILE_A, TILE_A), TILE_A)
        out[tile // 32, :, cols] = rows


def after(value, *others):
    return lax.optimization_barrier((value, *others))[0]


def paired_body(
    train_inputs,
    train_outgrads,
    sequence_ids,
    query_inputs,
    query_outgrads,
    eigenvalues,
    input_basis,
    slot_list,
    output_basis,
):
    x = lax.axis_index("parts")
    me = lax.axis_index("query")
    train_other = lax.ppermute(train_inputs, "parts", SWAP)
    ids = jnp.arange(64, dtype=jnp.int32)
    tile_of = jnp.sum(jnp.where(slot_list[None, :] == ids[:, None], ids[None, :], 0), axis=1)
    by_half = tile_of.reshape(NQ, 2, WAVES).transpose(1, 2, 0).reshape(2, WAVES * NQ)
    mine = jnp.where(x == 0, by_half[0], by_half[1])
    theirs = jnp.where(x == 0, by_half[1], by_half[0])
    ids = sequence_ids.reshape(1, sequence_ids.shape[0])
    ids_other = lax.ppermute(after(ids, mine), "parts", SWAP)
    side = x.reshape(1).astype(jnp.int32)
    info = jnp.concatenate([me.reshape(1).astype(jnp.int32), mine, side, theirs])

    packed = pl.pallas_call(
        pack_kernel,
        in_specs=[SMEM, VMEM, VMEM, VMEM, VMEM],
        out_specs=[VMEM] * WAVES,
        out_shape=[jax.ShapeDtypeStruct((UNIT, 32, TILE_A), BF)] * WAVES,
        compiler_params=pltpu.CompilerParams(vmem_limit_bytes=8 * 1024 * 1024),
    )(after(info, ids_other), train_inputs, train_other, query_inputs, input_basis)

    out_other = lax.ppermute(after(train_outgrads, packed[0]), "parts", SWAP)
    slab = train_outgrads.shape[2]
    little = pltpu.CompilerParams(vmem_limit_bytes=16 * 1024 * 1024)
    query_grads = pl.pallas_call(
        query_kernel,
        in_specs=[VMEM] * 2,
        out_specs=VMEM,
        out_shape=jax.ShapeDtypeStruct((LAYERS, slab, TOKENS), BF),
        compiler_params=little,
    )(query_outgrads, output_basis)
    grads, codes = pl.pallas_call(
        train_kernel,
        in_specs=[SMEM] + [VMEM] * 5,
        out_specs=[VMEM, VMEM],
        out_shape=[
            jax.ShapeDtypeStruct((LAYERS, TOKENS, slab), BF),
            jax.ShapeDtypeStruct((1, TOKENS), jnp.int32),
        ],
        compiler_params=little,
    )(info, train_outgrads, out_other, ids, ids_other, output_basis)

    units = [None] * NQ
    units[0] = packed[0]
    units[4] = hop(packed[0], 4)
    units[12] = hop(packed[0], 12)
    units[8] = hop(after(packed[0], units[4], units[12], query_grads), 8)
    units[2] = hop(units[0], 2)
    units[6] = hop(units[4], 2)
    units[14] = hop(after(units[12], out_other), 2)
    units[10] = hop(after(units[8], units[2], units[6], units[14]), 2)
    for d in (0, 2, 4, 6, 12, 8, 10):
        units[d ^ 1] = hop(units[d], 1)
    units[15] = hop(after(units[14], grads), 1)
    places0 = [(d, None) for d in range(NQ)]

    zero = jnp.zeros((GROUPS, TOKENS), jnp.float32)
    common = (grads, query_grads, codes, eigenvalues)
    part0, kept_a, given_a = score_tiles(0, 10, False, info, units, places0, *common, zero)

    second = after(packed[1], units[8])
    along = [hop(second, d) for d in (4, 12, 8)]
    near = hop(second, 2)
    first, third, near, _ = lax.optimization_barrier((along[0], along[1], near, part0))
    pair = jnp.stack([first, third])
    pair_beside = hop(pair, 2)
    last = after(along[2], part0)
    last_beside = hop(last, 2)
    part1, kept_b, given_b = score_tiles(10, 6, False, info, units, places0, *common, part0)
    pair_beside, last_beside, _ = lax.optimization_barrier((pair_beside, last_beside, part1))
    arrays = [second, near, pair, pair_beside, last, last_beside]
    arrays = arrays + [hop(array, 1) for array in arrays]
    held = {0: (0, None), 4: (2, 0), 12: (2, 1), 8: (4, None)}
    places1 = []
    for d in range(NQ):
        array, index = held[d & 12]
        places1.append((array + (d & 2) // 2 + 6 * (d & 1), index))
    keep, give, kept1, given1 = score_tiles(
        16, 16, True, info, arrays, places1, *common, part1
    )

    total = keep + lax.ppermute(give, "parts", SWAP)
    came = lax.ppermute(jnp.concatenate([given_a, given_b, given1], axis=0), "parts", SWAP)
    total = after(total, came)
    rotated_out = pl.pallas_call(
        unpack_kernel,
        in_specs=[SMEM] + [VMEM] * 4,
        out_specs=VMEM,
        out_shape=jax.ShapeDtypeStruct(train_inputs.shape, BF),
        compiler_params=pltpu.CompilerParams(vmem_limit_bytes=8 * 1024 * 1024),
    )(info, kept_a, kept_b, kept1, came)
    for bits in (1, 2, 4):
        total = total + hop(total, bits)
    total = after(total, rotated_out)
    total = total + hop(total, 8)
    scores = jnp.sum(total.reshape(SEQS, QUERIES, QLEN), axis=2).T
    return (scores, rotated_out)


def solution(mesh):
    paired = mesh.shape["parts"] == 2 and mesh.shape["query"] == NQ
    return jax.shard_map(
        paired_body if paired else general_body,
        mesh=mesh,
        in_specs=(
            P(None, ("parts", "query"), None),
            P(None, "parts", "query"),
            P("parts"),
            P(None, "query", None),
            P(None, None, "query"),
            P(None, "query", None),
            P("query", None, None),
            P(),
            P(None, "query", None, None),
        ),
        out_specs=(P(None, "parts"), P(None, ("parts", "query"), None)),
        check_vma=False,
    )
```

```python
import jax
import jax.numpy as jnp
from jax import lax
from jax.experimental import pallas as pl
from jax.experimental.pallas import tpu as pltpu
from jax.sharding import PartitionSpec as P

D = 4096
LAYERS = 2
TILE_A = 128
TILE_S = 64
SEQS = 4
QUERIES = 16
QLEN = 16


damping = 0.05


def rotate_blocks(rows, block_tiles, width):
    layer_count, row_count, feature_count = rows.shape
    blocks = rows.reshape(layer_count, row_count, feature_count // width, width)
    shaped = block_tiles.reshape(layer_count, feature_count // width, width, width)
    turned = jnp.einsum("lrbi,lbij->lrbj", blocks, shaped, preferred_element_type=jnp.float32)
    return turned.reshape(layer_count, row_count, feature_count).astype(jnp.bfloat16)


def general_body(
    train_inputs,
    train_outgrads,
    sequence_ids,
    query_inputs,
    query_outgrads,
    eigenvalues,
    input_basis,
    slot_list,
    output_basis,
):
    every_slot = lax.all_gather(input_basis, "query", axis=0, tiled=True)
    basis_tiles = jnp.take(every_slot, slot_list, axis=0)
    rotated_out = rotate_blocks(train_inputs, basis_tiles, TILE_A)
    own_query = rotate_blocks(query_inputs, basis_tiles, TILE_A)
    rotated_train, rotated_query = (
        lax.all_gather(rotated_out, "query", axis=1, tiled=True),
        lax.all_gather(own_query, "query", axis=1, tiled=True),
    )
    grads_rot = rotate_blocks(train_outgrads, output_basis, TILE_S)
    query_rot = rotate_blocks(query_outgrads, output_basis, TILE_S)
    token_count = grads_rot.shape[1]
    slab_width = grads_rot.shape[2]
    weights = 1.0 / (eigenvalues + damping)
    onehot = (sequence_ids[:, None] == jnp.arange(SEQS, dtype=jnp.int32)[None, :]).astype(
        jnp.bfloat16
    )
    totals = jnp.zeros((SEQS, QUERIES * QLEN), jnp.float32)
    for layer_index in range(LAYERS):
        masked = (onehot[:, :, None] * grads_rot[layer_index][:, None, :]).reshape(
            token_count, SEQS * slab_width
        )
        gram_block = lax.dot_general(
            masked,
            rotated_train[layer_index],
            (((0,), (0,)), ((), ())),
            preferred_element_type=jnp.float32,
        )
        scaled = (gram_block.reshape(SEQS, slab_width, D) * weights[layer_index][None]).astype(
            jnp.bfloat16
        )
        projected = jnp.einsum(
            "sij,uj->siu", scaled, rotated_query[layer_index], preferred_element_type=jnp.float32
        )
        totals = totals + jnp.einsum(
            "siu,ui->su", projected, query_rot[layer_index].astype(jnp.float32)
        )
    partial_value = jnp.sum(totals.reshape(SEQS, QUERIES, QLEN), axis=2).T
    scores = lax.psum(partial_value, "query")
    return (scores, rotated_out)


NQ = 16
WAVES = 2
GROUPS = 2 * SEQS
TOKENS = 256
UNIT = 20
SWAP = [(0, 1), (1, 0)]
BF = jnp.bfloat16


def hop(value, bits):
    return lax.ppermute(value, "query", [(i, i ^ bits) for i in range(NQ)])


def pack_kernel(info, own, other, query, basis, *units):
    x = info[1 + WAVES * NQ]

    for wave in range(WAVES):
        unit = units[wave]

        for owner in range(NQ):
            tile = info[1 + wave * NQ + owner]
            layer = tile // 32
            cols = pl.ds(pl.multiple_of((tile % 32) * TILE_A, TILE_A), TILE_A)
            mine = own[layer, :, cols].astype(jnp.float32)
            came = other[layer, :, cols].astype(jnp.float32)
            first = jnp.where(x == 0, mine, came)
            second = jnp.where(x == 0, came, mine)
            unit[owner, :16, :] = jnp.concatenate([first, second], axis=0).astype(BF)
            unit[owner, 16:, :] = query[layer, :, cols]

        unit[NQ:] = basis[2 * x + wave].reshape(4, 32, TILE_A)


def diagonal(tiles, layer, c):
    blank = jnp.zeros((TILE_S, TILE_S), jnp.float32)
    upper = jnp.concatenate([tiles[layer, 2 * c].astype(jnp.float32), blank], axis=1)
    lower = jnp.concatenate([blank, tiles[layer, 2 * c + 1].astype(jnp.float32)], axis=1)
    return jnp.concatenate([upper, lower], axis=0)


def query_kernel(query, tiles, query_grads):
    for layer in range(LAYERS):
        for c in range(tiles.shape[1] // 2):
            cols = slice(c * TILE_A, (c + 1) * TILE_A)
            block_t = diagonal(tiles, layer, c).T.astype(BF)
            query_grads[layer, cols, :] = across(block_t, query[layer, :, cols]).astype(BF)


def train_kernel(info, own, other, ids, ids_other, tiles, grads, codes):
    x = info[1 + WAVES * NQ]
    for layer in range(LAYERS):
        for c in range(tiles.shape[1] // 2):
            cols = slice(c * TILE_A, (c + 1) * TILE_A)
            tile = diagonal(tiles, layer, c).astype(BF)
            mine = jnp.dot(own[layer, :, cols], tile, preferred_element_type=jnp.float32)
            came = jnp.dot(other[layer, :, cols], tile, preferred_element_type=jnp.float32)
            first = jnp.where(x == 0, mine, came).reshape(NQ, 1, 8, TILE_A)
            second = jnp.where(x == 0, came, mine).reshape(NQ, 1, 8, TILE_A)
            rows = jnp.concatenate([first, second], axis=1).reshape(TOKENS, TILE_A)
            grads[layer, :, cols] = rows.astype(BF)
    half = TOKENS // 2
    row = lax.broadcasted_iota(jnp.int32, (half, TOKENS), 0)
    col = lax.broadcasted_iota(jnp.int32, (half, TOKENS), 1)
    hit = row == (col >> 4) * 8 + (col & 7)
    part = (col >> 3) & 1
    own_f, other_f = ids[...].astype(jnp.float32), ids_other[...].astype(jnp.float32)
    mine = jnp.where(hit & (part == x), 1.0, 0.0)
    came = jnp.where(hit & (part != x), 1.0, 0.0)
    placed = jnp.dot(
        jnp.broadcast_to(own_f, (8, half)), mine, preferred_element_type=jnp.float32
    ) + jnp.dot(jnp.broadcast_to(other_f, (8, half)), came, preferred_element_type=jnp.float32)
    codes[...] = (placed[:1] + 0.5).astype(jnp.int32) + SEQS * part[:1]


def across(left, right):
    return lax.dot_general(
        left, right, (((1,), (1,)), ((), ())), preferred_element_type=jnp.float32
    )


def score_kernel(base, count, last, info, *refs):
    units = refs[:NQ]
    grads, query_grads, codes, eigen, before = refs[NQ : NQ + 5]
    outs = refs[NQ + 5 : NQ + (9 if last else 8)]
    rows_kept, rows_given = outs[-2:]
    bases, train, query, train_t, query_t, eig, scaled0, scaled1, weights, acc, sems = refs[
        NQ + 5 + len(outs) :
    ]
    scaled = (scaled0, scaled1)
    me = info[0]
    x = info[1 + WAVES * NQ]
    start = base % NQ

    def piece(d, index):
        unit, which = units[d]
        return unit[index] if which is None else unit[which, index]

    def eig_copy(n):
        tile = info[1 + base + n]
        cols = pl.ds(pl.multiple_of((tile % 32) * TILE_A, TILE_A), TILE_A)
        return pltpu.make_async_copy(eigen.at[tile // 32, :, cols], eig.at[n], sems.at[n])

    for n in range(count):
        eig_copy(n).start()
    acc[...] = jnp.zeros_like(acc)
    for d in range(NQ):
        bases[me ^ d] = piece(d, slice(NQ, NQ + 4))

    def rotate(n):
        basis = bases[start + n].reshape(TILE_A, TILE_A)
        basis_t = basis.astype(jnp.float32).T.astype(BF)
        for d in range(NQ):
            rows = piece(d, start + n)
            place = pl.ds(pl.multiple_of((me ^ d) * 16, 16), 16)
            train[place, :] = rows[:16]
            query[place, :] = rows[16:]
        own = jnp.dot(piece(0, start + n)[:16], basis, preferred_element_type=jnp.float32)
        rows_kept[n] = jnp.where(x == 0, own[:8], own[8:]).astype(BF)
        rows_given[n] = jnp.where(x == 0, own[8:], own[:8]).astype(BF)
        train_t[n] = across(basis_t, train[...]).astype(BF)
        query_t[n] = across(basis_t, query[...]).astype(BF)

    def weigh(n, k):
        weights[k] = 1.0 / (eig[n].T + damping)

    def gram(n, k):
        layer = info[1 + base + n] // 32
        code = codes[...]
        rows = train_t[n]
        zero = jnp.zeros_like(rows)
        for h in range(2):
            left = jnp.concatenate(
                [jnp.where(code == s, rows, zero) for s in range(4 * h, 4 * h + 4)], axis=0
            )
            for c in range(3):
                cols = slice(c * 256, (c + 1) * 256)
                part = jnp.dot(left, grads[layer, :, cols], preferred_element_type=jnp.float32)
                part = part.reshape(4, TILE_A, 256) * weights[k, :, cols][None]
                scaled[k][h * 512 : (h + 1) * 512, cols] = part.astype(BF).reshape(512, 256)

    def project(n, k):
        layer = info[1 + base + n] // 32
        query = query_t[n].astype(jnp.float32)
        for h in range(2):
            part = jnp.dot(
                scaled[k][h * 512 : (h + 1) * 512, :],
                query_grads[layer],
                preferred_element_type=jnp.float32,
            )
            part = part.reshape(4, TILE_A, TOKENS) * query[None]
            acc[4 * h : 4 * h + 4] += jnp.sum(part.reshape(4, TILE_A // 8, 8, TOKENS), axis=1)

    rotate(0)
    rotate(1)
    eig_copy(0).wait()
    weigh(0, 0)
    eig_copy(1).wait()
    weigh(1, 1)
    gram(0, 0)

    @pl.loop(0, count - 2, step=2)
    def _(n):
        eig_copy(n + 2).wait()
        eig_copy(n + 3).wait()
        gram(n + 1, 1)
        rotate(n + 2)
        project(n, 0)
        weigh(n + 2, 0)
        gram(n + 2, 0)
        rotate(n + 3)
        project(n + 1, 1)
        weigh(n + 3, 1)

    gram(count - 1, 1)
    project(count - 2, 0)
    project(count - 1, 1)
    total = before[...] + jnp.sum(acc[...], axis=1)
    if last:
        outs[0][...] = jnp.where(x == 0, total[:SEQS], total[SEQS:])
        outs[1][...] = jnp.where(x == 0, total[SEQS:], total[:SEQS])
    else:
        outs[0][...] = total


VMEM = pl.BlockSpec(memory_space=pltpu.VMEM)
SMEM = pl.BlockSpec(memory_space=pltpu.SMEM)
HBM = pl.BlockSpec(memory_space=pltpu.HBM)


def score_tiles(base, count, last, info, arrays, places, grads, query_grads, codes, eigenvalues, before):
    width = grads.shape[2]

    def kernel(info_ref, *refs):
        held = refs[: len(arrays)]
        units = [(held[a], which) for a, which in places]
        score_kernel(base, count, last, info_ref, *units, *refs[len(arrays) :])

    sums = (
        [jax.ShapeDtypeStruct((SEQS, TOKENS), jnp.float32)] * 2
        if last
        else [jax.ShapeDtypeStruct((GROUPS, TOKENS), jnp.float32)]
    )
    rows = [jax.ShapeDtypeStruct((count, 8, TILE_A), BF)] * 2
    return pl.pallas_call(
        kernel,
        in_specs=[SMEM] + [VMEM] * len(arrays) + [VMEM, VMEM, VMEM, HBM, VMEM],
        out_specs=[VMEM] * len(sums + rows),
        out_shape=sums + rows,
        scratch_shapes=[
            pltpu.VMEM((NQ, 4, 32, TILE_A), BF),
            pltpu.VMEM((TOKENS, TILE_A), BF),
            pltpu.VMEM((TOKENS, TILE_A), BF),
            pltpu.VMEM((count, TILE_A, TOKENS), BF),
            pltpu.VMEM((count, TILE_A, TOKENS), BF),
            pltpu.VMEM((count, width, TILE_A), jnp.float32),
            pltpu.VMEM((GROUPS * TILE_A, width), BF),
            pltpu.VMEM((GROUPS * TILE_A, width), BF),
            pltpu.VMEM((2, TILE_A, width), jnp.float32),
            pltpu.VMEM((GROUPS, 8, TOKENS), jnp.float32),
            pltpu.SemaphoreType.DMA((count,)),
        ],
        compiler_params=pltpu.CompilerParams(vmem_limit_bytes=42 * 1024 * 1024),
        cost_estimate=pl.CostEstimate(
            flops=count * 10**7 if base == 0 else count * 10**9, bytes_accessed=count * 10**6 // 2, transcendentals=0
        ),
    )(info, *arrays, grads, query_grads, codes, eigenvalues, before)


def unpack_kernel(info, kept_a, kept_b, kept_c, came, out):
    first = kept_a.shape[0]
    both = WAVES * NQ
    for place in range(2 * both):
        half, n = place // both, place % both
        if half:
            rows = came[n]
        elif n < first:
            rows = kept_a[n]
        else:
            rows = kept_b[n - first] if n < NQ else kept_c[n - NQ]
        tile = info[1 + n + (both + 1 if half else 0)]
        cols = pl.ds(pl.multiple_of((tile % 32) * TILE_A, TILE_A), TILE_A)
        out[tile // 32, :, cols] = rows


def after(value, *others):
    return lax.optimization_barrier((value, *others))[0]


def paired_body(
    train_inputs,
    train_outgrads,
    sequence_ids,
    query_inputs,
    query_outgrads,
    eigenvalues,
    input_basis,
    slot_list,
    output_basis,
):
    x = lax.axis_index("parts")
    me = lax.axis_index("query")
    train_other = lax.ppermute(train_inputs, "parts", SWAP)
    ids = jnp.arange(64, dtype=jnp.int32)
    tile_of = jnp.sum(jnp.where(slot_list[None, :] == ids[:, None], ids[None, :], 0), axis=1)
    by_half = tile_of.reshape(NQ, 2, WAVES).transpose(1, 2, 0).reshape(2, WAVES * NQ)
    mine = jnp.where(x == 0, by_half[0], by_half[1])
    theirs = jnp.where(x == 0, by_half[1], by_half[0])
    ids = sequence_ids.reshape(1, sequence_ids.shape[0])
    ids_other = lax.ppermute(after(ids, mine), "parts", SWAP)
    side = x.reshape(1).astype(jnp.int32)
    info = jnp.concatenate([me.reshape(1).astype(jnp.int32), mine, side, theirs])

    packed = pl.pallas_call(
        pack_kernel,
        in_specs=[SMEM, VMEM, VMEM, VMEM, VMEM],
        out_specs=[VMEM] * WAVES,
        out_shape=[jax.ShapeDtypeStruct((UNIT, 32, TILE_A), BF)] * WAVES,
        compiler_params=pltpu.CompilerParams(vmem_limit_bytes=60 * 1024 * 1024),
    )(after(info, ids_other), train_inputs, train_other, query_inputs, input_basis)

    out_other = lax.ppermute(after(train_outgrads, packed[0]), "parts", SWAP)
    slab = train_outgrads.shape[2]
    little = pltpu.CompilerParams(vmem_limit_bytes=16 * 1024 * 1024)
    query_grads = pl.pallas_call(
        query_kernel,
        in_specs=[VMEM] * 2,
        out_specs=VMEM,
        out_shape=jax.ShapeDtypeStruct((LAYERS, slab, TOKENS), BF),
        compiler_params=little,
    )(query_outgrads, output_basis)
    grads, codes = pl.pallas_call(
        train_kernel,
        in_specs=[SMEM] + [VMEM] * 5,
        out_specs=[VMEM, VMEM],
        out_shape=[
            jax.ShapeDtypeStruct((LAYERS, TOKENS, slab), BF),
            jax.ShapeDtypeStruct((1, TOKENS), jnp.int32),
        ],
        compiler_params=little,
    )(info, train_outgrads, out_other, ids, ids_other, output_basis)

    units = [None] * NQ
    units[0] = packed[0]
    units[4] = hop(packed[0], 4)
    units[12] = hop(packed[0], 12)
    units[8] = hop(after(packed[0], units[4], units[12], query_grads), 8)
    units[2] = hop(units[0], 2)
    units[6] = hop(units[4], 2)
    units[14] = hop(after(units[12], out_other), 2)
    units[10] = hop(after(units[8], units[2], units[6], units[14]), 2)
    for d in (0, 2, 4, 6, 12, 8, 10):
        units[d ^ 1] = hop(units[d], 1)
    units[15] = hop(after(units[14], grads), 1)
    places0 = [(d, None) for d in range(NQ)]

    zero = jnp.zeros((GROUPS, TOKENS), jnp.float32)
    common = (grads, query_grads, codes, eigenvalues)
    part0, kept_a, given_a = score_tiles(0, 10, False, info, units, places0, *common, zero)

    second = after(packed[1], units[8])
    along = [hop(second, d) for d in (4, 12, 8)]
    near = hop(second, 2)
    first, third, near, _ = lax.optimization_barrier((along[0], along[1], near, part0))
    pair = jnp.stack([first, third])
    pair_beside = hop(pair, 2)
    last = after(along[2], part0)
    last_beside = hop(last, 2)
    part1, kept_b, given_b = score_tiles(10, 6, False, info, units, places0, *common, part0)
    pair_beside, last_beside, _ = lax.optimization_barrier((pair_beside, last_beside, part1))
    arrays = [second, near, pair, pair_beside, last, last_beside]
    arrays = arrays + [hop(array, 1) for array in arrays]
    held = {0: (0, None), 4: (2, 0), 12: (2, 1), 8: (4, None)}
    places1 = []
    for d in range(NQ):
        array, index = held[d & 12]
        places1.append((array + (d & 2) // 2 + 6 * (d & 1), index))
    keep, give, kept1, given1 = score_tiles(
        16, 16, True, info, arrays, places1, *common, part1
    )

    total = keep + lax.ppermute(give, "parts", SWAP)
    came = lax.ppermute(jnp.concatenate([given_a, given_b, given1], axis=0), "parts", SWAP)
    total = after(total, came)
    rotated_out = pl.pallas_call(
        unpack_kernel,
        in_specs=[SMEM] + [VMEM] * 4,
        out_specs=VMEM,
        out_shape=jax.ShapeDtypeStruct(train_inputs.shape, BF),
        compiler_params=pltpu.CompilerParams(vmem_limit_bytes=8 * 1024 * 1024),
    )(info, kept_a, kept_b, kept1, came)
    for bits in (1, 2, 4):
        total = total + hop(total, bits)
    total = after(total, rotated_out)
    total = total + hop(total, 8)
    scores = jnp.sum(total.reshape(SEQS, QUERIES, QLEN), axis=2).T
    return (scores, rotated_out)


def solution(mesh):
    paired = mesh.shape["parts"] == 2 and mesh.shape["query"] == NQ
    return jax.shard_map(
        paired_body if paired else general_body,
        mesh=mesh,
        in_specs=(
            P(None, ("parts", "query"), None),
            P(None, "parts", "query"),
            P("parts"),
            P(None, "query", None),
            P(None, None, "query"),
            P(None, "query", None),
            P("query", None, None),
            P(),
            P(None, "query", None, None),
        ),
        out_specs=(P(None, "parts"), P(None, ("parts", "query"), None)),
        check_vma=False,
    )
```
